32 devices in a mesh: dp: 16 (over z, y, core), seq: 2 (over x).
Axes of the slice: x: 2, y: 2, z: 4, core: 2. Of those that a mesh axis runs over, the one named last changes fastest.
Arguments:
- inputs: bfloat16 [32, 336, 1152], P('dp', 'seq'), may hold values from -6 to 6
- skipped: bfloat16 [32, 336, 1152], P('dp', None, 'seq'), may hold values from -6 to 6
- lengths: int32 [32], P('dp'), may hold values from 1 to 77, as said below
- cotangent: bfloat16 [32, 336, 1152], P('dp', 'seq'), may hold values from -6 to 6
- skip_weight: bfloat16 [2304, 1152], replicated, may hold values from -0.125 to 0.125
- skip_bias: float32 [1152], replicated, may hold values from -3 to 3
- gain_one: float32 [1152], replicated, may hold values from 0.25 to 1.75
- shift_one: float32 [1152], replicated, may hold values from -1.75 to 1.75
- qkv_weight: bfloat16 [1152, 3456], replicated, may hold values from -0.1875 to 0.1875
- proj_weight: bfloat16 [1152, 1152], replicated, may hold values from -0.75 to 0.75
- proj_bias: float32 [1152], replicated, may hold values from -1.75 to 1.75
- gain_two: float32 [1152], replicated, may hold values from 0.25 to 1.75
- shift_two: float32 [1152], replicated, may hold values from -1.75 to 1.75
- fc1_weight: bfloat16 [1152, 4608], replicated, may hold values from -0.1875 to 0.1875
- fc1_bias: float32 [4608], replicated, may hold values from -3 to 3
- fc2_weight: bfloat16 [4608, 1152], replicated, may hold values from -0.09375 to 0.09375
- fc2_bias: float32 [1152], replicated, may hold values from -3 to 3
Outputs:
- block_output: bfloat16 [32, 336, 1152], P('dp', 'seq')
- grad_inputs: float32 [32, 336, 1152], P('dp', 'seq')
- grad_skipped: float32 [32, 336, 1152], P('dp', None, 'seq')
- grad_skip_weight: float32 [2304, 1152], P(('dp', 'seq'))
- grad_skip_bias: float32 [1152], P(('dp', 'seq'))
- grad_gain_one: float32 [1152], P(('dp', 'seq'))
- grad_shift_one: float32 [1152], P(('dp', 'seq'))
- grad_qkv_weight: float32 [1152, 3456], P(('dp', 'seq'))
- grad_proj_weight: float32 [1152, 1152], P(('dp', 'seq'))
- grad_proj_bias: float32 [1152], P(('dp', 'seq'))
- grad_gain_two: float32 [1152], P(('dp', 'seq'))
- grad_shift_two: float32 [1152], P(('dp', 'seq'))
- grad_fc1_weight: float32 [1152, 4608], P(('dp', 'seq'))
- grad_fc1_bias: float32 [4608], P(('dp', 'seq'))
- grad_fc2_weight: float32 [4608, 1152], P(('dp', 'seq'))
- grad_fc2_bias: float32 [1152], P(('dp', 'seq'))
The draws below stay inside these ranges and needn't reach their ends.
Inputs may be any that keep to these rules, and one draw needn't show every extreme that they name: `lengths`: caption tokens of each item; some item has exactly 77.
All inputs are finite; a program needn't handle non-finite values.
Results may differ from the reference program's by a relative error of at most 0.014.
Values may be sent and summed in bfloat16 or wider, within the bound.
A program may use at most 320 MiB of HBM per device.

```python
from functools import partial
import jax
import jax.numpy as jnp
from jax import lax

D = 1152
HEADS = 16
HEAD_DIM = 72
FF = 4608
CAPTION = 77
IMAGE = 256
SLOTS = 336
ITEMS = 32


def draw_lengths(key, part):
    key = jax.random.fold_in(key, 7)
    key_len, key_pick = jax.random.split(key)
    drawn_len = jax.random.randint(key_len, (ITEMS,), 1, CAPTION + 1, dtype=jnp.int32)
    chosen = jax.random.randint(key_pick, (), 0, ITEMS, dtype=jnp.int32)
    return jnp.where(jnp.arange(ITEMS, dtype=jnp.int32) == chosen, CAPTION, drawn_len).astype(jnp.int32)


def block_scale(stream_key, extent, cuts, least, top_value):
    factor_of, own = 1.0, jax.random.fold_in(stream_key, 6)
    for dim, shards_of in cuts:
        heights = jnp.exp(jax.random.uniform(jax.random.fold_in(own, dim), (shards_of,), jnp.float32, least / len(cuts), top_value / len(cuts)))
        factor_of = factor_of * jnp.repeat(heights, extent[dim] // shards_of).reshape([-1 if axis == dim else 1 for axis in range(len(extent))])
    return factor_of


def gaussian(stream_key, dims, deviation, reach, cuts=(), kind=jnp.bfloat16):
    values = deviation * jax.random.normal(stream_key, dims, jnp.float32)
    if cuts:
        values = values * block_scale(stream_key, dims, cuts, -0.22, 0.18)
    return jnp.clip(values, -reach, reach).astype(kind)


def setup_inputs(seed: int = 0) -> dict:
    splits = jax.random.split(jax.random.key(seed), 18)
    return {
        "inputs": gaussian(splits[0], (ITEMS, SLOTS, D), 1.0, 6.0, ((0, 16), (1, 2))),
        "skipped": gaussian(splits[1], (ITEMS, SLOTS, D), 1.0, 6.0, ((0, 16), (2, 2))),
        "lengths": draw_lengths(jax.random.fold_in(splits[17], 71), 0),
        "cotangent": gaussian(splits[3], (ITEMS, SLOTS, D), 1.0, 6.0, ((0, 16), (1, 2))),
        "skip_weight": gaussian(splits[4], (2 * D, D), (2 * D) ** -0.5, 0.125),
        "skip_bias": gaussian(splits[5], (D,), 0.5, 3.0, (), jnp.float32),
        "gain_one": jnp.clip(1.0 + 0.15 * jax.random.normal(splits[6], (D,), jnp.float32), 0.25, 1.75),
        "shift_one": gaussian(splits[7], (D,), 0.3, 1.75, (), jnp.float32),
        "qkv_weight": gaussian(splits[8], (D, 3 * D), D ** -0.5, 0.1875),
        "proj_weight": gaussian(splits[9], (D, D), (D // 16) ** -0.5, 0.75),
        "proj_bias": gaussian(splits[10], (D,), 0.3, 1.75, (), jnp.float32),
        "gain_two": jnp.clip(1.0 + 0.15 * jax.random.normal(splits[11], (D,), jnp.float32), 0.25, 1.75),
        "shift_two": gaussian(splits[12], (D,), 0.3, 1.75, (), jnp.float32),
        "fc1_weight": gaussian(splits[13], (D, FF), D ** -0.5, 0.1875),
        "fc1_bias": gaussian(splits[14], (FF,), 0.5, 3.0, (), jnp.float32),
        "fc2_weight": gaussian(splits[15], (FF, D), FF ** -0.5, 0.09375),
        "fc2_bias": gaussian(splits[16], (D,), 0.5, 3.0, (), jnp.float32),
    }


@jax.custom_vjp
def low(v):
    return lax.optimization_barrier(v.astype(jnp.bfloat16)).astype(jnp.float32)

@jax.custom_vjp
def low_back(v):
    return v

def low_keep(v):
    return (low(v), None)

def low_pass(kept, grad):
    return (grad,)

def back_keep(v):
    return (v, None)

def back_low(kept, grad):
    return (low(grad),)
low.defvjp(low_keep, low_pass)
low_back.defvjp(back_keep, back_low)
exact_prec = lax.Precision.HIGHEST
epsilon = 1e-05
masked_score = -1e+30

def matmul(left, right):
    return jnp.dot(left, right, precision=exact_prec)

def layer_norm(stream, gain, shift):
    center = stream - lax.optimization_barrier(jnp.mean(stream, axis=-1, keepdims=True))
    spread = lax.optimization_barrier(jnp.mean(center * center, axis=-1, keepdims=True))
    return center * lax.rsqrt(spread + epsilon) * gain + shift

def key_valid(lengths):
    positions = jnp.arange(SLOTS, dtype=jnp.int32)[None, :]
    caption = (positions >= 1) & (positions <= lengths[:, None])
    image = (positions >= 1 + CAPTION) & (positions < 1 + CAPTION + IMAGE)
    return (positions == 0) | caption | image

def block_group(params, inputs, skipped, lengths):
    skip_weight, skip_bias, gain_one, shift_one, qkv_weight, proj_weight, proj_bias, gain_two, shift_two, fc1_weight, fc1_bias, fc2_weight, fc2_bias = params
    groups, slots, width = inputs.shape
    joined = jnp.concatenate([inputs, skipped], axis=-1).reshape(groups * slots, 2 * width)
    stream = low_back(matmul(joined, skip_weight) + skip_bias)
    normed = low(layer_norm(stream, gain_one, shift_one))
    packed = low(low_back(matmul(normed, qkv_weight)))
    packed = packed.reshape(groups, slots, 3, HEADS, HEAD_DIM)
    query = packed[:, :, 0]
    keys = packed[:, :, 1]
    values = packed[:, :, 2]
    scores = jnp.einsum('gqhd,gkhd->ghqk', query, keys, precision=exact_prec) * HEAD_DIM ** (-0.5)
    valid = key_valid(lengths)
    scores = low_back(jnp.where(valid[:, None, None, :], scores, masked_score))
    top = lax.optimization_barrier(jnp.max(scores, axis=-1, keepdims=True))
    expo = jnp.exp(scores - top)
    probs = expo / lax.optimization_barrier(jnp.sum(expo, axis=-1, keepdims=True))
    mixed = jnp.einsum('ghqk,gkhd->gqhd', low(probs), values, precision=exact_prec)
    mixed = low(low_back(mixed.reshape(groups * slots, width)))
    stream = stream + low_back(matmul(mixed, proj_weight) + proj_bias)
    normed_two = low(layer_norm(stream, gain_two, shift_two))
    hidden = low_back(matmul(normed_two, fc1_weight) + fc1_bias)
    acted = low(jax.nn.gelu(hidden, approximate=False))
    stream = stream + low_back(matmul(acted, fc2_weight) + fc2_bias)
    return stream.reshape(groups, slots, width)

def forward(params, inputs, skipped, lengths):
    blocks = ITEMS // 8
    step_fn = jax.checkpoint(partial(block_group, params))
    grouped = (inputs.reshape((blocks, 8) + inputs.shape[1:]), skipped.reshape((blocks, 8) + skipped.shape[1:]), lengths.reshape(blocks, 8))
    result = lax.map(lambda packed: step_fn(packed[0], packed[1], packed[2]), grouped)
    return result.reshape(inputs.shape)

def reference(inputs, skipped, lengths, cotangent, skip_weight, skip_bias, gain_one, shift_one, qkv_weight, proj_weight, proj_bias, gain_two, shift_two, fc1_weight, fc1_bias, fc2_weight, fc2_bias):
    params = tuple((weight.astype(jnp.float32) for weight in (skip_weight, skip_bias, gain_one, shift_one, qkv_weight, proj_weight, proj_bias, gain_two, shift_two, fc1_weight, fc1_bias, fc2_weight, fc2_bias)))

    def run(params, inputs, skipped):
        return forward(params, inputs, skipped, lengths)
    result, pullback = jax.vjp(run, params, inputs.astype(jnp.float32), skipped.astype(jnp.float32))
    grad_params, grad_inputs, grad_skipped = pullback(cotangent.astype(jnp.float32))
    return (result.astype(jnp.bfloat16), grad_inputs, grad_skipped, grad_params[0], grad_params[1], grad_params[2], grad_params[3], grad_params[4], grad_params[5], grad_params[6], grad_params[7], grad_params[8], grad_params[9], grad_params[10], grad_params[11], grad_params[12])
```

```python
import jax
import jax.numpy as jnp
from jax import lax
from jax.sharding import PartitionSpec as P

HEADS = 16
HEAD_DIM = 72
CAPTION = 77
IMAGE = 256


epsilon = 1e-05
masked_score = -1e30


def layer_norm(stream, gain, shift):
    center = stream - jnp.mean(stream, axis=-1, keepdims=True)
    spread = jnp.mean(center * center, axis=-1, keepdims=True)
    return center * lax.rsqrt(spread + epsilon) * gain + shift


def gelu_exact(values):
    return jax.nn.gelu(values, approximate=False)


def column_sum(values):
    return jnp.sum(values.astype(jnp.float32), axis=0)


def matmul(left, right):
    return jnp.dot(left, right, preferred_element_type=jnp.float32)


def swap_seq(values):
    return lax.ppermute(values, "seq", [(0, 1), (1, 0)])


def swap_dp(values, bit):
    count = lax.axis_size("dp")
    return lax.ppermute(values, "dp", [(i, i ^ (1 << bit)) for i in range(count)])


def pick(values, index, axis):
    return lax.dynamic_index_in_dim(values, index, axis, keepdims=False)


def place(first, own, got, axis):
    return jnp.where(
        first, jnp.concatenate([own, got], axis=axis), jnp.concatenate([got, own], axis=axis)
    )


def halving(block, order, bits):
    dp_index = lax.axis_index("dp")
    seq_index = lax.axis_index("seq")
    dims = list(reversed(range(1, bits))) + ["seq"]
    for name in order:
        axis = dims.index(name)
        own = seq_index if name == "seq" else (dp_index >> name) & 1
        sent = pick(block, 1 - own, axis)
        kept = pick(block, own, axis)
        got = swap_seq(sent) if name == "seq" else swap_dp(sent, name)
        total = kept.astype(jnp.float32) + got.astype(jnp.float32)
        dims.pop(axis)
        block = total.astype(jnp.bfloat16) if dims else total
    return block


def local(
    inputs,
    skipped,
    lengths,
    cotangent,
    skip_weight,
    skip_bias,
    gain_one,
    shift_one,
    qkv_weight,
    proj_weight,
    proj_bias,
    gain_two,
    shift_two,
    fc1_weight,
    fc1_bias,
    fc2_weight,
    fc2_bias,
):
    items, half, width = inputs.shape
    seq_count = lax.axis_size("seq")
    dp_count = lax.axis_size("dp")
    bits = dp_count.bit_length() - 1
    seq_index = lax.axis_index("seq")
    core = lax.axis_index("dp") & 1
    first = seq_index == 0
    slots = half * seq_count

    def whole_item(values, axis):
        own = pick(values, seq_index, 0)
        got = swap_seq(pick(values, 1 - seq_index, 0))
        return place(first, own, got, axis)

    def to_owner(values, axis):
        parts = jnp.split(values, 2, axis=axis)
        own = jnp.where(first, parts[0], parts[1])
        other = jnp.where(first, parts[1], parts[0])
        got = swap_seq(other.astype(jnp.bfloat16)).astype(values.dtype)
        return place(first, own[None], got[None], 0)

    own_inputs = whole_item(inputs, 0)
    own_skip = whole_item(skipped, 1)
    grad_out = whole_item(cotangent, 0)
    length = pick(lengths, seq_index, 0)
    rows = slots

    joined = jnp.concatenate([own_inputs, own_skip], axis=-1)
    stream = matmul(joined, skip_weight) + skip_bias
    normed = layer_norm(stream, gain_one, shift_one).astype(jnp.bfloat16)
    packed = matmul(normed, qkv_weight).astype(jnp.bfloat16)
    heads = packed.reshape(rows, 3, HEADS, HEAD_DIM)
    query, keys, values = heads[:, 0], heads[:, 1], heads[:, 2]
    scale = HEAD_DIM ** (-0.5)
    positions = jnp.arange(slots, dtype=jnp.int32)
    caption = (positions >= 1) & (positions <= length)
    image = (positions >= 1 + CAPTION) & (positions < 1 + CAPTION + IMAGE)
    valid = (positions == 0) | caption | image

    def product(spec, left, right):
        return jnp.einsum(spec, left, right, preferred_element_type=jnp.float32)

    scores = product("qhd,khd->hqk", query, keys) * scale
    scores = jnp.where(valid[None, None, :], scores, masked_score)
    top = jnp.max(scores, axis=-1, keepdims=True)
    expo = jnp.exp(scores - top)
    probs = expo / jnp.sum(expo, axis=-1, keepdims=True)
    probs_low = probs.astype(jnp.bfloat16)
    mixed = product("hqk,khd->qhd", probs_low, values)
    mixed = mixed.astype(jnp.bfloat16).reshape(rows, width)
    attended = matmul(mixed, proj_weight) + proj_bias
    stream_two = stream + attended
    normed_two = layer_norm(stream_two, gain_two, shift_two).astype(jnp.bfloat16)
    hidden = matmul(normed_two, fc1_weight) + fc1_bias
    acted, gelu_back = jax.vjp(gelu_exact, hidden)
    acted_low = acted.astype(jnp.bfloat16)
    block_output = (stream_two + (matmul(acted_low, fc2_weight) + fc2_bias)).astype(jnp.bfloat16)

    blocks = dp_count // 2

    def own_rows(left, right):
        parts = left.reshape(rows, blocks, 2, -1)
        kept = pick(parts, core, 2).reshape(rows, -1)
        sent = pick(parts, 1 - core, 2).reshape(rows, -1)
        left_both = jnp.concatenate([kept, swap_dp(sent, 0)], axis=0)
        right_both = jnp.concatenate([right, swap_dp(right, 0)], axis=0)
        total = matmul(left_both.T, right_both).astype(jnp.bfloat16)
        share = total.shape[0] // (blocks * 2)
        return total.reshape((2,) * bits + (share, right.shape[1]))

    above = list(range(1, bits))
    order_x = ["seq"] + above
    order_y = above + ["seq"]
    order_z = above[1:] + ["seq"] + above[:1]

    grad_fc2 = halving(own_rows(acted_low, grad_out), order_x, bits)
    grad_fc2_bias = column_sum(grad_out)
    grad_acted = matmul(grad_out, fc2_weight.T)
    grad_hidden = gelu_back(grad_acted)[0].astype(jnp.bfloat16)
    grad_fc1 = halving(own_rows(normed_two, grad_hidden), order_x, bits)
    grad_fc1_bias = column_sum(grad_hidden)
    grad_normed_two = matmul(grad_hidden, fc1_weight.T)
    _, norm_back_two = jax.vjp(layer_norm, stream_two, gain_two, shift_two)
    back_two, grad_gain_two, grad_shift_two = norm_back_two(grad_normed_two)
    grad_stream_two = grad_out.astype(jnp.float32) + back_two
    grad_attended = grad_stream_two.astype(jnp.bfloat16)
    grad_proj = halving(own_rows(mixed, grad_attended), order_y, bits)
    grad_proj_bias = column_sum(grad_attended)
    grad_mixed = matmul(grad_attended, proj_weight.T)
    grad_mixed = grad_mixed.astype(jnp.bfloat16).reshape(rows, HEADS, HEAD_DIM)
    grad_probs = product("qhd,khd->hqk", grad_mixed, values)
    grad_scores = probs * (grad_probs - jnp.sum(probs * grad_probs, axis=-1, keepdims=True))
    grad_scores = grad_scores.astype(jnp.bfloat16)
    grad_values = product("hqk,qhd->khd", probs_low, grad_mixed)
    grad_query = product("hqk,khd->qhd", grad_scores, keys) * scale
    grad_keys = product("hqk,qhd->khd", grad_scores, query) * scale
    grad_packed = jnp.stack([grad_query, grad_keys, grad_values], axis=1)
    grad_packed = grad_packed.astype(jnp.bfloat16).reshape(rows, 3 * width)
    grad_qkv = halving(own_rows(normed, grad_packed), order_y, bits)
    grad_normed = matmul(grad_packed, qkv_weight.T)
    _, norm_back_one = jax.vjp(layer_norm, stream, gain_one, shift_one)
    back_one, grad_gain_one, grad_shift_one = norm_back_one(grad_normed)
    grad_stream = (grad_stream_two + back_one).astype(jnp.bfloat16)
    grad_skip = halving(own_rows(joined, grad_stream), order_z, bits)
    grad_skip_bias = column_sum(grad_stream)
    grad_joined = matmul(grad_stream, skip_weight.T)

    vectors = (
        grad_skip_bias,
        grad_gain_one,
        grad_shift_one,
        grad_proj_bias,
        grad_gain_two,
        grad_shift_two,
        grad_fc1_bias,
        grad_fc2_bias,
    )
    chunks = dp_count * seq_count
    line = jnp.concatenate([v.reshape(chunks, -1) for v in vectors], axis=1)
    line = lax.psum_scatter(line, ("dp", "seq"), scatter_dimension=0, tiled=True)[0]
    pieces, start = [], 0
    for vector in vectors:
        size = vector.shape[0] // chunks
        pieces.append(line[start : start + size])
        start += size

    return (
        to_owner(block_output, 0),
        to_owner(grad_joined[:, :width], 0),
        to_owner(grad_joined[:, width:], 1),
        grad_skip,
        pieces[0],
        pieces[1],
        pieces[2],
        grad_qkv,
        grad_proj,
        pieces[3],
        pieces[4],
        pieces[5],
        grad_fc1,
        pieces[6],
        grad_fc2,
        pieces[7],
    )


def solution(mesh):
    return jax.shard_map(
        local,
        mesh=mesh,
        in_specs=(
            P("dp", "seq", None),
            P("dp", None, "seq"),
            P("dp"),
            P("dp", "seq", None),
        )
        + (P(),) * 13,
        out_specs=(
            P("dp", "seq", None),
            P("dp", "seq", None),
            P("dp", None, "seq"),
            P(("dp", "seq"), None),
            P(("dp", "seq")),
            P(("dp", "seq")),
            P(("dp", "seq")),
            P(("dp", "seq"), None),
            P(("dp", "seq"), None),
            P(("dp", "seq")),
            P(("dp", "seq")),
            P(("dp", "seq")),
            P(("dp", "seq"), None),
            P(("dp", "seq")),
            P(("dp", "seq"), None),
            P(("dp", "seq")),
        ),
        check_vma=False,
    )
```

```python
import functools

import jax
import jax.numpy as jnp
import numpy as np
from jax import lax
from jax.experimental import pallas as pl
from jax.experimental.pallas import tpu as pltpu
from jax.sharding import PartitionSpec as P

HEADS = 16
HEAD_DIM = 72
CAPTION = 77
IMAGE = 256


epsilon = 1e-05
masked_score = -1e30


def layer_norm(stream, gain, shift):
    center = stream - jnp.mean(stream, axis=-1, keepdims=True)
    spread = jnp.mean(center * center, axis=-1, keepdims=True)
    return center * lax.rsqrt(spread + epsilon) * gain + shift


def gelu_exact(values):
    return jax.nn.gelu(values, approximate=False)


def column_sum(values):
    return jnp.sum(values.astype(jnp.float32), axis=0)


def matmul(left, right):
    return jnp.dot(left, right, preferred_element_type=jnp.float32)


def swap_seq(values):
    return lax.ppermute(values, "seq", [(0, 1), (1, 0)])


def swap_dp(values, bit):
    count = lax.axis_size("dp")
    return lax.ppermute(values, "dp", [(i, i ^ (1 << bit)) for i in range(count)])


def pick(values, index, axis):
    return lax.dynamic_index_in_dim(values, index, axis, keepdims=False)


def place(first, own, got, axis):
    return jnp.where(
        first, jnp.concatenate([own, got], axis=axis), jnp.concatenate([got, own], axis=axis)
    )


MESH = pl.DeviceIdType.MESH
LANES = 384
TWO = 2 * LANES


class Matrix:
    def __init__(self, share, columns, pieces, cuts):
        self.share, self.columns = share, columns
        self.main = share - share % 16
        self.rest = share % 16
        self.pieces, start = [], 0
        for width in pieces:
            self.pieces.append((start, width))
            start += width
        self.cuts = cuts
        self.fold = self.rest and 16
        self.fold_width = max(pieces)

    def left_rows(self, blocks):
        folds = len(self.pieces) if self.rest else 0
        return blocks * (self.main + folds * 16)


class Unit:
    def __init__(self, matrix, rows, start, columns, hops, folded):
        self.matrix, self.rows, self.start, self.columns = matrix, rows, start, columns
        self.hops, self.folded = hops, folded


def make_units(matrices, hops_of):
    units = []
    for m, matrix in enumerate(matrices):
        for start, columns in matrix.cuts:
            units.append(Unit(m, matrix.main, start, columns, hops_of[len(units)], False))
        if matrix.rest:
            units.append(Unit(m, 16, 0, matrix.fold_width, hops_of[len(units)], True))
    return units


def reduce_kernel(matrices, units, events, dims, *refs):
    count = len(matrices)
    lefts = [(refs[2 * i], refs[2 * i + 1]) for i in range(count)]
    refs = refs[2 * count :]
    rights = [(refs[2 * i], refs[2 * i + 1]) for i in range(count)]
    refs = refs[2 * count :]
    vector_ref, refs = refs[0], refs[1:]
    outs, refs = refs[: len(units)], refs[len(units) :]
    vector_out, refs = refs[0], refs[1:]
    grads, refs = refs[: len(units)], refs[len(units) :]
    hops = len(dims)
    landed = [refs[i * hops : (i + 1) * hops] for i in range(len(units))]
    refs = refs[len(units) * hops :]
    vector_land, refs = refs[: hops + 1], refs[hops + 1 :]
    vector_sum, refs = refs[0], refs[1:]
    fold_sum, left_buffer, right_buffer, refs = refs[0], refs[1], refs[2], refs[3:]
    send_sem, recv_sem, vsend_sem, vrecv_sem, left_sem, right_sem = refs

    dp = lax.axis_index("dp")
    seq = lax.axis_index("seq")
    core = lax.rem(dp, 2)

    def bit(name):
        return seq if name == "seq" else lax.rem(lax.div(dp, 1 << name), 2)

    def partner(name):
        if name == "seq":
            return (dp, 1 - seq)
        return (dp + (1 - 2 * bit(name)) * (1 << name), seq)

    barrier = pltpu.get_barrier_semaphore()
    for name in [0] + list(dims):
        pl.semaphore_signal(barrier, inc=1, device_id=partner(name), device_id_type=MESH)
    pl.semaphore_wait(barrier, len(dims) + 1)

    def left_copies(m):
        rows = matrices[m].left_rows(2 ** len(dims))
        return [
            pltpu.make_async_copy(
                lefts[m][k],
                left_buffer.at[m % 2, pl.ds(0, rows), pl.ds(k * LANES, LANES)],
                left_sem.at[m % 2, k],
            )
            for k in range(2)
        ]

    all_pieces = [(m, p) for m, matrix in enumerate(matrices) for p in range(len(matrix.pieces))]

    def right_copies(index):
        m, p = all_pieces[index]
        start, width = matrices[m].pieces[p]
        return [
            pltpu.make_async_copy(
                rights[m][k].at[:, pl.ds(start, width)],
                right_buffer.at[index % 2, pl.ds(k * LANES, LANES), pl.ds(0, width)],
                right_sem.at[index % 2, k],
            )
            for k in range(2)
        ]

    def start(copies):
        for copy in copies:
            copy.start()

    def wait(copies):
        for copy in copies:
            copy.wait()

    for m in range(2):
        start(left_copies(m))
    for index in range(2):
        start(right_copies(index))

    sent = []

    def send(u, h):
        unit = units[u]
        index = []
        for name in dims:
            if name in unit.hops[:h]:
                index.append(bit(name))
            elif name == unit.hops[h]:
                index.append(1 - bit(name))
            else:
                index.append(slice(None))
        copy = pltpu.make_async_remote_copy(
            src_ref=grads[u].at[tuple(index)],
            dst_ref=landed[u][h],
            send_sem=send_sem.at[u, h],
            recv_sem=recv_sem.at[u, h],
            device_id=partner(unit.hops[h]),
            device_id_type=MESH,
        )
        copy.start()
        sent.append(copy)
        return copy

    flying = {}

    def add(u, h):
        unit = units[u]
        flying[u, h].wait_recv()
        done = unit.hops[: h + 1]
        free = [name for name in dims if name not in done]
        step = 16
        last = h + 1 == hops

        @pl.loop(0, 2 ** len(free) * (unit.rows // step))
        def _(i):
            block, row = lax.div(i, unit.rows // step), lax.rem(i, unit.rows // step) * step
            place = {
                name: lax.rem(lax.div(block, 1 << (len(free) - 1 - k)), 2)
                for k, name in enumerate(free)
            }
            rows = pl.ds(pl.multiple_of(row, step), step)
            own = tuple(place.get(name, bit(name)) for name in dims) + (rows,)
            got = tuple(place[name] for name in free) + (rows,)
            total = grads[u][own].astype(jnp.float32) + landed[u][h][got].astype(jnp.float32)
            if last:
                outs[u][rows] = total
            else:
                grads[u][own] = total.astype(jnp.bfloat16)

        if not last:
            flying[u, h + 1] = send(u, h + 1)

    def multiply(index):
        m, p = all_pieces[index]
        matrix = matrices[m]
        start_column, width = matrix.pieces[p]
        blocks = 2 ** len(dims)
        if p == 0:
            wait(left_copies(m))
        wait(right_copies(index))
        left, right = left_buffer.at[m % 2], right_buffer.at[index % 2]
        u = next(
            i
            for i, unit in enumerate(units)
            if unit.matrix == m
            and not unit.folded
            and unit.start <= start_column < unit.start + unit.columns
        )
        group = blocks
        while group * matrix.main > 640:
            group //= 2
        free = group.bit_length() - 1
        step = next(s for s in (384, 640, 512, 128) if width % s == 0)

        @pl.loop(0, (blocks // group) * (width // step))
        def _(i):
            g, j = lax.div(i, width // step), lax.rem(i, width // step)
            rows = pl.ds(pl.multiple_of(g * (group * matrix.main), 16), group * matrix.main)
            columns = pl.ds(pl.multiple_of(j * step, 128), step)
            result = jnp.dot(left[rows, :], right[:, columns], preferred_element_type=jnp.float32)
            high = len(dims) - free
            where = tuple(lax.rem(lax.div(g, 1 << (high - 1 - k)), 2) for k in range(high))
            target = pl.ds(pl.multiple_of(start_column - units[u].start + j * step, 128), step)
            grads[u][where + (slice(None),) * (free + 1) + (target,)] = result.astype(
                jnp.bfloat16
            ).reshape((2,) * free + (matrix.main, step))

        if matrix.rest:
            offset = blocks * (matrix.main + 16 * p)

            @pl.loop(0, width // step)
            def _(j):
                columns = pl.ds(pl.multiple_of(j * step, 128), step)
                result = jnp.dot(
                    left[pl.ds(offset, blocks * 16), :],
                    right[:, columns],
                    preferred_element_type=jnp.float32,
                )
                if p == 0:
                    fold_sum[:, columns] = result
                else:
                    fold_sum[:, columns] += result

        if index + 2 < len(all_pieces):
            start(right_copies(index + 2))
        last = p + 1 == len(matrix.pieces)
        if last and m + 2 < count:
            start(left_copies(m + 2))
        if start_column + width == units[u].start + units[u].columns:
            flying[u, 0] = send(u, 0)
        if last and matrix.rest:
            f = next(i for i, unit in enumerate(units) if unit.matrix == m and unit.folded)
            folded = fold_sum[:, pl.ds(0, units[f].columns)].astype(jnp.bfloat16)
            grads[f][...] = folded.reshape((2,) * len(dims) + (16, units[f].columns))
            flying[f, 0] = send(f, 0)

    def vector_send(h):
        name = 0 if h == 0 else dims[h - 1]
        source = vector_ref.at[1 - core] if h == 0 else vector_sum.at[
            tuple(bit(n) for n in dims[: h - 1]) + (1 - bit(name),)
        ]
        copy = pltpu.make_async_remote_copy(
            src_ref=source,
            dst_ref=vector_land[h],
            send_sem=vsend_sem.at[h],
            recv_sem=vrecv_sem.at[h],
            device_id=partner(name),
            device_id_type=MESH,
        )
        copy.start()
        sent.append(copy)
        return copy

    vector_flying = {}

    def vector_add(h):
        vector_flying[h].wait_recv()
        own = tuple(bit(n) for n in dims[:h])
        if h == 0:
            vector_sum[...] = vector_ref[core] + vector_land[0][...]
        elif h < hops:
            vector_sum[own] = vector_sum[own] + vector_land[h][...]
        else:
            vector_out[...] = vector_sum[own] + vector_land[h][...]
        if h < hops:
            vector_flying[h + 1] = vector_send(h + 1)

    vector_flying[0] = vector_send(0)
    vector_done, since = 0, 0
    for event in events:
        if event[0] == "c":
            multiply(event[1])
        else:
            add(*event)
            since += 1
            if since % 4 == 0 and vector_done <= hops:
                vector_add(vector_done)
                vector_done += 1
    while vector_done <= hops:
        vector_add(vector_done)
        vector_done += 1
    for copy in sent:
        copy.wait_send()


def left_operand(values, matrix, blocks, core_count):
    rows, depth = values.shape
    padded = jnp.pad(values, ((0, LANES - rows), (0, 0)))
    if not matrix.rest:
        parts = padded.T.reshape(blocks // 2, core_count, 2, matrix.share, LANES)
        return parts.transpose(1, 0, 2, 3, 4).reshape(core_count, -1, LANES)
    folds = len(matrix.pieces)
    size = matrix.left_rows(blocks)
    row = np.arange(core_count * size)
    at_core, at = row // size, row % size
    body = at < blocks * matrix.main
    fold_at = np.maximum(at - blocks * matrix.main, 0)
    piece, fold_row = fold_at // (blocks * 16), fold_at % (blocks * 16)
    block = np.where(body, at // max(matrix.main, 1), fold_row // 16)
    inner = np.where(body, at % max(matrix.main, 1), matrix.main + fold_row % 16 - piece * matrix.rest)
    inside = body | ((fold_row % 16 >= piece * matrix.rest) & (fold_row % 16 < (piece + 1) * matrix.rest))
    column = ((block // 2 * core_count + at_core) * 2 + block % 2) * matrix.share + inner
    column = jnp.asarray(np.where(inside, column, -1), jnp.int32)
    choose = (column[:, None] == jnp.arange(depth, dtype=jnp.int32)[None, :]).astype(jnp.bfloat16)
    picked = lax.dot_general(
        choose, padded, (((1,), (1,)), ((), ())), preferred_element_type=jnp.float32
    )
    return picked.astype(jnp.bfloat16).reshape(core_count, size, LANES)


HOPS = {
    "xyz": ("seq", 1, 2, 3),
    "yxz": (1, "seq", 2, 3),
    "yzx": (1, 2, 3, "seq"),
    "zxy": (2, 3, "seq", 1),
    "zyx": (2, 3, 1, "seq"),
    "xzy": ("seq", 2, 3, 1),
}
HOP_PLAN = ["xyz", "zxy", "yzx", "yzx", "xyz", "xyz", "zyx", "yxz", "xyz", "yxz", "xyz", "xyz", "xyz", "xyz", "yzx", "xyz", "xzy"]
EVENTS = [
    ("c", 0), ("c", 1), ("c", 2), ("c", 3), ("c", 4), ("c", 5), ("c", 6), ("c", 7), ("c", 8),
    ("c", 9), ("c", 10), (0, 0), (1, 0), ("c", 11), (2, 0), ("c", 12), ("c", 13), (4, 0),
    ("c", 14), (6, 0), (3, 0), (5, 0), (7, 0), (9, 0), (1, 1), (2, 1), (0, 1), (8, 0), (6, 1),
    (3, 1), (10, 0), (2, 2), (14, 0), (0, 2), (3, 2), (4, 1), (11, 0), (5, 1), (0, 3), (14, 1),
    (8, 1), (4, 2), (6, 2), (5, 2), (12, 0), (14, 2), (10, 1), (4, 3), (13, 0), (8, 2), (5, 3),
    (11, 1), (8, 3), (10, 2), (12, 1), (15, 0), (11, 2), (10, 3), (13, 1), (16, 0), (12, 2),
    (11, 3), (7, 1), (9, 1), (13, 2), (15, 1), (16, 1), (12, 3), (13, 3), (1, 2), (7, 2), (9, 2),
    (16, 2), (2, 3), (3, 3), (15, 2), (1, 3), (7, 3), (16, 3), (6, 3), (9, 3), (14, 3), (15, 3),
]


def weight_gradients(pairs, lines, plan, bits):
    matrices, units, events = plan
    blocks = 2**bits
    dims = list(reversed(range(1, bits))) + ["seq"]
    core = lax.axis_index("dp") & 1
    operands = []
    for (left, _), matrix in zip(pairs, matrices):
        both = left_operand(left, matrix, blocks, 2)
        operands += [pick(both, core, 0), swap_dp(pick(both, 1 - core, 0), 0)]
    for _, right in pairs:
        padded = jnp.pad(right, ((0, LANES - right.shape[0]), (0, 0)))
        operands += [padded, swap_dp(padded, 0)]
    operands.append(lines)
    anywhere = pl.BlockSpec(memory_space=pl.ANY)
    vmem = pl.BlockSpec(memory_space=pltpu.VMEM)
    hops = len(dims)
    outs = [jax.ShapeDtypeStruct((unit.rows, unit.columns), jnp.float32) for unit in units]
    outs.append(jax.ShapeDtypeStruct(lines.shape[-2:], jnp.float32))
    low = jnp.bfloat16
    scratch = [pltpu.VMEM((2,) * hops + (unit.rows, unit.columns), low) for unit in units]
    for unit in units:
        for h in range(hops):
            scratch.append(pltpu.VMEM((2,) * (hops - 1 - h) + (unit.rows, unit.columns), low))
    tail = lines.shape[-2:]
    for h in range(hops + 1):
        scratch.append(pltpu.VMEM((2,) * (hops - h) + tail, jnp.float32))
    scratch.append(pltpu.VMEM((2,) * hops + tail, jnp.float32))
    folded = [matrix.fold_width for matrix in matrices if matrix.rest]
    scratch.append(pltpu.VMEM((blocks * 16, max(folded)), jnp.float32))
    scratch.append(pltpu.VMEM((2, max(m.left_rows(blocks) for m in matrices), TWO), low))
    scratch.append(pltpu.VMEM((2, TWO, max(max(w for _, w in m.pieces) for m in matrices)), low))
    scratch += [pltpu.SemaphoreType.DMA((len(units), hops))] * 2
    scratch += [pltpu.SemaphoreType.DMA((hops + 1,))] * 2
    scratch += [pltpu.SemaphoreType.DMA((2, 2))] * 2
    results = pl.pallas_call(
        functools.partial(reduce_kernel, matrices, units, events, dims),
        out_shape=outs,
        in_specs=[anywhere] * (4 * len(matrices)) + [vmem],
        out_specs=[vmem] * len(outs),
        scratch_shapes=scratch,
        compiler_params=pltpu.CompilerParams(
            collective_id=0, has_side_effects=True, vmem_limit_bytes=62 * 2**20
        ),
        name="reduce_weights",
    )(*operands)
    wholes = []
    for m, matrix in enumerate(matrices):
        mains = [r for r, u in zip(results, units) if u.matrix == m and not u.folded]
        whole = jnp.concatenate(mains, axis=1) if len(mains) > 1 else mains[0]
        if matrix.rest:
            fold = next(r for r, u in zip(results, units) if u.matrix == m and u.folded)
            parts = [
                fold[p * matrix.rest : (p + 1) * matrix.rest, :width]
                for p, (_, width) in enumerate(matrix.pieces)
            ]
            whole = jnp.concatenate([whole, jnp.concatenate(parts, axis=1)], axis=0)
        wholes.append(whole)
    return wholes, results[-1]


def even_cuts(columns, width):
    return [(start, width) for start in range(0, columns, width)]


def make_plan(width, hidden, chunks):
    matrices = [
        Matrix(hidden // chunks, width, [384] * 3, even_cuts(width, 384)),
        Matrix(width // chunks, hidden, [1152] * 4, even_cuts(hidden, 1152)),
        Matrix(width // chunks, width, [384] * 3, [(0, width)]),
        Matrix(width // chunks, 3 * width, [1152] * 3, even_cuts(3 * width, 1152)),
        Matrix(2 * width // chunks, width, [640, 512], [(0, 640), (640, 512)]),
    ]
    units = make_units(matrices, [HOPS[name] for name in HOP_PLAN])
    return matrices, units, EVENTS


def halving(block, order, bits):
    dp_index = lax.axis_index("dp")
    seq_index = lax.axis_index("seq")
    dims = list(reversed(range(1, bits))) + ["seq"]
    for name in order:
        axis = dims.index(name)
        own = seq_index if name == "seq" else (dp_index >> name) & 1
        sent = pick(block, 1 - own, axis)
        kept = pick(block, own, axis)
        got = swap_seq(sent) if name == "seq" else swap_dp(sent, name)
        total = kept.astype(jnp.float32) + got.astype(jnp.float32)
        dims.pop(axis)
        block = total.astype(jnp.bfloat16) if dims else total
    return block


def local(
    inputs,
    skipped,
    lengths,
    cotangent,
    skip_weight,
    skip_bias,
    gain_one,
    shift_one,
    qkv_weight,
    proj_weight,
    proj_bias,
    gain_two,
    shift_two,
    fc1_weight,
    fc1_bias,
    fc2_weight,
    fc2_bias,
):
    items, half, width = inputs.shape
    seq_count = lax.axis_size("seq")
    dp_count = lax.axis_size("dp")
    bits = dp_count.bit_length() - 1
    seq_index = lax.axis_index("seq")
    core = lax.axis_index("dp") & 1
    first = seq_index == 0
    slots = half * seq_count

    def whole_item(values, axis):
        own = pick(values, seq_index, 0)
        got = swap_seq(pick(values, 1 - seq_index, 0))
        return place(first, own, got, axis)

    def to_owner(values, axis):
        parts = jnp.split(values, 2, axis=axis)
        own = jnp.where(first, parts[0], parts[1])
        other = jnp.where(first, parts[1], parts[0])
        got = swap_seq(other.astype(jnp.bfloat16)).astype(values.dtype)
        return place(first, own[None], got[None], 0)

    own_inputs = whole_item(inputs, 0)
    own_skip = whole_item(skipped, 1)
    grad_out = whole_item(cotangent, 0)
    length = pick(lengths, seq_index, 0)
    rows = slots

    joined = jnp.concatenate([own_inputs, own_skip], axis=-1)
    stream = matmul(joined, skip_weight) + skip_bias
    normed = layer_norm(stream, gain_one, shift_one).astype(jnp.bfloat16)
    packed = matmul(normed, qkv_weight).astype(jnp.bfloat16)
    heads = packed.reshape(rows, 3, HEADS, HEAD_DIM)
    query, keys, values = heads[:, 0], heads[:, 1], heads[:, 2]
    scale = HEAD_DIM ** (-0.5)
    positions = jnp.arange(slots, dtype=jnp.int32)
    caption = (positions >= 1) & (positions <= length)
    image = (positions >= 1 + CAPTION) & (positions < 1 + CAPTION + IMAGE)
    valid = (positions == 0) | caption | image

    def product(spec, left, right):
        return jnp.einsum(spec, left, right, preferred_element_type=jnp.float32)

    scores = product("qhd,khd->hqk", query, keys) * scale
    scores = jnp.where(valid[None, None, :], scores, masked_score)
    top = jnp.max(scores, axis=-1, keepdims=True)
    expo = jnp.exp(scores - top)
    probs = expo / jnp.sum(expo, axis=-1, keepdims=True)
    probs_low = probs.astype(jnp.bfloat16)
    mixed = product("hqk,khd->qhd", probs_low, values)
    mixed = mixed.astype(jnp.bfloat16).reshape(rows, width)
    attended = matmul(mixed, proj_weight) + proj_bias
    stream_two = stream + attended
    normed_two = layer_norm(stream_two, gain_two, shift_two).astype(jnp.bfloat16)
    hidden = matmul(normed_two, fc1_weight) + fc1_bias
    acted, gelu_back = jax.vjp(gelu_exact, hidden)
    acted_low = acted.astype(jnp.bfloat16)
    block_output = (stream_two + (matmul(acted_low, fc2_weight) + fc2_bias)).astype(jnp.bfloat16)

    blocks = dp_count // 2

    def own_rows(left, right):
        parts = left.reshape(rows, blocks, 2, -1)
        kept = pick(parts, core, 2).reshape(rows, -1)
        sent = pick(parts, 1 - core, 2).reshape(rows, -1)
        left_both = jnp.concatenate([kept, swap_dp(sent, 0)], axis=0)
        right_both = jnp.concatenate([right, swap_dp(right, 0)], axis=0)
        total = matmul(left_both.T, right_both).astype(jnp.bfloat16)
        share = total.shape[0] // (blocks * 2)
        return total.reshape((2,) * bits + (share, right.shape[1]))

    above = list(range(1, bits))
    order_x = ["seq"] + above
    order_y = above + ["seq"]
    order_z = above[1:] + ["seq"] + above[:1]

    grad_fc2_bias = column_sum(grad_out)
    grad_acted = matmul(grad_out, fc2_weight.T)
    grad_hidden = gelu_back(grad_acted)[0].astype(jnp.bfloat16)
    grad_fc1_bias = column_sum(grad_hidden)
    grad_normed_two = matmul(grad_hidden, fc1_weight.T)
    _, norm_back_two = jax.vjp(layer_norm, stream_two, gain_two, shift_two)
    back_two, grad_gain_two, grad_shift_two = norm_back_two(grad_normed_two)
    grad_stream_two = grad_out.astype(jnp.float32) + back_two
    grad_attended = grad_stream_two.astype(jnp.bfloat16)
    grad_proj_bias = column_sum(grad_attended)
    grad_mixed = matmul(grad_attended, proj_weight.T)
    grad_mixed = grad_mixed.astype(jnp.bfloat16).reshape(rows, HEADS, HEAD_DIM)
    grad_probs = product("qhd,khd->hqk", grad_mixed, values)
    grad_scores = probs * (grad_probs - jnp.sum(probs * grad_probs, axis=-1, keepdims=True))
    grad_scores = grad_scores.astype(jnp.bfloat16)
    grad_values = product("hqk,qhd->khd", probs_low, grad_mixed)
    grad_query = product("hqk,khd->qhd", grad_scores, keys) * scale
    grad_keys = product("hqk,qhd->khd", grad_scores, query) * scale
    grad_packed = jnp.stack([grad_query, grad_keys, grad_values], axis=1)
    grad_packed = grad_packed.astype(jnp.bfloat16).reshape(rows, 3 * width)
    grad_normed = matmul(grad_packed, qkv_weight.T)
    _, norm_back_one = jax.vjp(layer_norm, stream, gain_one, shift_one)
    back_one, grad_gain_one, grad_shift_one = norm_back_one(grad_normed)
    grad_stream = (grad_stream_two + back_one).astype(jnp.bfloat16)
    grad_skip_bias = column_sum(grad_stream)
    grad_joined = matmul(grad_stream, skip_weight.T)

    vectors = (
        grad_skip_bias,
        grad_gain_one,
        grad_shift_one,
        grad_proj_bias,
        grad_gain_two,
        grad_shift_two,
        grad_fc1_bias,
        grad_fc2_bias,
    )
    chunks = dp_count * seq_count
    pairs = [
        (acted_low, grad_out),
        (normed_two, grad_hidden),
        (mixed, grad_attended),
        (normed, grad_packed),
        (joined, grad_stream),
    ]
    line = jnp.concatenate([v.reshape(chunks, -1) for v in vectors], axis=1)
    used = line.shape[1]
    if chunks == 32:
        lines = jnp.pad(line, ((0, 0), (0, 8 * 128 - used)))
        lines = lines.reshape((2,) * (bits - 1) + (2, 2, 8, 128))
        lines = jnp.moveaxis(lines, bits - 1, 0)
        plan = make_plan(width, fc1_weight.shape[1], chunks)
        weights, line = weight_gradients(pairs, lines, plan, bits)
        line = line.reshape(-1)
    else:
        orders = [order_x, order_x, order_y, order_y, order_z]
        weights = [halving(own_rows(*p), o, bits) for p, o in zip(pairs, orders)]
        line = lax.psum_scatter(line, ("dp", "seq"), scatter_dimension=0, tiled=True)[0]
    grad_fc2, grad_fc1, grad_proj, grad_qkv, grad_skip = weights
    pieces, start = [], 0
    for vector in vectors:
        size = vector.shape[0] // chunks
        pieces.append(line[start : start + size])
        start += size

    return (
        to_owner(block_output, 0),
        to_owner(grad_joined[:, :width], 0),
        to_owner(grad_joined[:, width:], 1),
        grad_skip,
        pieces[0],
        pieces[1],
        pieces[2],
        grad_qkv,
        grad_proj,
        pieces[3],
        pieces[4],
        pieces[5],
        grad_fc1,
        pieces[6],
        grad_fc2,
        pieces[7],
    )


def solution(mesh):
    return jax.shard_map(
        local,
        mesh=mesh,
        in_specs=(
            P("dp", "seq", None),
            P("dp", None, "seq"),
            P("dp"),
            P("dp", "seq", None),
        )
        + (P(),) * 13,
        out_specs=(
            P("dp", "seq", None),
            P("dp", "seq", None),
            P("dp", None, "seq"),
            P(("dp", "seq"), None),
            P(("dp", "seq")),
            P(("dp", "seq")),
            P(("dp", "seq")),
            P(("dp", "seq"), None),
            P(("dp", "seq"), None),
            P(("dp", "seq")),
            P(("dp", "seq")),
            P(("dp", "seq")),
            P(("dp", "seq"), None),
            P(("dp", "seq")),
            P(("dp", "seq"), None),
            P(("dp", "seq")),
        ),
        check_vma=False,
    )
```

```python
import functools
import types
import typing

import jax
import jax.numpy as jnp
from jax import lax
from jax.experimental import pallas as pl
from jax.experimental.pallas import tpu as pltpu
from jax.sharding import PartitionSpec as P

HEADS = 16
HEAD_DIM = 72
CAPTION = 77
IMAGE = 256


epsilon = 1e-05
masked_score = -1e30


def layer_norm(stream, gain, shift):
    center = stream - jnp.mean(stream, axis=-1, keepdims=True)
    spread = jnp.mean(center * center, axis=-1, keepdims=True)
    return center * lax.rsqrt(spread + epsilon) * gain + shift


def gelu_exact(values):
    return jax.nn.gelu(values, approximate=False)


def column_sum(values):
    return jnp.sum(values.astype(jnp.float32), axis=0)


def matmul(left, right):
    return jnp.dot(left, right, preferred_element_type=jnp.float32)


def swap_seq(values):
    return lax.ppermute(values, "seq", [(0, 1), (1, 0)])


def swap_dp(values, bit):
    count = lax.axis_size("dp")
    return lax.ppermute(values, "dp", [(i, i ^ (1 << bit)) for i in range(count)])


def pick(values, index, axis):
    return lax.dynamic_index_in_dim(values, index, axis, keepdims=False)


def place(first, own, got, axis):
    return jnp.where(
        first, jnp.concatenate([own, got], axis=axis), jnp.concatenate([got, own], axis=axis)
    )


PAD = 192
ROWS = 2 * PAD


def matmul_t(left, right):
    return lax.dot_general(
        left, right, (((1,), (1,)), ((), ())), preferred_element_type=jnp.float32
    )


def t_matmul(left, right):
    return lax.dot_general(
        left, right, (((0,), (0,)), ((), ())), preferred_element_type=jnp.float32
    )


def norm_parts(values):
    center = values - jnp.mean(values, axis=-1, keepdims=True)
    spread = jnp.mean(center * center, axis=-1, keepdims=True)
    scale = lax.rsqrt(spread + epsilon)
    return center * scale, scale


def fold_rows(values):
    rows, width = values.shape
    return jnp.sum(values.reshape(rows // 8, 8, width), axis=0)


def block_kernel(half, hidden, matrices, names, *refs):
    r = types.SimpleNamespace(**dict(zip(names, refs)))
    width = r.skip_weight.shape[1]
    seq = lax.axis_index("seq")
    core = lax.rem(lax.axis_index("dp"), 2)
    sems = r.sems
    low = jnp.bfloat16
    counter = iter(range(64))

    def copy(source, target):
        return pltpu.make_async_copy(source, target, sems.at[next(counter)])

    loads = types.SimpleNamespace(
        in0=copy(r.inputs.at[seq], r.raw_in.at[seq]),
        in1=copy(r.inputs_got, r.raw_in.at[1 - seq]),
        sk0=copy(r.skipped.at[seq], r.raw_skip.at[seq]),
        sk1=copy(r.skipped_got, r.raw_skip.at[1 - seq]),
        skip0=copy(r.skip_weight.at[pl.ds(0, width), :], r.feed.at[0]),
        skip1=copy(r.skip_weight.at[pl.ds(width, width), :], r.feed.at[1]),
        ct0=copy(r.cotangent.at[seq], r.raw_out.at[seq]),
        ct1=copy(r.cotangent_got, r.raw_out.at[1 - seq]),
        qkv=copy(r.qkv_weight, r.qkv_buffer),
        proj=copy(r.proj_weight, r.proj_buffer),
    )
    for load in vars(loads).values():
        load.start()
    chunk, feed = width, r.feed
    feeds = []
    for j in range(hidden // chunk):
        part = pl.ds(j * chunk, chunk)
        at = 2 - 2 * (j % 2)
        feeds.append(
            (
                copy(r.fc1_weight.at[:, part], feed.at[at]),
                copy(r.fc2_weight.at[part, :], feed.at[at + 1]),
            )
        )

    def start(copies):
        for item in copies:
            item.start()

    start(feeds[0])
    stores = {}

    def store(source, target):
        item = copy(source, target)
        item.start()
        stores[id(item)] = item
        return item

    def finish(item):
        stores.pop(id(item)).wait()

    joined, skips, grad_out = r.joined, r.skips, r.grad_out
    gap = PAD - half
    for load in (loads.in0, loads.in1, loads.sk0, loads.sk1):
        load.wait()
    for h in range(2):
        joined[pl.ds(h * PAD, PAD), :] = jnp.concatenate(
            [r.raw_in[h], jnp.zeros((gap, width), low)], axis=0
        )
        for f in range(2):
            skips[f, pl.ds(h * PAD, PAD), :] = jnp.concatenate(
                [r.raw_skip[f, h], jnp.zeros((gap, width // 2), low)], axis=0
            )
    loads.skip0.wait()
    loads.skip1.wait()
    stream, tile = r.stream, 384

    @pl.loop(0, width // tile)
    def _(j):
        columns = pl.ds(pl.multiple_of(j * tile, 128), tile)
        total = matmul(joined[...], feed[0, :, columns])
        total += matmul(skips[0], feed[1, pl.ds(0, width // 2), columns])
        total += matmul(skips[1], feed[1, pl.ds(width // 2, width // 2), columns])
        stream[:, columns] = total + r.skip_bias[:, columns]

    start(feeds[1])
    step = 32

    def norm(source, gain, shift, target):
        @pl.loop(0, ROWS // step)
        def _(i):
            rows = pl.ds(pl.multiple_of(i * step, step), step)
            unit, _ = norm_parts(source[rows, :])
            target[rows, :] = (unit * gain[...] + shift[...]).astype(low)

    normed, packed = r.normed, r.packed
    norm(stream, r.gain_one, r.shift_one, normed)
    loads.qkv.wait()

    @pl.loop(0, 3 * width // tile)
    def _(j):
        columns = pl.ds(pl.multiple_of(j * tile, 128), tile)
        packed[:, columns] = matmul(normed[...], r.qkv_buffer[:, columns]).astype(low)

    length = r.lengths[seq]
    at = lax.broadcasted_iota(jnp.int32, (1, ROWS), 1)
    inner = jnp.where(at >= PAD, at - PAD, at)
    position = jnp.where(at >= PAD, at - PAD + half, at)
    valid = (position == 0) | ((position >= 1) & (position <= length))
    valid = valid | ((position >= 1 + CAPTION) & (position < 1 + CAPTION + IMAGE))
    valid = valid & (inner < half)
    scale = HEAD_DIM ** (-0.5)
    window = 256

    def head_window(h):
        start = jnp.minimum(lax.div(h * HEAD_DIM, 128) * 128, width - window)
        start = pl.multiple_of(start, 128)
        lane = lax.broadcasted_iota(jnp.int32, (1, window), 1) + start
        mine = (lane >= h * HEAD_DIM) & (lane < (h + 1) * HEAD_DIM)
        return start, mine

    def part(which, start):
        return packed[:, pl.ds(pl.multiple_of(which * width + start, 128), window)]

    mixed_sum, probs = r.sum_a, r.probs

    def attend(h, carry):
        start, mine = head_window(h)
        query = jnp.where(mine, part(0, start), jnp.zeros((), low))
        scores = matmul_t(query, part(1, start)) * scale
        scores = jnp.where(valid, scores, masked_score)
        expo = jnp.exp(scores - jnp.max(scores, axis=-1, keepdims=True))
        share = expo * (1.0 / jnp.sum(expo, axis=-1, keepdims=True))
        share = share.astype(low)
        probs[h] = share
        found = matmul(share, part(2, start))
        columns = pl.ds(start, window)
        mixed_sum[:, columns] = jnp.where(mine, found, mixed_sum[:, columns])
        return carry

    lax.fori_loop(0, HEADS, attend, 0, unroll=2)
    mixed, stream_two = r.mixed, r.stream_two
    mixed[...] = mixed_sum[...].astype(low)
    loads.proj.wait()

    @pl.loop(0, width // tile)
    def _(j):
        columns = pl.ds(pl.multiple_of(j * tile, 128), tile)
        total = matmul(mixed[...], r.proj_buffer[:, columns]) + r.proj_bias[:, columns]
        stream_two[:, columns] = stream[:, columns] + total

    normed_two = r.normed_two
    norm(stream_two, r.gain_two, r.shift_two, normed_two)
    for load in (loads.ct0, loads.ct1):
        load.wait()
    for h in range(2):
        grad_out[pl.ds(h * PAD, PAD), :] = jnp.concatenate(
            [r.raw_out[h], jnp.zeros((gap, width), low)], axis=0
        )
    store(grad_out, r.right_fc2)
    sums = r.sums
    sums[7:8, :] = jnp.sum(grad_out[...].astype(jnp.float32), axis=0, keepdims=True)

    forward, backward = r.sum_a, r.sum_b
    acted, grad_hidden, staged = r.acted, r.grad_hidden, r.left_fc2_stage
    pending = {}
    for j, loading in enumerate(feeds):
        slot = j % 2
        first, second = feed.at[2 - 2 * slot], feed.at[3 - 2 * slot]
        for load in loading:
            load.wait()
        for item in pending.get(slot, ()):
            finish(item)

        @pl.loop(0, chunk // tile)
        def _(t):
            columns = pl.ds(pl.multiple_of(t * tile, 128), tile)
            whole = pl.ds(pl.multiple_of(j * chunk + t * tile, 128), tile)
            value = matmul(normed_two[...], first[:, columns])
            value += r.fc1_bias[:, whole]
            phi = 0.5 + 0.5 * lax.erf(value * (0.5**0.5))
            bell = jnp.exp(-0.5 * value * value) * ((2 * jnp.pi) ** -0.5)
            acted[slot, :, columns] = (value * phi).astype(low)
            back = matmul_t(grad_out[...], second[columns, :])
            back = (back * (phi + value * bell)).astype(low)
            grad_hidden[slot, :, columns] = back
            sums[pl.ds(8 + j, 1), columns] = jnp.sum(
                back.astype(jnp.float32), axis=0, keepdims=True
            )

        @pl.loop(0, width // tile)
        def _(t):
            columns = pl.ds(pl.multiple_of(t * tile, 128), tile)
            ahead = matmul(acted[slot], second[:, columns])
            back = matmul_t(grad_hidden[slot], first[columns, :])
            if j == 0:
                forward[:, columns] = ahead
                backward[:, columns] = back
            else:
                forward[:, columns] += ahead
                backward[:, columns] += back

        share = matrices[0].share
        turned = acted[slot].T
        groups = chunk // (4 * share)
        for g in range(groups):
            for c in range(2):
                begin = (g * 2 + c) * 2 * share
                staged[slot, c ^ core, pl.ds(g * 2 * share, 2 * share), :] = turned[
                    begin : begin + 2 * share
                ]
        count = groups * 2 * share
        pending[slot] = [
            store(staged.at[slot], r.left_fc2.at[:, pl.ds(j * count, count), :]),
            store(grad_hidden.at[slot], r.right_fc1.at[:, pl.ds(j * chunk, chunk)]),
        ]
        if j + 2 < len(feeds):
            start(feeds[j + 2])
        elif slot == 0:
            again = [copy(r.skip_weight.at[pl.ds(k * width, width), :], feed.at[2 + k]) for k in range(2)]
            start(again)

    turned_ref = r.turned
    stages = {}

    def left(m, target, sources):
        matrix = matrices[m]
        stage = r.left_stage
        if stages:
            finish(stages.pop(0))
        share, main, rest = matrix.share, matrix.main, matrix.rest
        folds, body = len(matrix.pieces), 16 * main
        first = 0
        for source in sources:
            turned_ref[pl.ds(32, width), :] = source.astype(jnp.float32).T
            for k in range(width // share):
                number = first + k
                c, block = number // 2 % 2, number // 4 * 2 + number % 2
                base = 32 + k * share
                place = c ^ core
                stage[place, pl.ds(block * main, main), :] = turned_ref[
                    pl.ds(base, main), :
                ].astype(low)
                row = lax.broadcasted_iota(jnp.int32, (16, 1), 0)
                for q in range(folds):
                    part = turned_ref[pl.ds(base + main - q * rest, 16), :]
                    part = jnp.where((row >= q * rest) & (row < (q + 1) * rest), part, 0.0)
                    stage[place, pl.ds(body + (q * 16 + block) * 16, 16), :] = part.astype(low)
            first += width // share
        rows = matrix.left_rows(16)
        stages[0] = store(stage.at[:, pl.ds(0, rows), :], target)

    left(1, r.left_fc1, [normed_two[...]])
    left(2, r.left_proj, [mixed[...]])
    left(3, r.left_qkv, [normed[...]])
    left(4, r.left_skip, [joined[...], jnp.concatenate([skips[0], skips[1]], axis=1)])

    grad_two = r.grad_two
    out_stage, grad_low = r.out_stage, r.grad_low
    for h in range(2):
        rows = pl.ds(h * PAD, half)
        value = stream_two[rows, :] + (forward[rows, :] + r.fc2_bias[...])
        out_stage[h] = value.astype(low)
    store(out_stage.at[seq], r.block_own)
    store(out_stage.at[1 - seq], r.block_send)

    def norm_back(source, gain, back, extra, target, target_low, gain_row, shift_row):
        partial = r.partial
        partial[...] = jnp.zeros_like(partial)

        @pl.loop(0, ROWS // step)
        def _(i):
            rows = pl.ds(pl.multiple_of(i * step, step), step)
            unit, spread = norm_parts(source[rows, :])
            value = back[rows, :]
            partial[0] += fold_rows(value * unit)
            partial[1] += fold_rows(value)
            value = value * gain[...]
            mean = jnp.mean(value, axis=-1, keepdims=True)
            slope = jnp.mean(value * unit, axis=-1, keepdims=True)
            value = spread * (value - mean - unit * slope)
            value = value + extra[rows, :].astype(jnp.float32)
            if target is not None:
                target[rows, :] = value
            rounded = value.astype(low)
            target_low[rows, :] = rounded
            partial[2] += fold_rows(rounded.astype(jnp.float32))

        sums[gain_row : gain_row + 1, :] = jnp.sum(partial[0], axis=0, keepdims=True)
        sums[shift_row : shift_row + 1, :] = jnp.sum(partial[1], axis=0, keepdims=True)
        return jnp.sum(partial[2], axis=0, keepdims=True)

    sums[3:4, :] = norm_back(stream_two, r.gain_two, backward, grad_out, grad_two, grad_low, 4, 5)
    store(grad_low, r.right_proj)
    grad_mixed = r.grad_mixed

    @pl.loop(0, width // tile)
    def _(j):
        columns = pl.ds(pl.multiple_of(j * tile, 128), tile)
        grad_mixed[:, columns] = matmul_t(grad_low[...], r.proj_buffer[columns, :]).astype(low)

    grad_query, grad_key, grad_value = r.sum_a, r.sum_b, r.sum_c

    def attend_back(h, carry):
        start, mine = head_window(h)
        zero = jnp.zeros((), low)
        columns = pl.ds(start, window)
        query = jnp.where(mine, part(0, start), zero)
        back = jnp.where(mine, grad_mixed[:, columns], zero)
        share = probs[h]
        grad_share = matmul_t(back, part(2, start))
        wide = share.astype(jnp.float32)
        level = jnp.sum(wide * grad_share, axis=-1, keepdims=True)
        grad_score = (wide * (grad_share - level)).astype(low)
        found = t_matmul(share, back)
        grad_value[:, columns] = jnp.where(mine, found, grad_value[:, columns])
        found = matmul(grad_score, part(1, start)) * scale
        grad_query[:, columns] = jnp.where(mine, found, grad_query[:, columns])
        found = t_matmul(grad_score, query) * scale
        grad_key[:, columns] = jnp.where(mine, found, grad_key[:, columns])
        return carry

    lax.fori_loop(0, HEADS, attend_back, 0, unroll=2)
    for k, source in enumerate((grad_query, grad_key, grad_value)):
        packed[:, pl.ds(k * width, width)] = source[...].astype(low)
    store(packed, r.right_qkv)
    grad_normed = r.sum_a

    @pl.loop(0, width // tile)
    def _(j):
        columns = pl.ds(pl.multiple_of(j * tile, 128), tile)
        grad_normed[:, columns] = matmul_t(packed[...], r.qkv_buffer[columns, :])

    grad_stream = r.grad_mixed
    sums[0:1, :] = norm_back(stream, r.gain_one, grad_normed, grad_two, None, grad_stream, 1, 2)
    store(grad_stream, r.right_skip)
    sums[12:16, :] = jnp.zeros((4, width), jnp.float32)
    sums[6:7, :] = jnp.zeros((1, width), jnp.float32)
    store(sums, r.vectors)

    back_in = r.sum_b
    for load in again:
        load.wait()

    @pl.loop(0, width // tile)
    def _(j):
        columns = pl.ds(pl.multiple_of(j * tile, 128), tile)
        back_in[:, columns] = matmul_t(grad_stream[...], feed[2, columns, :])

    store(back_in.at[pl.ds(pl.multiple_of(seq * PAD, 64), half), :], r.grad_in_own)
    send_in = r.send_in
    send_in[...] = back_in[pl.ds(pl.multiple_of((1 - seq) * PAD, 64), half), :].astype(low)
    store(send_in, r.grad_in_send)
    feature = width // 2
    for f in range(2):
        value = matmul_t(grad_stream[...], feed[3, pl.ds(f * feature, feature), :])
        for h in range(2):
            piece = value[h * PAD : h * PAD + half]

            @pl.when(seq == f)
            def _():
                r.own_skip[h] = piece

            @pl.when(seq != f)
            def _():
                r.send_skip[h] = piece.astype(low)

    store(r.own_skip, r.grad_skip_own)
    store(r.send_skip, r.grad_skip_send)
    for item in stores.values():
        item.wait()


LEFTS = ["left_fc2", "left_fc1", "left_proj", "left_qkv", "left_skip"]
RIGHTS = ["right_fc2", "right_fc1", "right_proj", "right_qkv", "right_skip"]


def run_block(arrays, matrices, width, hidden, half):
    low, wide = jnp.bfloat16, jnp.float32
    shape = jax.ShapeDtypeStruct
    outs = dict(
        block_own=shape((half, width), low),
        block_send=shape((half, width), low),
        grad_in_own=shape((half, width), wide),
        grad_in_send=shape((half, width), low),
        grad_skip_own=shape((2, half, width // 2), wide),
        grad_skip_send=shape((2, half, width // 2), low),
        vectors=shape((16, width), wide),
    )
    lefts = [shape((2, matrix.left_rows(16), ROWS), low) for matrix in matrices]
    rights = [shape((ROWS, matrix.columns), low) for matrix in matrices]
    outs.update(zip(LEFTS, lefts))
    outs.update(zip(RIGHTS, rights))
    staged = 16 * matrices[0].share // (hidden // width)
    square = (ROWS, width)
    scratch = dict(
        raw_in=((2, half, width), low),
        raw_skip=((2, 2, half, width // 2), low),
        raw_out=((2, half, width), low),
        qkv_buffer=((width, 3 * width), low),
        proj_buffer=((width, width), low),
        feed=((4, width, width), low),
        joined=(square, low),
        skips=((2, ROWS, width // 2), low),
        grad_out=(square, low),
        stream=(square, wide),
        normed=(square, low),
        packed=((ROWS, 3 * width), low),
        probs=((HEADS, ROWS, ROWS), low),
        sum_a=(square, wide),
        sum_b=(square, wide),
        sum_c=(square, wide),
        mixed=(square, low),
        stream_two=(square, wide),
        normed_two=(square, low),
        acted=((2,) + square, low),
        grad_hidden=((2,) + square, low),
        left_fc2_stage=((2, 2, staged, ROWS), low),
        left_stage=((2, max(m.left_rows(16) for m in matrices[1:]), ROWS), low),
        turned=((width + 64, ROWS), wide),
        sums=((16, width), wide),
        partial=((3, 8, width), wide),
        grad_two=(square, wide),
        out_stage=((2, half, width), low),
        grad_low=(square, low),
        grad_mixed=(square, low),
        send_in=((half, width), low),
        own_skip=((2, half, width // 2), wide),
        send_skip=((2, half, width // 2), low),
    )
    anywhere = pl.BlockSpec(memory_space=pl.ANY)
    vmem = pl.BlockSpec(memory_space=pltpu.VMEM)
    smem = pl.BlockSpec(memory_space=pltpu.SMEM)
    small = {name for name, a in arrays.items() if a.dtype == wide}
    specs = [smem if n == "lengths" else vmem if n in small else anywhere for n in arrays]
    names = list(arrays) + list(outs) + list(scratch) + ["sems"]
    results = pl.pallas_call(
        functools.partial(block_kernel, half, hidden, matrices, names),
        out_shape=list(outs.values()),
        in_specs=specs,
        out_specs=[anywhere] * len(outs),
        scratch_shapes=[pltpu.VMEM(*s) for s in scratch.values()]
        + [pltpu.SemaphoreType.DMA((64,))],
        compiler_params=pltpu.CompilerParams(vmem_limit_bytes=63 * 2**20),
        name="block",
    )(*arrays.values())
    return types.SimpleNamespace(**dict(zip(outs, results)))


MESH = pl.DeviceIdType.MESH
LANES = 384
SHIPS = 3
TWO = 2 * LANES


class Matrix:
    def __init__(self, share, columns, pieces, cuts):
        self.share, self.columns = share, columns
        self.main = share - share % 16
        self.rest = share % 16
        self.pieces, start = [], 0
        for width in pieces:
            self.pieces.append((start, width))
            start += width
        self.cuts = cuts
        self.fold = self.rest and 16
        self.fold_width = max(pieces)

    def left_rows(self, blocks):
        folds = len(self.pieces) if self.rest else 0
        return blocks * (self.main + folds * 16)


class Unit:
    def __init__(self, matrix, rows, start, columns, hops, folded):
        self.matrix, self.rows, self.start, self.columns = matrix, rows, start, columns
        self.hops, self.folded = hops, folded


def make_units(matrices, hops_of):
    units = []
    for m, matrix in enumerate(matrices):
        for start, columns in matrix.cuts:
            units.append(Unit(m, matrix.main, start, columns, hops_of[len(units)], False))
        if matrix.rest:
            units.append(Unit(m, 16, 0, matrix.fold_width, hops_of[len(units)], True))
    return units


def reduce_kernel(matrices, units, events, dims, *refs):
    count = len(matrices)
    lefts, refs = refs[:count], refs[count:]
    rights, refs = refs[:count], refs[count:]
    vector_ref, refs = refs[0], refs[1:]
    ships, refs = refs[:SHIPS], refs[SHIPS:]
    outs, refs = refs[: len(units)], refs[len(units) :]
    docks, refs = refs[:SHIPS], refs[SHIPS:]
    far_lefts, refs = refs[:count], refs[count:]
    far_rights, refs = refs[:count], refs[count:]
    vector_out, refs = refs[0], refs[1:]
    grads, refs = refs[: len(units)], refs[len(units) :]
    hops = len(dims)
    landed = [refs[i * hops : (i + 1) * hops] for i in range(len(units))]
    refs = refs[len(units) * hops :]
    vector_land, vector_sum, refs = refs[0], refs[1], refs[2:]
    fold_sum, left_buffer, right_buffer, refs = refs[0], refs[1], refs[2], refs[3:]
    send_sem, recv_sem, vsend_sem, vrecv_sem, left_sem, right_sem, *refs = refs
    xsend_sem, xrecv_sem, ship_send, ship_recv = refs

    dp = lax.axis_index("dp")
    seq = lax.axis_index("seq")
    core = lax.rem(dp, 2)

    def bit(name):
        return seq if name == "seq" else lax.rem(lax.div(dp, 1 << name), 2)

    def partner(name):
        if name == "seq":
            return (dp, 1 - seq)
        return (dp + (1 - 2 * bit(name)) * (1 << name), seq)

    barrier = pltpu.get_barrier_semaphore()
    for name in [0] + list(dims):
        pl.semaphore_signal(barrier, inc=1, device_id=partner(name), device_id_type=MESH)
    pl.semaphore_wait(barrier, len(dims) + 1)

    sent = []

    def remote(source, target, send_at, recv_at, name):
        copy = pltpu.make_async_remote_copy(
            src_ref=source,
            dst_ref=target,
            send_sem=send_at,
            recv_sem=recv_at,
            device_id=partner(name),
            device_id_type=MESH,
        )
        copy.start()
        sent.append(copy)
        return copy

    crossing = {}
    for m in range(count):
        crossing[m] = [
            remote(lefts[m].at[1], far_lefts[m], xsend_sem.at[m, 0], xrecv_sem.at[m, 0], 0),
            remote(rights[m], far_rights[m], xsend_sem.at[m, 1], xrecv_sem.at[m, 1], 0),
        ]
    arrived = set()

    def meet(m):
        if m not in arrived:
            arrived.add(m)
            for copy in crossing[m]:
                copy.wait_recv()

    def left_copies(m):
        meet(m)
        rows = matrices[m].left_rows(2 ** len(dims))
        return [
            pltpu.make_async_copy(
                (lefts[m].at[0], far_lefts[m])[k],
                left_buffer.at[m % 2, pl.ds(0, rows), pl.ds(k * LANES, LANES)],
                left_sem.at[m % 2, k],
            )
            for k in range(2)
        ]

    all_pieces = [(m, p) for m, matrix in enumerate(matrices) for p in range(len(matrix.pieces))]

    def right_copies(index):
        m, p = all_pieces[index]
        meet(m)
        start, width = matrices[m].pieces[p]
        return [
            pltpu.make_async_copy(
                (rights[m], far_rights[m])[k].at[:, pl.ds(start, width)],
                right_buffer.at[index % 2, pl.ds(k * LANES, LANES), pl.ds(0, width)],
                right_sem.at[index % 2, k],
            )
            for k in range(2)
        ]

    def start(copies):
        for copy in copies:
            copy.start()

    def wait(copies):
        for copy in copies:
            copy.wait()

    start(left_copies(0))
    for index in range(2):
        start(right_copies(index))
    start(left_copies(1))

    def send(u, h):
        unit = units[u]
        index = []
        for name in dims:
            if name in unit.hops[:h]:
                index.append(bit(name))
            elif name == unit.hops[h]:
                index.append(1 - bit(name))
            else:
                index.append(slice(None))
        return remote(
            grads[u].at[tuple(index)],
            landed[u][h],
            send_sem.at[u, h],
            recv_sem.at[u, h],
            unit.hops[h],
        )

    flying = {}

    def add(u, h):
        unit = units[u]
        flying[u, h].wait_recv()
        done = unit.hops[: h + 1]
        free = [name for name in dims if name not in done]
        step = 16
        last = h + 1 == hops

        @pl.loop(0, 2 ** len(free) * (unit.rows // step))
        def _(i):
            block, row = lax.div(i, unit.rows // step), lax.rem(i, unit.rows // step) * step
            place = {
                name: lax.rem(lax.div(block, 1 << (len(free) - 1 - k)), 2)
                for k, name in enumerate(free)
            }
            rows = pl.ds(pl.multiple_of(row, step), step)
            own = tuple(place.get(name, bit(name)) for name in dims) + (rows,)
            got = tuple(place[name] for name in free) + (rows,)
            total = grads[u][own].astype(jnp.float32) + landed[u][h][got].astype(jnp.float32)
            if last:
                outs[u][rows] = total
            else:
                grads[u][own] = total.astype(jnp.bfloat16)

    def multiply(index):
        m, p = all_pieces[index]
        matrix = matrices[m]
        start_column, width = matrix.pieces[p]
        blocks = 2 ** len(dims)
        if p == 0:
            wait(left_copies(m))
        wait(right_copies(index))
        left, right = left_buffer.at[m % 2], right_buffer.at[index % 2]
        u = next(
            i
            for i, unit in enumerate(units)
            if unit.matrix == m
            and not unit.folded
            and unit.start <= start_column < unit.start + unit.columns
        )
        group = blocks
        while group * matrix.main > 640:
            group //= 2
        free = group.bit_length() - 1
        step = next(s for s in (384, 640, 512, 128) if width % s == 0)

        @pl.loop(0, (blocks // group) * (width // step))
        def _(i):
            g, j = lax.div(i, width // step), lax.rem(i, width // step)
            rows = pl.ds(pl.multiple_of(g * (group * matrix.main), 16), group * matrix.main)
            columns = pl.ds(pl.multiple_of(j * step, 128), step)
            result = jnp.dot(left[rows, :], right[:, columns], preferred_element_type=jnp.float32)
            high = len(dims) - free
            where = tuple(lax.rem(lax.div(g, 1 << (high - 1 - k)), 2) for k in range(high))
            target = pl.ds(pl.multiple_of(start_column - units[u].start + j * step, 128), step)
            grads[u][where + (slice(None),) * (free + 1) + (target,)] = result.astype(
                jnp.bfloat16
            ).reshape((2,) * free + (matrix.main, step))

        if matrix.rest:
            offset = blocks * (matrix.main + 16 * p)

            @pl.loop(0, width // step)
            def _(j):
                columns = pl.ds(pl.multiple_of(j * step, 128), step)
                result = jnp.dot(
                    left[pl.ds(offset, blocks * 16), :],
                    right[:, columns],
                    preferred_element_type=jnp.float32,
                )
                if p == 0:
                    fold_sum[:, columns] = result
                else:
                    fold_sum[:, columns] += result

        if index + 2 < len(all_pieces):
            start(right_copies(index + 2))
        last = p + 1 == len(matrix.pieces)
        if last and m + 2 < count:
            start(left_copies(m + 2))
        if last and matrix.rest:
            f = next(i for i, unit in enumerate(units) if unit.matrix == m and unit.folded)
            folded = fold_sum[:, pl.ds(0, units[f].columns)].astype(jnp.bfloat16)
            grads[f][...] = folded.reshape((2,) * len(dims) + (16, units[f].columns))

    shipped = {}

    def ship(k):
        return remote(ships[k], docks[k], ship_send.at[k], ship_recv.at[k], "seq")

    path = [0] + list(dims)
    vector_flying = {}

    def vector_send(h):
        source = vector_ref if h == 0 else vector_sum.at[h - 1]
        return remote(source, vector_land.at[h], vsend_sem.at[h], vrecv_sem.at[h], path[h])

    def vector_add(h):
        vector_flying[h].wait_recv()
        before = vector_ref[...] if h == 0 else vector_sum[h - 1]
        total = before + vector_land[h]
        if h < hops:
            vector_sum[h] = total
            vector_flying[h + 1] = vector_send(h + 1)
        else:
            vector_out[...] = total

    vector_flying[0] = vector_send(0)
    vector_done, since = 0, 0
    for action, u, h in events:
        if action == COMPUTE:
            multiply(u)
        elif action == SEND and u == SHIP:
            shipped[h] = ship(h)
        elif action == SEND:
            flying[u, h] = send(u, h)
        elif u == SHIP:
            shipped[h].wait_recv()
        else:
            add(u, h)
            since += 1
            if since % 4 == 0 and vector_done <= hops:
                vector_add(vector_done)
                vector_done += 1
    while vector_done <= hops:
        vector_add(vector_done)
        vector_done += 1
    for copy in sent:
        copy.wait_send()


X, Y, Z, ZZ = "seq", 1, 2, 3
XYZ, YXZ, YZX = (X, Y, Z, ZZ), (Y, X, Z, ZZ), (Y, Z, ZZ, X)
ZXY, ZYX, XZY = (Z, ZZ, X, Y), (Z, ZZ, Y, X), (X, Z, ZZ, Y)
COMPUTE, SEND, TAKE, SHIP = 0, 1, 2, -1
HOP_PLAN = [YXZ, ZYX, YXZ, XYZ, XYZ, ZXY, YXZ, ZXY, YZX, XZY, YXZ, YXZ, XZY, XYZ, YXZ, XZY, XYZ]
EVENTS = [
    (SEND, SHIP, 0), (SEND, SHIP, 1), (COMPUTE, 0, 0), (SEND, 0, 0), (COMPUTE, 1, 0),
    (SEND, 1, 0), (COMPUTE, 2, 0), (SEND, 2, 0), (COMPUTE, 3, 0), (TAKE, SHIP, 0), (SEND, 3, 0),
    (COMPUTE, 4, 0), (COMPUTE, 5, 0), (SEND, 5, 0), (TAKE, SHIP, 1), (SEND, 4, 0),
    (COMPUTE, 6, 0), (COMPUTE, 7, 0), (COMPUTE, 8, 0), (SEND, 6, 0), (TAKE, 0, 0),
    (COMPUTE, 9, 0), (SEND, 7, 0), (TAKE, 1, 0), (SEND, 1, 1), (COMPUTE, 10, 0), (SEND, 0, 1),
    (TAKE, 3, 0), (COMPUTE, 11, 0), (COMPUTE, 12, 0), (COMPUTE, 13, 0), (TAKE, 5, 0),
    (SEND, 5, 1), (COMPUTE, 14, 0), (SEND, 14, 0), (TAKE, 2, 0), (SEND, 12, 0), (TAKE, 4, 0),
    (TAKE, 7, 0), (SEND, 7, 1), (TAKE, 1, 1), (SEND, 15, 0), (TAKE, 0, 1), (SEND, 0, 2),
    (SEND, 8, 0), (TAKE, 6, 0), (TAKE, 5, 1), (SEND, 2, 1), (TAKE, 12, 0), (SEND, 12, 1),
    (TAKE, 7, 1), (SEND, 10, 0), (TAKE, 14, 0), (TAKE, 0, 2), (SEND, 0, 3), (SEND, 14, 1),
    (TAKE, 15, 0), (SEND, 15, 1), (TAKE, 12, 1), (SEND, 12, 2), (TAKE, 0, 3), (SEND, 11, 0),
    (TAKE, 8, 0), (SEND, 8, 1), (TAKE, 15, 1), (SEND, 15, 2), (SEND, 13, 0), (TAKE, 2, 1),
    (SEND, 2, 2), (TAKE, 12, 2), (SEND, 6, 1), (TAKE, 14, 1), (TAKE, 15, 2), (SEND, 14, 2),
    (TAKE, 8, 1), (SEND, 8, 2), (SEND, 3, 1), (TAKE, 10, 0), (SEND, 10, 1), (TAKE, 13, 0),
    (TAKE, 2, 2), (SEND, 2, 3), (TAKE, 8, 2), (TAKE, 14, 2), (SEND, 14, 3), (SEND, 16, 0),
    (TAKE, 6, 1), (SEND, 6, 2), (SEND, 4, 1), (TAKE, 11, 0), (TAKE, 2, 3), (SEND, 11, 1),
    (TAKE, 10, 1), (SEND, 10, 2), (TAKE, 14, 3), (SEND, 1, 2), (TAKE, 3, 1), (SEND, 3, 2),
    (SEND, 5, 2), (TAKE, 16, 0), (TAKE, 6, 2), (SEND, 6, 3), (TAKE, 10, 2), (SEND, 10, 3),
    (SEND, 13, 1), (TAKE, 4, 1), (SEND, 4, 2), (SEND, 9, 0), (SEND, 7, 2), (SEND, 8, 3),
    (TAKE, 11, 1), (SEND, 11, 2), (TAKE, 6, 3), (TAKE, 3, 2), (SEND, 3, 3), (SEND, 16, 1),
    (SEND, 12, 3), (SEND, 15, 3), (TAKE, 1, 2), (SEND, 1, 3), (TAKE, 5, 2), (TAKE, 10, 3),
    (SEND, SHIP, 2), (TAKE, 9, 0), (SEND, 9, 1), (SEND, 5, 3), (TAKE, 13, 1), (SEND, 13, 2),
    (TAKE, 4, 2), (SEND, 4, 3), (TAKE, 3, 3), (TAKE, 7, 2), (SEND, 7, 3), (TAKE, 16, 1),
    (SEND, 16, 2), (TAKE, 8, 3), (TAKE, 12, 3), (TAKE, 11, 2), (SEND, 11, 3), (TAKE, 15, 3),
    (TAKE, 1, 3), (TAKE, 5, 3), (TAKE, 9, 1), (SEND, 9, 2), (TAKE, 4, 3), (TAKE, 7, 3),
    (TAKE, 13, 2), (SEND, 13, 3), (TAKE, 11, 3), (TAKE, 16, 2), (SEND, 16, 3), (TAKE, 9, 2),
    (SEND, 9, 3), (TAKE, 13, 3), (TAKE, SHIP, 2), (TAKE, 9, 3), (TAKE, 16, 3),
]


def weight_gradients(lefts, rights, vectors, ships, plan, bits):
    matrices, units, events = plan
    blocks = 2**bits
    dims = list(reversed(range(1, bits))) + ["seq"]
    operands = [*lefts, *rights, vectors, *ships]
    anywhere = pl.BlockSpec(memory_space=pl.ANY)
    vmem = pl.BlockSpec(memory_space=pltpu.VMEM)
    hops, count = len(dims), len(matrices)
    shape = jax.ShapeDtypeStruct
    outs = [shape((unit.rows, unit.columns), jnp.float32) for unit in units]
    outs += [shape(ship.shape, ship.dtype) for ship in ships]
    outs += [shape(left.shape[1:], left.dtype) for left in lefts]
    outs += [shape(right.shape, right.dtype) for right in rights]
    outs.append(shape(vectors.shape, jnp.float32))
    low = jnp.bfloat16
    scratch = [pltpu.VMEM((2,) * hops + (unit.rows, unit.columns), low) for unit in units]
    for unit in units:
        for h in range(hops):
            scratch.append(pltpu.VMEM((2,) * (hops - 1 - h) + (unit.rows, unit.columns), low))
    scratch.append(pltpu.VMEM((hops + 1,) + vectors.shape, jnp.float32))
    scratch.append(pltpu.VMEM((hops,) + vectors.shape, jnp.float32))
    folded = [matrix.fold_width for matrix in matrices if matrix.rest]
    scratch.append(pltpu.VMEM((blocks * 16, max(folded)), jnp.float32))
    scratch.append(pltpu.VMEM((2, max(m.left_rows(blocks) for m in matrices), TWO), low))
    scratch.append(pltpu.VMEM((2, TWO, max(max(w for _, w in m.pieces) for m in matrices)), low))
    scratch += [pltpu.SemaphoreType.DMA((len(units), hops))] * 2
    scratch += [pltpu.SemaphoreType.DMA((hops + 1,))] * 2
    scratch += [pltpu.SemaphoreType.DMA((2, 2))] * 2
    scratch += [pltpu.SemaphoreType.DMA((count, 2))] * 2
    scratch += [pltpu.SemaphoreType.DMA((SHIPS,))] * 2
    results = pl.pallas_call(
        functools.partial(reduce_kernel, matrices, units, events, dims),
        out_shape=outs,
        in_specs=[anywhere] * (2 * count) + [vmem] + [anywhere] * SHIPS,
        out_specs=[vmem] * len(units) + [anywhere] * (SHIPS + 2 * count) + [vmem],
        scratch_shapes=scratch,
        compiler_params=pltpu.CompilerParams(
            collective_id=0, has_side_effects=True, vmem_limit_bytes=62 * 2**20
        ),
        name="reduce_weights",
    )(*operands)
    wholes = []
    for m, matrix in enumerate(matrices):
        mains = [r for r, u in zip(results, units) if u.matrix == m and not u.folded]
        whole = jnp.concatenate(mains, axis=1) if len(mains) > 1 else mains[0]
        if matrix.rest:
            fold = next(r for r, u in zip(results, units) if u.matrix == m and u.folded)
            parts = [
                fold[p * matrix.rest : (p + 1) * matrix.rest, :width]
                for p, (_, width) in enumerate(matrix.pieces)
            ]
            whole = jnp.concatenate([whole, jnp.concatenate(parts, axis=1)], axis=0)
        wholes.append(whole)
    return wholes, results[-1], results[len(units) : len(units) + SHIPS]


def even_cuts(columns, width):
    return [(start, width) for start in range(0, columns, width)]


def make_plan(width, hidden, chunks):
    matrices = [
        Matrix(hidden // chunks, width, [384] * 3, even_cuts(width, 384)),
        Matrix(width // chunks, hidden, [1152] * 4, even_cuts(hidden, 1152)),
        Matrix(width // chunks, width, [384] * 3, [(0, width)]),
        Matrix(width // chunks, 3 * width, [1152] * 3, even_cuts(3 * width, 1152)),
        Matrix(2 * width // chunks, width, [640, 512], [(0, 640), (640, 512)]),
    ]
    units = make_units(matrices, HOP_PLAN)
    return matrices, units, EVENTS


def halving(block, order, bits):
    dp_index = lax.axis_index("dp")
    seq_index = lax.axis_index("seq")
    dims = list(reversed(range(1, bits))) + ["seq"]
    for name in order:
        axis = dims.index(name)
        own = seq_index if name == "seq" else (dp_index >> name) & 1
        sent = pick(block, 1 - own, axis)
        kept = pick(block, own, axis)
        got = swap_seq(sent) if name == "seq" else swap_dp(sent, name)
        total = kept.astype(jnp.float32) + got.astype(jnp.float32)
        dims.pop(axis)
        block = total.astype(jnp.bfloat16) if dims else total
    return block


def local_permutes(
    inputs,
    skipped,
    lengths,
    cotangent,
    skip_weight,
    skip_bias,
    gain_one,
    shift_one,
    qkv_weight,
    proj_weight,
    proj_bias,
    gain_two,
    shift_two,
    fc1_weight,
    fc1_bias,
    fc2_weight,
    fc2_bias,
):
    items, half, width = inputs.shape
    seq_count = lax.axis_size("seq")
    dp_count = lax.axis_size("dp")
    bits = dp_count.bit_length() - 1
    seq_index = lax.axis_index("seq")
    core = lax.axis_index("dp") & 1
    first = seq_index == 0
    slots = half * seq_count

    def whole_item(values, axis):
        own = pick(values, seq_index, 0)
        got = swap_seq(pick(values, 1 - seq_index, 0))
        return place(first, own, got, axis)

    def to_owner(values, axis):
        parts = jnp.split(values, 2, axis=axis)
        own = jnp.where(first, parts[0], parts[1])
        other = jnp.where(first, parts[1], parts[0])
        got = swap_seq(other.astype(jnp.bfloat16)).astype(values.dtype)
        return place(first, own[None], got[None], 0)

    own_inputs = whole_item(inputs, 0)
    own_skip = whole_item(skipped, 1)
    grad_out = whole_item(cotangent, 0)
    length = pick(lengths, seq_index, 0)
    rows = slots

    joined = jnp.concatenate([own_inputs, own_skip], axis=-1)
    stream = matmul(joined, skip_weight) + skip_bias
    normed = layer_norm(stream, gain_one, shift_one).astype(jnp.bfloat16)
    packed = matmul(normed, qkv_weight).astype(jnp.bfloat16)
    heads = packed.reshape(rows, 3, HEADS, HEAD_DIM)
    query, keys, values = heads[:, 0], heads[:, 1], heads[:, 2]
    scale = HEAD_DIM ** (-0.5)
    positions = jnp.arange(slots, dtype=jnp.int32)
    caption = (positions >= 1) & (positions <= length)
    image = (positions >= 1 + CAPTION) & (positions < 1 + CAPTION + IMAGE)
    valid = (positions == 0) | caption | image

    def product(spec, left, right):
        return jnp.einsum(spec, left, right, preferred_element_type=jnp.float32)

    scores = product("qhd,khd->hqk", query, keys) * scale
    scores = jnp.where(valid[None, None, :], scores, masked_score)
    top = jnp.max(scores, axis=-1, keepdims=True)
    expo = jnp.exp(scores - top)
    probs = expo / jnp.sum(expo, axis=-1, keepdims=True)
    probs_low = probs.astype(jnp.bfloat16)
    mixed = product("hqk,khd->qhd", probs_low, values)
    mixed = mixed.astype(jnp.bfloat16).reshape(rows, width)
    attended = matmul(mixed, proj_weight) + proj_bias
    stream_two = stream + attended
    normed_two = layer_norm(stream_two, gain_two, shift_two).astype(jnp.bfloat16)
    hidden = matmul(normed_two, fc1_weight) + fc1_bias
    acted, gelu_back = jax.vjp(gelu_exact, hidden)
    acted_low = acted.astype(jnp.bfloat16)
    block_output = (stream_two + (matmul(acted_low, fc2_weight) + fc2_bias)).astype(jnp.bfloat16)

    blocks = dp_count // 2

    def own_rows(left, right):
        parts = left.reshape(rows, blocks, 2, -1)
        kept = pick(parts, core, 2).reshape(rows, -1)
        sent = pick(parts, 1 - core, 2).reshape(rows, -1)
        left_both = jnp.concatenate([kept, swap_dp(sent, 0)], axis=0)
        right_both = jnp.concatenate([right, swap_dp(right, 0)], axis=0)
        total = matmul(left_both.T, right_both).astype(jnp.bfloat16)
        share = total.shape[0] // (blocks * 2)
        return total.reshape((2,) * bits + (share, right.shape[1]))

    above = list(range(1, bits))
    order_x = ["seq"] + above
    order_y = above + ["seq"]
    order_z = above[1:] + ["seq"] + above[:1]

    grad_fc2 = halving(own_rows(acted_low, grad_out), order_x, bits)
    grad_fc2_bias = column_sum(grad_out)
    grad_acted = matmul(grad_out, fc2_weight.T)
    grad_hidden = gelu_back(grad_acted)[0].astype(jnp.bfloat16)
    grad_fc1 = halving(own_rows(normed_two, grad_hidden), order_x, bits)
    grad_fc1_bias = column_sum(grad_hidden)
    grad_normed_two = matmul(grad_hidden, fc1_weight.T)
    _, norm_back_two = jax.vjp(layer_norm, stream_two, gain_two, shift_two)
    back_two, grad_gain_two, grad_shift_two = norm_back_two(grad_normed_two)
    grad_stream_two = grad_out.astype(jnp.float32) + back_two
    grad_attended = grad_stream_two.astype(jnp.bfloat16)
    grad_proj = halving(own_rows(mixed, grad_attended), order_y, bits)
    grad_proj_bias = column_sum(grad_attended)
    grad_mixed = matmul(grad_attended, proj_weight.T)
    grad_mixed = grad_mixed.astype(jnp.bfloat16).reshape(rows, HEADS, HEAD_DIM)
    grad_probs = product("qhd,khd->hqk", grad_mixed, values)
    grad_scores = probs * (grad_probs - jnp.sum(probs * grad_probs, axis=-1, keepdims=True))
    grad_scores = grad_scores.astype(jnp.bfloat16)
    grad_values = product("hqk,qhd->khd", probs_low, grad_mixed)
    grad_query = product("hqk,khd->qhd", grad_scores, keys) * scale
    grad_keys = product("hqk,qhd->khd", grad_scores, query) * scale
    grad_packed = jnp.stack([grad_query, grad_keys, grad_values], axis=1)
    grad_packed = grad_packed.astype(jnp.bfloat16).reshape(rows, 3 * width)
    grad_qkv = halving(own_rows(normed, grad_packed), order_y, bits)
    grad_normed = matmul(grad_packed, qkv_weight.T)
    _, norm_back_one = jax.vjp(layer_norm, stream, gain_one, shift_one)
    back_one, grad_gain_one, grad_shift_one = norm_back_one(grad_normed)
    grad_stream = (grad_stream_two + back_one).astype(jnp.bfloat16)
    grad_skip = halving(own_rows(joined, grad_stream), order_z, bits)
    grad_skip_bias = column_sum(grad_stream)
    grad_joined = matmul(grad_stream, skip_weight.T)

    vectors = (
        grad_skip_bias,
        grad_gain_one,
        grad_shift_one,
        grad_proj_bias,
        grad_gain_two,
        grad_shift_two,
        grad_fc1_bias,
        grad_fc2_bias,
    )
    chunks = dp_count * seq_count
    line = jnp.concatenate([v.reshape(chunks, -1) for v in vectors], axis=1)
    line = lax.psum_scatter(line, ("dp", "seq"), scatter_dimension=0, tiled=True)[0]
    pieces, start = [], 0
    for vector in vectors:
        size = vector.shape[0] // chunks
        pieces.append(line[start : start + size])
        start += size

    return (
        to_owner(block_output, 0),
        to_owner(grad_joined[:, :width], 0),
        to_owner(grad_joined[:, width:], 1),
        grad_skip,
        pieces[0],
        pieces[1],
        pieces[2],
        grad_qkv,
        grad_proj,
        pieces[3],
        pieces[4],
        pieces[5],
        grad_fc1,
        pieces[6],
        grad_fc2,
        pieces[7],
    )


def local_kernels(*arguments):
    arrays = Arguments(*arguments)
    items, half, width = arrays.inputs.shape
    hidden = arrays.fc1_weight.shape[1]
    dp_count = lax.axis_size("dp")
    bits = dp_count.bit_length() - 1
    seq_index = lax.axis_index("seq")
    device = lax.axis_index("dp") * 2 + seq_index
    first = seq_index == 0
    chunks = dp_count * 2
    skipped = arrays.skipped.reshape(items, 2, half, width // 2)
    plan = make_plan(width, hidden, chunks)
    feed = dict(
        inputs=arrays.inputs,
        inputs_got=swap_seq(pick(arrays.inputs, 1 - seq_index, 0)),
        skipped=skipped,
        skipped_got=swap_seq(pick(skipped, 1 - seq_index, 0)),
        cotangent=arrays.cotangent,
        cotangent_got=swap_seq(pick(arrays.cotangent, 1 - seq_index, 0)),
        lengths=arrays.lengths,
    )
    for name in Arguments._fields[4:]:
        value = getattr(arrays, name)
        feed[name] = value if value.ndim == 2 else value.reshape(1, -1)
    found = run_block(feed, plan[0], width, hidden, half)
    weights, vectors, got = weight_gradients(
        [getattr(found, name) for name in LEFTS],
        [getattr(found, name) for name in RIGHTS],
        found.vectors,
        [found.block_send, found.grad_in_send, found.grad_skip_send],
        plan,
        bits,
    )
    block_got, grad_in_got, grad_skip_got = got

    def owner(own, other):
        other = other.astype(own.dtype)
        return jnp.where(first, jnp.stack([own, other]), jnp.stack([other, own]))

    share = width // chunks
    mine = lax.dynamic_slice(vectors, (0, device * share), (8, share))
    wide_share = hidden // chunks
    per_row = width // wide_share
    row = 8 + device // per_row
    bias = lax.dynamic_slice(vectors, (row, device % per_row * wide_share), (1, wide_share))[0]
    grad_fc2, grad_fc1, grad_proj, grad_qkv, grad_skip = weights
    grad_skip_own = found.grad_skip_own.reshape(2 * half, -1)
    return (
        owner(found.block_own, block_got),
        owner(found.grad_in_own, grad_in_got),
        owner(grad_skip_own, grad_skip_got.reshape(2 * half, -1)),
        grad_skip,
        mine[0],
        mine[1],
        mine[2],
        grad_qkv,
        grad_proj,
        mine[3],
        mine[4],
        mine[5],
        grad_fc1,
        bias,
        grad_fc2,
        mine[7],
    )


class Arguments(typing.NamedTuple):
    inputs: jax.Array
    skipped: jax.Array
    lengths: jax.Array
    cotangent: jax.Array
    skip_weight: jax.Array
    skip_bias: jax.Array
    gain_one: jax.Array
    shift_one: jax.Array
    qkv_weight: jax.Array
    proj_weight: jax.Array
    proj_bias: jax.Array
    gain_two: jax.Array
    shift_two: jax.Array
    fc1_weight: jax.Array
    fc1_bias: jax.Array
    fc2_weight: jax.Array
    fc2_bias: jax.Array


def solution(mesh):
    small = mesh.shape["dp"] == 16
    return jax.shard_map(
        local_kernels if small else local_permutes,
        mesh=mesh,
        in_specs=(
            P("dp", "seq", None),
            P("dp", None, "seq"),
            P("dp"),
            P("dp", "seq", None),
        )
        + (P(),) * 13,
        out_specs=(
            P("dp", "seq", None),
            P("dp", "seq", None),
            P("dp", None, "seq"),
            P(("dp", "seq"), None),
            P(("dp", "seq")),
            P(("dp", "seq")),
            P(("dp", "seq")),
            P(("dp", "seq"), None),
            P(("dp", "seq"), None),
            P(("dp", "seq")),
            P(("dp", "seq")),
            P(("dp", "seq")),
            P(("dp", "seq"), None),
            P(("dp", "seq")),
            P(("dp", "seq"), None),
            P(("dp", "seq")),
        ),
        check_vma=False,
    )
```

```python
import functools
import types
import typing

import jax
import jax.numpy as jnp
from jax import lax
from jax.experimental import pallas as pl
from jax.experimental.pallas import tpu as pltpu
from jax.sharding import PartitionSpec as P

HEADS = 16
HEAD_DIM = 72
CAPTION = 77
IMAGE = 256


epsilon = 1e-05
masked_score = -1e30


def layer_norm(stream, gain, shift):
    center = stream - jnp.mean(stream, axis=-1, keepdims=True)
    spread = jnp.mean(center * center, axis=-1, keepdims=True)
    return center * lax.rsqrt(spread + epsilon) * gain + shift


def gelu_exact(values):
    return jax.nn.gelu(values, approximate=False)


def column_sum(values):
    return jnp.sum(values.astype(jnp.float32), axis=0)


def matmul(left, right):
    return jnp.dot(left, right, preferred_element_type=jnp.float32)


def swap_seq(values):
    return lax.ppermute(values, "seq", [(0, 1), (1, 0)])


def swap_dp(values, bit):
    count = lax.axis_size("dp")
    return lax.ppermute(values, "dp", [(i, i ^ (1 << bit)) for i in range(count)])


def pick(values, index, axis):
    return lax.dynamic_index_in_dim(values, index, axis, keepdims=False)


def place(first, own, got, axis):
    return jnp.where(
        first, jnp.concatenate([own, got], axis=axis), jnp.concatenate([got, own], axis=axis)
    )


PAD = 192
ROWS = 2 * PAD


def matmul_t(left, right):
    return lax.dot_general(
        left, right, (((1,), (1,)), ((), ())), preferred_element_type=jnp.float32
    )


def t_matmul(left, right):
    return lax.dot_general(
        left, right, (((0,), (0,)), ((), ())), preferred_element_type=jnp.float32
    )


def tiles_of(width):
    starts = list(range(0, width - 255, 512))
    ends = starts[1:] + [width]
    return [pl.ds(a, b - a) for a, b in zip(starts, ends)]


def norm_parts(values):
    center = values - jnp.mean(values, axis=-1, keepdims=True)
    spread = jnp.mean(center * center, axis=-1, keepdims=True)
    scale = lax.rsqrt(spread + epsilon)
    return center * scale, scale


def fold_rows(values):
    rows, width = values.shape
    return jnp.sum(values.reshape(rows // 8, 8, width), axis=0)


def block_kernel(half, hidden, matrices, names, *refs):
    r = types.SimpleNamespace(**dict(zip(names, refs)))
    width = r.skip_weight.shape[1]
    seq = lax.axis_index("seq")
    core = lax.rem(lax.axis_index("dp"), 2)
    sems = r.sems
    low = jnp.bfloat16
    counter = iter(range(64))

    def copy(source, target):
        return pltpu.make_async_copy(source, target, sems.at[next(counter)])

    loads = types.SimpleNamespace(
        in0=copy(r.inputs.at[seq], r.raw_in.at[seq]),
        sk0=copy(r.skipped.at[seq], r.raw_skip.at[seq]),
        skip0=copy(r.skip_weight.at[pl.ds(0, width), :], r.feed.at[0]),
        skip1=copy(r.skip_weight.at[pl.ds(width, width), :], r.feed.at[1]),
        ct0=copy(r.cotangent.at[seq], r.raw_out.at[seq]),
        qkv=copy(r.qkv_weight, r.qkv_buffer),
        proj=copy(r.proj_weight, r.proj_buffer),
    )
    neighbour = (lax.axis_index("dp"), 1 - seq)
    barrier = pltpu.get_barrier_semaphore()
    pl.semaphore_signal(barrier, inc=1, device_id=neighbour, device_id_type=MESH)
    for load in vars(loads).values():
        load.start()
    pl.semaphore_wait(barrier, 1)

    def trade(k, source, landing):
        return pltpu.make_async_remote_copy(
            src_ref=source.at[1 - seq],
            dst_ref=landing.at[seq],
            send_sem=r.send_sem.at[k],
            recv_sem=r.recv_sem.at[k],
            device_id=neighbour,
            device_id_type=MESH,
        )

    traded = [
        trade(0, r.inputs, r.raw_in),
        trade(1, r.skipped, r.raw_skip),
        trade(2, r.cotangent, r.raw_out),
    ]
    traded[0].start()
    traded[1].start()
    chunk, feed = width, r.feed
    feeds = []
    for j in range(hidden // chunk):
        part = pl.ds(j * chunk, chunk)
        at = 2 - 2 * (j % 2)
        feeds.append(
            (
                copy(r.fc1_weight.at[:, part], feed.at[at]),
                copy(r.fc2_weight.at[part, :], feed.at[at + 1]),
            )
        )

    def start(copies):
        for item in copies:
            item.start()

    start(feeds[0])
    stores = {}

    def store(source, target):
        item = copy(source, target)
        item.start()
        stores[id(item)] = item
        return item

    def finish(item):
        stores.pop(id(item)).wait()

    joined, skips, grad_out = r.joined, r.skips, r.grad_out
    gap = PAD - half
    for load in (loads.in0, loads.sk0, traded[0], traded[1]):
        load.wait()
    traded[2].start()
    for h in range(2):
        joined[pl.ds(h * PAD, PAD), :] = jnp.concatenate(
            [r.raw_in[h], jnp.zeros((gap, width), low)], axis=0
        )
        for f in range(2):
            skips[f, pl.ds(h * PAD, PAD), :] = jnp.concatenate(
                [r.raw_skip[f, h], jnp.zeros((gap, width // 2), low)], axis=0
            )
    loads.skip0.wait()
    loads.skip1.wait()
    stream = r.stream
    tiles = tiles_of(width)

    for columns in tiles:
        total = matmul(joined[...], feed[0, :, columns])
        total += matmul(skips[0], feed[1, pl.ds(0, width // 2), columns])
        total += matmul(skips[1], feed[1, pl.ds(width // 2, width // 2), columns])
        stream[:, columns] = total + r.skip_bias[columns]

    start(feeds[1])
    step = 128

    def norm(source, gain, shift, target):
        @pl.loop(0, ROWS // step)
        def _(i):
            rows = pl.ds(pl.multiple_of(i * step, step), step)
            unit, _ = norm_parts(source[rows, :])
            target[rows, :] = (unit * gain[...] + shift[...]).astype(low)

    normed, packed = r.normed, r.packed
    norm(stream, r.gain_one, r.shift_one, normed)
    loads.qkv.wait()

    for columns in tiles_of(3 * width):
        packed[:, columns] = matmul(normed[...], r.qkv_buffer[:, columns]).astype(low)

    length = r.lengths[seq]
    at = lax.broadcasted_iota(jnp.int32, (1, ROWS), 1)
    inner = jnp.where(at >= PAD, at - PAD, at)
    position = jnp.where(at >= PAD, at - PAD + half, at)
    valid = (position == 0) | ((position >= 1) & (position <= length))
    valid = valid | ((position >= 1 + CAPTION) & (position < 1 + CAPTION + IMAGE))
    valid = valid & (inner < half)
    scale = HEAD_DIM ** (-0.5)
    window = 256

    def head_window(h):
        start = jnp.minimum(lax.div(h * HEAD_DIM, 128) * 128, width - window)
        start = pl.multiple_of(start, 128)
        lane = lax.broadcasted_iota(jnp.int32, (1, window), 1) + start
        mine = (lane >= h * HEAD_DIM) & (lane < (h + 1) * HEAD_DIM)
        return start, mine

    def part(which, start):
        return packed[:, pl.ds(pl.multiple_of(which * width + start, 128), window)]

    mixed_sum, probs = r.sum_a, r.probs

    def attend(h, carry):
        start, mine = head_window(h)
        query = jnp.where(mine, part(0, start), jnp.zeros((), low))
        scores = matmul_t(query, part(1, start)) * scale
        scores = jnp.where(valid, scores, masked_score)
        expo = jnp.exp(scores - jnp.max(scores, axis=-1, keepdims=True))
        share = expo * (1.0 / jnp.sum(expo, axis=-1, keepdims=True))
        share = share.astype(low)
        probs[h] = share
        found = matmul(share, part(2, start))
        columns = pl.ds(start, window)
        mixed_sum[:, columns] = jnp.where(mine, found, mixed_sum[:, columns])
        return carry

    lax.fori_loop(0, HEADS, attend, 0, unroll=4)
    mixed, stream_two = r.mixed, r.stream_two
    mixed[...] = mixed_sum[...].astype(low)
    loads.proj.wait()

    for columns in tiles:
        total = matmul(mixed[...], r.proj_buffer[:, columns]) + r.proj_bias[columns]
        stream_two[:, columns] = stream[:, columns] + total

    normed_two = r.normed_two
    norm(stream_two, r.gain_two, r.shift_two, normed_two)
    for load in (loads.ct0, traded[2]):
        load.wait()
    for h in range(2):
        grad_out[pl.ds(h * PAD, PAD), :] = jnp.concatenate(
            [r.raw_out[h], jnp.zeros((gap, width), low)], axis=0
        )
    store(grad_out, r.right_fc2)
    sums = r.sums
    sums[7:8, :] = jnp.sum(grad_out[...].astype(jnp.float32), axis=0, keepdims=True)

    forward, backward = r.sum_a, r.sum_b
    acted, grad_hidden, staged = r.acted, r.grad_hidden, r.left_fc2_stage
    pending = {}
    for j, loading in enumerate(feeds):
        slot = j % 2
        first, second = feed.at[2 - 2 * slot], feed.at[3 - 2 * slot]
        for load in loading:
            load.wait()
        for item in pending.get(slot, ()):
            finish(item)

        for columns in tiles:
            whole = pl.ds(j * chunk + columns.start, columns.size)
            value = matmul(normed_two[...], first[:, columns])
            value += r.fc1_bias[whole]
            phi = 0.5 + 0.5 * lax.erf(value * (0.5**0.5))
            bell = jnp.exp(-0.5 * value * value) * ((2 * jnp.pi) ** -0.5)
            acted[slot, :, columns] = (value * phi).astype(low)
            back = matmul_t(grad_out[...], second[columns, :])
            back = (back * (phi + value * bell)).astype(low)
            grad_hidden[slot, :, columns] = back
            sums[pl.ds(8 + j, 1), columns] = jnp.sum(
                back.astype(jnp.float32), axis=0, keepdims=True
            )

        for columns in tiles:
            ahead = matmul(acted[slot], second[:, columns])
            back = matmul_t(grad_hidden[slot], first[columns, :])
            if j == 0:
                forward[:, columns] = ahead
                backward[:, columns] = back
            else:
                forward[:, columns] += ahead
                backward[:, columns] += back

        share = matrices[0].share
        turned = acted[slot].T
        groups = chunk // (4 * share)
        for g in range(groups):
            for c in range(2):
                begin = (g * 2 + c) * 2 * share
                staged[slot, c ^ core, pl.ds(g * 2 * share, 2 * share), :] = turned[
                    begin : begin + 2 * share
                ]
        count = groups * 2 * share
        pending[slot] = [
            store(staged.at[slot], r.left_fc2.at[:, pl.ds(j * count, count), :]),
            store(grad_hidden.at[slot], r.right_fc1.at[:, pl.ds(j * chunk, chunk)]),
        ]
        if j + 2 < len(feeds):
            start(feeds[j + 2])
        elif slot == 0:
            again = [copy(r.skip_weight.at[pl.ds(k * width, width), :], feed.at[2 + k]) for k in range(2)]
            start(again)

    turned_ref = r.turned
    stages = {}

    def left(m, target, sources):
        matrix = matrices[m]
        stage = r.left_stage
        if stages:
            finish(stages.pop(0))
        share, main, rest = matrix.share, matrix.main, matrix.rest
        folds, body = len(matrix.pieces), 16 * main
        first = 0
        for source in sources:
            turned_ref[pl.ds(32, width), :] = source.astype(jnp.float32).T
            for k in range(width // share):
                number = first + k
                c, block = number // 2 % 2, number // 4 * 2 + number % 2
                base = 32 + k * share
                place = c ^ core
                stage[place, pl.ds(block * main, main), :] = turned_ref[
                    pl.ds(base, main), :
                ].astype(low)
                row = lax.broadcasted_iota(jnp.int32, (16, 1), 0)
                for q in range(folds):
                    part = turned_ref[pl.ds(base + main - q * rest, 16), :]
                    part = jnp.where((row >= q * rest) & (row < (q + 1) * rest), part, 0.0)
                    stage[place, pl.ds(body + (q * 16 + block) * 16, 16), :] = part.astype(low)
            first += width // share
        rows = matrix.left_rows(16)
        stages[0] = store(stage.at[:, pl.ds(0, rows), :], target)

    left(1, r.left_fc1, [normed_two[...]])
    left(2, r.left_proj, [mixed[...]])
    left(3, r.left_qkv, [normed[...]])
    left(4, r.left_skip, [joined[...], jnp.concatenate([skips[0], skips[1]], axis=1)])

    grad_two = r.grad_two
    out_stage, grad_low = r.out_stage, r.grad_low
    for h in range(2):
        rows = pl.ds(h * PAD, half)
        value = stream_two[rows, :] + (forward[rows, :] + r.fc2_bias[...])
        out_stage[h] = value.astype(low)
    store(out_stage.at[seq], r.block_own)
    store(out_stage.at[1 - seq], r.block_send)

    def norm_back(source, gain, back, extra, target, target_low, gain_row, shift_row):
        partial = r.partial
        partial[...] = jnp.zeros_like(partial)

        @pl.loop(0, ROWS // step)
        def _(i):
            rows = pl.ds(pl.multiple_of(i * step, step), step)
            unit, spread = norm_parts(source[rows, :])
            value = back[rows, :]
            partial[0] += fold_rows(value * unit)
            partial[1] += fold_rows(value)
            value = value * gain[...]
            mean = jnp.mean(value, axis=-1, keepdims=True)
            slope = jnp.mean(value * unit, axis=-1, keepdims=True)
            value = spread * (value - mean - unit * slope)
            value = value + extra[rows, :].astype(jnp.float32)
            if target is not None:
                target[rows, :] = value
            rounded = value.astype(low)
            target_low[rows, :] = rounded
            partial[2] += fold_rows(rounded.astype(jnp.float32))

        sums[gain_row : gain_row + 1, :] = jnp.sum(partial[0], axis=0, keepdims=True)
        sums[shift_row : shift_row + 1, :] = jnp.sum(partial[1], axis=0, keepdims=True)
        return jnp.sum(partial[2], axis=0, keepdims=True)

    sums[3:4, :] = norm_back(stream_two, r.gain_two, backward, grad_out, grad_two, grad_low, 4, 5)
    store(grad_low, r.right_proj)
    grad_mixed = r.grad_mixed

    for columns in tiles:
        grad_mixed[:, columns] = matmul_t(grad_low[...], r.proj_buffer[columns, :]).astype(low)

    grad_query, grad_key, grad_value = r.sum_a, r.sum_b, r.sum_c

    def attend_back(h, carry):
        start, mine = head_window(h)
        zero = jnp.zeros((), low)
        columns = pl.ds(start, window)
        query = jnp.where(mine, part(0, start), zero)
        back = jnp.where(mine, grad_mixed[:, columns], zero)
        share = probs[h]
        grad_share = matmul_t(back, part(2, start))
        wide = share.astype(jnp.float32)
        level = jnp.sum(wide * grad_share, axis=-1, keepdims=True)
        grad_score = (wide * (grad_share - level)).astype(low)
        found = t_matmul(share, back)
        grad_value[:, columns] = jnp.where(mine, found, grad_value[:, columns])
        found = matmul(grad_score, part(1, start)) * scale
        grad_query[:, columns] = jnp.where(mine, found, grad_query[:, columns])
        found = t_matmul(grad_score, query) * scale
        grad_key[:, columns] = jnp.where(mine, found, grad_key[:, columns])
        return carry

    lax.fori_loop(0, HEADS, attend_back, 0, unroll=4)
    for k, source in enumerate((grad_query, grad_key, grad_value)):
        packed[:, pl.ds(k * width, width)] = source[...].astype(low)
    store(packed, r.right_qkv)
    grad_normed = r.sum_a

    for columns in tiles:
        grad_normed[:, columns] = matmul_t(packed[...], r.qkv_buffer[columns, :])

    grad_stream = r.grad_mixed
    sums[0:1, :] = norm_back(stream, r.gain_one, grad_normed, grad_two, None, grad_stream, 1, 2)
    store(grad_stream, r.right_skip)
    sums[12:16, :] = jnp.zeros((4, width), jnp.float32)
    sums[6:7, :] = jnp.zeros((1, width), jnp.float32)
    store(sums, r.vectors)

    back_in = r.sum_b
    for load in again:
        load.wait()

    for columns in tiles:
        back_in[:, columns] = matmul_t(grad_stream[...], feed[2, columns, :])

    store(back_in.at[pl.ds(pl.multiple_of(seq * PAD, 64), half), :], r.grad_in_own)
    send_in = r.send_in
    send_in[...] = back_in[pl.ds(pl.multiple_of((1 - seq) * PAD, 64), half), :].astype(low)
    store(send_in, r.grad_in_send)
    feature = width // 2
    for f in range(2):
        value = matmul_t(grad_stream[...], feed[3, pl.ds(f * feature, feature), :])
        for h in range(2):
            piece = value[h * PAD : h * PAD + half]

            @pl.when(seq == f)
            def _():
                r.own_skip[h] = piece

            @pl.when(seq != f)
            def _():
                r.send_skip[h] = piece.astype(low)

    store(r.own_skip, r.grad_skip_own)
    store(r.send_skip, r.grad_skip_send)
    for item in stores.values():
        item.wait()


LEFTS = ["left_fc2", "left_fc1", "left_proj", "left_qkv", "left_skip"]
RIGHTS = ["right_fc2", "right_fc1", "right_proj", "right_qkv", "right_skip"]


def run_block(arrays, matrices, width, hidden, half):
    low, wide = jnp.bfloat16, jnp.float32
    shape = jax.ShapeDtypeStruct
    outs = dict(
        block_own=shape((half, width), low),
        block_send=shape((half, width), low),
        grad_in_own=shape((half, width), wide),
        grad_in_send=shape((half, width), low),
        grad_skip_own=shape((2, half, width // 2), wide),
        grad_skip_send=shape((2, half, width // 2), low),
        vectors=shape((16, width), wide),
    )
    lefts = [shape((2, matrix.left_rows(16), ROWS), low) for matrix in matrices]
    rights = [shape((ROWS, matrix.columns), low) for matrix in matrices]
    outs.update(zip(LEFTS, lefts))
    outs.update(zip(RIGHTS, rights))
    staged = 16 * matrices[0].share // (hidden // width)
    square = (ROWS, width)
    scratch = dict(
        raw_in=((2, half, width), low),
        raw_skip=((2, 2, half, width // 2), low),
        raw_out=((2, half, width), low),
        qkv_buffer=((width, 3 * width), low),
        proj_buffer=((width, width), low),
        feed=((4, width, width), low),
        joined=(square, low),
        skips=((2, ROWS, width // 2), low),
        grad_out=(square, low),
        stream=(square, wide),
        normed=(square, low),
        packed=((ROWS, 3 * width), low),
        probs=((HEADS, ROWS, ROWS), low),
        sum_a=(square, wide),
        sum_b=(square, wide),
        sum_c=(square, wide),
        mixed=(square, low),
        stream_two=(square, wide),
        normed_two=(square, low),
        acted=((2,) + square, low),
        grad_hidden=((2,) + square, low),
        left_fc2_stage=((2, 2, staged, ROWS), low),
        left_stage=((2, max(m.left_rows(16) for m in matrices[1:]), ROWS), low),
        turned=((width + 64, ROWS), wide),
        sums=((16, width), wide),
        partial=((3, 8, width), wide),
        grad_two=(square, wide),
        out_stage=((2, half, width), low),
        grad_low=(square, low),
        grad_mixed=(square, low),
        send_in=((half, width), low),
        own_skip=((2, half, width // 2), wide),
        send_skip=((2, half, width // 2), low),
    )
    anywhere = pl.BlockSpec(memory_space=pl.ANY)
    vmem = pl.BlockSpec(memory_space=pltpu.VMEM)
    smem = pl.BlockSpec(memory_space=pltpu.SMEM)
    small = {name for name, a in arrays.items() if a.dtype == wide}
    specs = [smem if n == "lengths" else vmem if n in small else anywhere for n in arrays]
    names = list(arrays) + list(outs) + list(scratch) + ["sems", "send_sem", "recv_sem"]
    results = pl.pallas_call(
        functools.partial(block_kernel, half, hidden, matrices, names),
        out_shape=list(outs.values()),
        in_specs=specs,
        out_specs=[anywhere] * len(outs),
        scratch_shapes=[pltpu.VMEM(*s) for s in scratch.values()]
        + [pltpu.SemaphoreType.DMA((n,)) for n in (64, 3, 3)],
        compiler_params=pltpu.CompilerParams(
            collective_id=1, has_side_effects=True, vmem_limit_bytes=63 * 2**20
        ),
        name="block",
    )(*arrays.values())
    return types.SimpleNamespace(**dict(zip(outs, results)))


MESH = pl.DeviceIdType.MESH
LANES = 384
SHIPS = 3
TWO = 2 * LANES


class Matrix:
    def __init__(self, share, columns, pieces, cuts):
        self.share, self.columns = share, columns
        self.main = share - share % 16
        self.rest = share % 16
        self.pieces, start = [], 0
        for width in pieces:
            self.pieces.append((start, width))
            start += width
        self.cuts = cuts
        self.fold = self.rest and 16
        self.fold_width = max(pieces)

    def left_rows(self, blocks):
        folds = len(self.pieces) if self.rest else 0
        return blocks * (self.main + folds * 16)


class Unit:
    def __init__(self, matrix, rows, start, columns, hops, folded):
        self.matrix, self.rows, self.start, self.columns = matrix, rows, start, columns
        self.hops, self.folded = hops, folded


def make_units(matrices, hops_of):
    units = []
    for m, matrix in enumerate(matrices):
        for start, columns in matrix.cuts:
            units.append(Unit(m, matrix.main, start, columns, hops_of[len(units)], False))
        if matrix.rest:
            units.append(Unit(m, 16, 0, matrix.fold_width, hops_of[len(units)], True))
    return units


def reduce_kernel(matrices, units, events, dims, *refs):
    count = len(matrices)
    lefts, refs = refs[:count], refs[count:]
    rights, refs = refs[:count], refs[count:]
    vector_ref, refs = refs[0], refs[1:]
    ships, refs = refs[:SHIPS], refs[SHIPS:]
    outs, refs = refs[: len(units)], refs[len(units) :]
    docks, refs = refs[:SHIPS], refs[SHIPS:]
    far_lefts, refs = refs[:count], refs[count:]
    far_rights, refs = refs[:count], refs[count:]
    vector_out, refs = refs[0], refs[1:]
    grads, refs = refs[: len(units)], refs[len(units) :]
    hops = len(dims)
    landed = [refs[i * hops : (i + 1) * hops] for i in range(len(units))]
    refs = refs[len(units) * hops :]
    vector_land, vector_sum, refs = refs[0], refs[1], refs[2:]
    fold_sum, left_buffer, right_buffer, refs = refs[0], refs[1], refs[2], refs[3:]
    send_sem, recv_sem, vsend_sem, vrecv_sem, left_sem, right_sem, *refs = refs
    xsend_sem, xrecv_sem, ship_send, ship_recv = refs

    dp = lax.axis_index("dp")
    seq = lax.axis_index("seq")
    core = lax.rem(dp, 2)

    def bit(name):
        return seq if name == "seq" else lax.rem(lax.div(dp, 1 << name), 2)

    def partner(name):
        if name == "seq":
            return (dp, 1 - seq)
        return (dp + (1 - 2 * bit(name)) * (1 << name), seq)

    barrier = pltpu.get_barrier_semaphore()
    for name in [0] + list(dims):
        pl.semaphore_signal(barrier, inc=1, device_id=partner(name), device_id_type=MESH)
    pl.semaphore_wait(barrier, len(dims) + 1)

    sent = []

    def remote(source, target, send_at, recv_at, name):
        copy = pltpu.make_async_remote_copy(
            src_ref=source,
            dst_ref=target,
            send_sem=send_at,
            recv_sem=recv_at,
            device_id=partner(name),
            device_id_type=MESH,
        )
        copy.start()
        sent.append(copy)
        return copy

    crossing = {}
    for m in range(count):
        crossing[m] = [
            remote(lefts[m].at[1], far_lefts[m], xsend_sem.at[m, 0], xrecv_sem.at[m, 0], 0),
            remote(rights[m], far_rights[m], xsend_sem.at[m, 1], xrecv_sem.at[m, 1], 0),
        ]
    arrived = set()

    def meet(m):
        if m not in arrived:
            arrived.add(m)
            for copy in crossing[m]:
                copy.wait_recv()

    def left_copies(m):
        meet(m)
        rows = matrices[m].left_rows(2 ** len(dims))
        return [
            pltpu.make_async_copy(
                (lefts[m].at[0], far_lefts[m])[k],
                left_buffer.at[m % 2, pl.ds(0, rows), pl.ds(k * LANES, LANES)],
                left_sem.at[m % 2, k],
            )
            for k in range(2)
        ]

    all_pieces = [(m, p) for m, matrix in enumerate(matrices) for p in range(len(matrix.pieces))]

    def right_copies(index):
        m, p = all_pieces[index]
        meet(m)
        start, width = matrices[m].pieces[p]
        return [
            pltpu.make_async_copy(
                (rights[m], far_rights[m])[k].at[:, pl.ds(start, width)],
                right_buffer.at[index % 2, pl.ds(k * LANES, LANES), pl.ds(0, width)],
                right_sem.at[index % 2, k],
            )
            for k in range(2)
        ]

    def start(copies):
        for copy in copies:
            copy.start()

    def wait(copies):
        for copy in copies:
            copy.wait()

    start(left_copies(0))
    for index in range(2):
        start(right_copies(index))
    start(left_copies(1))

    def send(u, h):
        unit = units[u]
        index = []
        for name in dims:
            if name in unit.hops[:h]:
                index.append(bit(name))
            elif name == unit.hops[h]:
                index.append(1 - bit(name))
            else:
                index.append(slice(None))
        return remote(
            grads[u].at[tuple(index)],
            landed[u][h],
            send_sem.at[u, h],
            recv_sem.at[u, h],
            unit.hops[h],
        )

    flying = {}

    def add(u, h):
        unit = units[u]
        flying[u, h].wait_recv()
        done = unit.hops[: h + 1]
        free = [name for name in dims if name not in done]
        step = 16
        last = h + 1 == hops

        @pl.loop(0, 2 ** len(free) * (unit.rows // step))
        def _(i):
            block, row = lax.div(i, unit.rows // step), lax.rem(i, unit.rows // step) * step
            place = {
                name: lax.rem(lax.div(block, 1 << (len(free) - 1 - k)), 2)
                for k, name in enumerate(free)
            }
            rows = pl.ds(pl.multiple_of(row, step), step)
            own = tuple(place.get(name, bit(name)) for name in dims) + (rows,)
            got = tuple(place[name] for name in free) + (rows,)
            total = grads[u][own].astype(jnp.float32) + landed[u][h][got].astype(jnp.float32)
            if last:
                outs[u][rows] = total
            else:
                grads[u][own] = total.astype(jnp.bfloat16)

    def multiply(index):
        m, p = all_pieces[index]
        matrix = matrices[m]
        start_column, width = matrix.pieces[p]
        blocks = 2 ** len(dims)
        if p == 0:
            wait(left_copies(m))
        wait(right_copies(index))
        left, right = left_buffer.at[m % 2], right_buffer.at[index % 2]
        u = next(
            i
            for i, unit in enumerate(units)
            if unit.matrix == m
            and not unit.folded
            and unit.start <= start_column < unit.start + unit.columns
        )
        group = blocks
        while group * matrix.main > 640:
            group //= 2
        free = group.bit_length() - 1
        step = next(s for s in (384, 640, 512, 128) if width % s == 0)

        @pl.loop(0, (blocks // group) * (width // step))
        def _(i):
            g, j = lax.div(i, width // step), lax.rem(i, width // step)
            rows = pl.ds(pl.multiple_of(g * (group * matrix.main), 16), group * matrix.main)
            columns = pl.ds(pl.multiple_of(j * step, 128), step)
            result = jnp.dot(left[rows, :], right[:, columns], preferred_element_type=jnp.float32)
            high = len(dims) - free
            where = tuple(lax.rem(lax.div(g, 1 << (high - 1 - k)), 2) for k in range(high))
            target = pl.ds(pl.multiple_of(start_column - units[u].start + j * step, 128), step)
            grads[u][where + (slice(None),) * (free + 1) + (target,)] = result.astype(
                jnp.bfloat16
            ).reshape((2,) * free + (matrix.main, step))

        if matrix.rest:
            offset = blocks * (matrix.main + 16 * p)

            @pl.loop(0, width // step)
            def _(j):
                columns = pl.ds(pl.multiple_of(j * step, 128), step)
                result = jnp.dot(
                    left[pl.ds(offset, blocks * 16), :],
                    right[:, columns],
                    preferred_element_type=jnp.float32,
                )
                if p == 0:
                    fold_sum[:, columns] = result
                else:
                    fold_sum[:, columns] += result

        if index + 2 < len(all_pieces):
            start(right_copies(index + 2))
        last = p + 1 == len(matrix.pieces)
        if last and m + 2 < count:
            start(left_copies(m + 2))
        if last and matrix.rest:
            f = next(i for i, unit in enumerate(units) if unit.matrix == m and unit.folded)
            folded = fold_sum[:, pl.ds(0, units[f].columns)].astype(jnp.bfloat16)
            grads[f][...] = folded.reshape((2,) * len(dims) + (16, units[f].columns))

    shipped = {}

    def ship(k):
        return remote(ships[k], docks[k], ship_send.at[k], ship_recv.at[k], "seq")

    path = [0] + list(dims)
    vector_flying = {}

    def vector_send(h):
        source = vector_ref if h == 0 else vector_sum.at[h - 1]
        return remote(source, vector_land.at[h], vsend_sem.at[h], vrecv_sem.at[h], path[h])

    def vector_add(h):
        vector_flying[h].wait_recv()
        before = vector_ref[...] if h == 0 else vector_sum[h - 1]
        total = before + vector_land[h]
        if h < hops:
            vector_sum[h] = total
            vector_flying[h + 1] = vector_send(h + 1)
        else:
            vector_out[...] = total

    vector_flying[0] = vector_send(0)
    vector_done, since = 0, 0
    for action, u, h in events:
        if action == COMPUTE:
            multiply(u)
        elif action == SEND and u == SHIP:
            shipped[h] = ship(h)
        elif action == SEND:
            flying[u, h] = send(u, h)
        elif u == SHIP:
            shipped[h].wait_recv()
        else:
            add(u, h)
            since += 1
            if since % 4 == 0 and vector_done <= hops:
                vector_add(vector_done)
                vector_done += 1
    while vector_done <= hops:
        vector_add(vector_done)
        vector_done += 1
    for copy in sent:
        copy.wait_send()


X, Y, Z, ZZ = "seq", 1, 2, 3
XYZ, YXZ, YZX = (X, Y, Z, ZZ), (Y, X, Z, ZZ), (Y, Z, ZZ, X)
ZXY, ZYX, XZY = (Z, ZZ, X, Y), (Z, ZZ, Y, X), (X, Z, ZZ, Y)
COMPUTE, SEND, TAKE, SHIP = 0, 1, 2, -1
HOP_PLAN = [YXZ, ZYX, YXZ, XYZ, XYZ, ZXY, YXZ, ZXY, YZX, XZY, YXZ, YXZ, XZY, XYZ, YXZ, XZY, XYZ]
EVENTS = [
    (SEND, SHIP, 0), (SEND, SHIP, 1), (COMPUTE, 0, 0), (SEND, 0, 0), (COMPUTE, 1, 0),
    (SEND, 1, 0), (COMPUTE, 2, 0), (SEND, 2, 0), (COMPUTE, 3, 0), (TAKE, SHIP, 0), (SEND, 3, 0),
    (COMPUTE, 4, 0), (COMPUTE, 5, 0), (SEND, 5, 0), (TAKE, SHIP, 1), (SEND, 4, 0),
    (COMPUTE, 6, 0), (COMPUTE, 7, 0), (COMPUTE, 8, 0), (SEND, 6, 0), (TAKE, 0, 0),
    (COMPUTE, 9, 0), (SEND, 7, 0), (TAKE, 1, 0), (SEND, 1, 1), (COMPUTE, 10, 0), (SEND, 0, 1),
    (TAKE, 3, 0), (COMPUTE, 11, 0), (COMPUTE, 12, 0), (COMPUTE, 13, 0), (TAKE, 5, 0),
    (SEND, 5, 1), (COMPUTE, 14, 0), (SEND, 14, 0), (TAKE, 2, 0), (SEND, 12, 0), (TAKE, 4, 0),
    (TAKE, 7, 0), (SEND, 7, 1), (TAKE, 1, 1), (SEND, 15, 0), (TAKE, 0, 1), (SEND, 0, 2),
    (SEND, 8, 0), (TAKE, 6, 0), (TAKE, 5, 1), (SEND, 2, 1), (TAKE, 12, 0), (SEND, 12, 1),
    (TAKE, 7, 1), (SEND, 10, 0), (TAKE, 14, 0), (TAKE, 0, 2), (SEND, 0, 3), (SEND, 14, 1),
    (TAKE, 15, 0), (SEND, 15, 1), (TAKE, 12, 1), (SEND, 12, 2), (TAKE, 0, 3), (SEND, 11, 0),
    (TAKE, 8, 0), (SEND, 8, 1), (TAKE, 15, 1), (SEND, 15, 2), (SEND, 13, 0), (TAKE, 2, 1),
    (SEND, 2, 2), (TAKE, 12, 2), (SEND, 6, 1), (TAKE, 14, 1), (TAKE, 15, 2), (SEND, 14, 2),
    (TAKE, 8, 1), (SEND, 8, 2), (SEND, 3, 1), (TAKE, 10, 0), (SEND, 10, 1), (TAKE, 13, 0),
    (TAKE, 2, 2), (SEND, 2, 3), (TAKE, 8, 2), (TAKE, 14, 2), (SEND, 14, 3), (SEND, 16, 0),
    (TAKE, 6, 1), (SEND, 6, 2), (SEND, 4, 1), (TAKE, 11, 0), (TAKE, 2, 3), (SEND, 11, 1),
    (TAKE, 10, 1), (SEND, 10, 2), (TAKE, 14, 3), (SEND, 1, 2), (TAKE, 3, 1), (SEND, 3, 2),
    (SEND, 5, 2), (TAKE, 16, 0), (TAKE, 6, 2), (SEND, 6, 3), (TAKE, 10, 2), (SEND, 10, 3),
    (SEND, 13, 1), (TAKE, 4, 1), (SEND, 4, 2), (SEND, 9, 0), (SEND, 7, 2), (SEND, 8, 3),
    (TAKE, 11, 1), (SEND, 11, 2), (TAKE, 6, 3), (TAKE, 3, 2), (SEND, 3, 3), (SEND, 16, 1),
    (SEND, 12, 3), (SEND, 15, 3), (TAKE, 1, 2), (SEND, 1, 3), (TAKE, 5, 2), (TAKE, 10, 3),
    (SEND, SHIP, 2), (TAKE, 9, 0), (SEND, 9, 1), (SEND, 5, 3), (TAKE, 13, 1), (SEND, 13, 2),
    (TAKE, 4, 2), (SEND, 4, 3), (TAKE, 3, 3), (TAKE, 7, 2), (SEND, 7, 3), (TAKE, 16, 1),
    (SEND, 16, 2), (TAKE, 8, 3), (TAKE, 12, 3), (TAKE, 11, 2), (SEND, 11, 3), (TAKE, 15, 3),
    (TAKE, 1, 3), (TAKE, 5, 3), (TAKE, 9, 1), (SEND, 9, 2), (TAKE, 4, 3), (TAKE, 7, 3),
    (TAKE, 13, 2), (SEND, 13, 3), (TAKE, 11, 3), (TAKE, 16, 2), (SEND, 16, 3), (TAKE, 9, 2),
    (SEND, 9, 3), (TAKE, 13, 3), (TAKE, SHIP, 2), (TAKE, 9, 3), (TAKE, 16, 3),
]


def weight_gradients(lefts, rights, vectors, ships, plan, bits):
    matrices, units, events = plan
    blocks = 2**bits
    dims = list(reversed(range(1, bits))) + ["seq"]
    operands = [*lefts, *rights, vectors, *ships]
    anywhere = pl.BlockSpec(memory_space=pl.ANY)
    vmem = pl.BlockSpec(memory_space=pltpu.VMEM)
    hops, count = len(dims), len(matrices)
    shape = jax.ShapeDtypeStruct
    outs = [shape((unit.rows, unit.columns), jnp.float32) for unit in units]
    outs += [shape(ship.shape, ship.dtype) for ship in ships]
    outs += [shape(left.shape[1:], left.dtype) for left in lefts]
    outs += [shape(right.shape, right.dtype) for right in rights]
    outs.append(shape(vectors.shape, jnp.float32))
    low = jnp.bfloat16
    scratch = [pltpu.VMEM((2,) * hops + (unit.rows, unit.columns), low) for unit in units]
    for unit in units:
        for h in range(hops):
            scratch.append(pltpu.VMEM((2,) * (hops - 1 - h) + (unit.rows, unit.columns), low))
    scratch.append(pltpu.VMEM((hops + 1,) + vectors.shape, jnp.float32))
    scratch.append(pltpu.VMEM((hops,) + vectors.shape, jnp.float32))
    folded = [matrix.fold_width for matrix in matrices if matrix.rest]
    scratch.append(pltpu.VMEM((blocks * 16, max(folded)), jnp.float32))
    scratch.append(pltpu.VMEM((2, max(m.left_rows(blocks) for m in matrices), TWO), low))
    scratch.append(pltpu.VMEM((2, TWO, max(max(w for _, w in m.pieces) for m in matrices)), low))
    scratch += [pltpu.SemaphoreType.DMA((len(units), hops))] * 2
    scratch += [pltpu.SemaphoreType.DMA((hops + 1,))] * 2
    scratch += [pltpu.SemaphoreType.DMA((2, 2))] * 2
    scratch += [pltpu.SemaphoreType.DMA((count, 2))] * 2
    scratch += [pltpu.SemaphoreType.DMA((SHIPS,))] * 2
    results = pl.pallas_call(
        functools.partial(reduce_kernel, matrices, units, events, dims),
        out_shape=outs,
        in_specs=[anywhere] * (2 * count) + [vmem] + [anywhere] * SHIPS,
        out_specs=[vmem] * len(units) + [anywhere] * (SHIPS + 2 * count) + [vmem],
        scratch_shapes=scratch,
        compiler_params=pltpu.CompilerParams(
            collective_id=0, has_side_effects=True, vmem_limit_bytes=62 * 2**20
        ),
        name="reduce_weights",
    )(*operands)
    wholes = []
    for m, matrix in enumerate(matrices):
        mains = [r for r, u in zip(results, units) if u.matrix == m and not u.folded]
        whole = jnp.concatenate(mains, axis=1) if len(mains) > 1 else mains[0]
        if matrix.rest:
            fold = next(r for r, u in zip(results, units) if u.matrix == m and u.folded)
            parts = [
                fold[p * matrix.rest : (p + 1) * matrix.rest, :width]
                for p, (_, width) in enumerate(matrix.pieces)
            ]
            whole = jnp.concatenate([whole, jnp.concatenate(parts, axis=1)], axis=0)
        wholes.append(whole)
    return wholes, results[-1], results[len(units) : len(units) + SHIPS]


def even_cuts(columns, width):
    return [(start, width) for start in range(0, columns, width)]


def make_plan(width, hidden, chunks):
    matrices = [
        Matrix(hidden // chunks, width, [384] * 3, even_cuts(width, 384)),
        Matrix(width // chunks, hidden, [1152] * 4, even_cuts(hidden, 1152)),
        Matrix(width // chunks, width, [384] * 3, [(0, width)]),
        Matrix(width // chunks, 3 * width, [1152] * 3, even_cuts(3 * width, 1152)),
        Matrix(2 * width // chunks, width, [640, 512], [(0, 640), (640, 512)]),
    ]
    units = make_units(matrices, HOP_PLAN)
    return matrices, units, EVENTS


def halving(block, order, bits):
    dp_index = lax.axis_index("dp")
    seq_index = lax.axis_index("seq")
    dims = list(reversed(range(1, bits))) + ["seq"]
    for name in order:
        axis = dims.index(name)
        own = seq_index if name == "seq" else (dp_index >> name) & 1
        sent = pick(block, 1 - own, axis)
        kept = pick(block, own, axis)
        got = swap_seq(sent) if name == "seq" else swap_dp(sent, name)
        total = kept.astype(jnp.float32) + got.astype(jnp.float32)
        dims.pop(axis)
        block = total.astype(jnp.bfloat16) if dims else total
    return block


def local_permutes(
    inputs,
    skipped,
    lengths,
    cotangent,
    skip_weight,
    skip_bias,
    gain_one,
    shift_one,
    qkv_weight,
    proj_weight,
    proj_bias,
    gain_two,
    shift_two,
    fc1_weight,
    fc1_bias,
    fc2_weight,
    fc2_bias,
):
    items, half, width = inputs.shape
    seq_count = lax.axis_size("seq")
    dp_count = lax.axis_size("dp")
    bits = dp_count.bit_length() - 1
    seq_index = lax.axis_index("seq")
    core = lax.axis_index("dp") & 1
    first = seq_index == 0
    slots = half * seq_count

    def whole_item(values, axis):
        own = pick(values, seq_index, 0)
        got = swap_seq(pick(values, 1 - seq_index, 0))
        return place(first, own, got, axis)

    def to_owner(values, axis):
        parts = jnp.split(values, 2, axis=axis)
        own = jnp.where(first, parts[0], parts[1])
        other = jnp.where(first, parts[1], parts[0])
        got = swap_seq(other.astype(jnp.bfloat16)).astype(values.dtype)
        return place(first, own[None], got[None], 0)

    own_inputs = whole_item(inputs, 0)
    own_skip = whole_item(skipped, 1)
    grad_out = whole_item(cotangent, 0)
    length = pick(lengths, seq_index, 0)
    rows = slots

    joined = jnp.concatenate([own_inputs, own_skip], axis=-1)
    stream = matmul(joined, skip_weight) + skip_bias
    normed = layer_norm(stream, gain_one, shift_one).astype(jnp.bfloat16)
    packed = matmul(normed, qkv_weight).astype(jnp.bfloat16)
    heads = packed.reshape(rows, 3, HEADS, HEAD_DIM)
    query, keys, values = heads[:, 0], heads[:, 1], heads[:, 2]
    scale = HEAD_DIM ** (-0.5)
    positions = jnp.arange(slots, dtype=jnp.int32)
    caption = (positions >= 1) & (positions <= length)
    image = (positions >= 1 + CAPTION) & (positions < 1 + CAPTION + IMAGE)
    valid = (positions == 0) | caption | image

    def product(spec, left, right):
        return jnp.einsum(spec, left, right, preferred_element_type=jnp.float32)

    scores = product("qhd,khd->hqk", query, keys) * scale
    scores = jnp.where(valid[None, None, :], scores, masked_score)
    top = jnp.max(scores, axis=-1, keepdims=True)
    expo = jnp.exp(scores - top)
    probs = expo / jnp.sum(expo, axis=-1, keepdims=True)
    probs_low = probs.astype(jnp.bfloat16)
    mixed = product("hqk,khd->qhd", probs_low, values)
    mixed = mixed.astype(jnp.bfloat16).reshape(rows, width)
    attended = matmul(mixed, proj_weight) + proj_bias
    stream_two = stream + attended
    normed_two = layer_norm(stream_two, gain_two, shift_two).astype(jnp.bfloat16)
    hidden = matmul(normed_two, fc1_weight) + fc1_bias
    acted, gelu_back = jax.vjp(gelu_exact, hidden)
    acted_low = acted.astype(jnp.bfloat16)
    block_output = (stream_two + (matmul(acted_low, fc2_weight) + fc2_bias)).astype(jnp.bfloat16)

    blocks = dp_count // 2

    def own_rows(left, right):
        parts = left.reshape(rows, blocks, 2, -1)
        kept = pick(parts, core, 2).reshape(rows, -1)
        sent = pick(parts, 1 - core, 2).reshape(rows, -1)
        left_both = jnp.concatenate([kept, swap_dp(sent, 0)], axis=0)
        right_both = jnp.concatenate([right, swap_dp(right, 0)], axis=0)
        total = matmul(left_both.T, right_both).astype(jnp.bfloat16)
        share = total.shape[0] // (blocks * 2)
        return total.reshape((2,) * bits + (share, right.shape[1]))

    above = list(range(1, bits))
    order_x = ["seq"] + above
    order_y = above + ["seq"]
    order_z = above[1:] + ["seq"] + above[:1]

    grad_fc2 = halving(own_rows(acted_low, grad_out), order_x, bits)
    grad_fc2_bias = column_sum(grad_out)
    grad_acted = matmul(grad_out, fc2_weight.T)
    grad_hidden = gelu_back(grad_acted)[0].astype(jnp.bfloat16)
    grad_fc1 = halving(own_rows(normed_two, grad_hidden), order_x, bits)
    grad_fc1_bias = column_sum(grad_hidden)
    grad_normed_two = matmul(grad_hidden, fc1_weight.T)
    _, norm_back_two = jax.vjp(layer_norm, stream_two, gain_two, shift_two)
    back_two, grad_gain_two, grad_shift_two = norm_back_two(grad_normed_two)
    grad_stream_two = grad_out.astype(jnp.float32) + back_two
    grad_attended = grad_stream_two.astype(jnp.bfloat16)
    grad_proj = halving(own_rows(mixed, grad_attended), order_y, bits)
    grad_proj_bias = column_sum(grad_attended)
    grad_mixed = matmul(grad_attended, proj_weight.T)
    grad_mixed = grad_mixed.astype(jnp.bfloat16).reshape(rows, HEADS, HEAD_DIM)
    grad_probs = product("qhd,khd->hqk", grad_mixed, values)
    grad_scores = probs * (grad_probs - jnp.sum(probs * grad_probs, axis=-1, keepdims=True))
    grad_scores = grad_scores.astype(jnp.bfloat16)
    grad_values = product("hqk,qhd->khd", probs_low, grad_mixed)
    grad_query = product("hqk,khd->qhd", grad_scores, keys) * scale
    grad_keys = product("hqk,qhd->khd", grad_scores, query) * scale
    grad_packed = jnp.stack([grad_query, grad_keys, grad_values], axis=1)
    grad_packed = grad_packed.astype(jnp.bfloat16).reshape(rows, 3 * width)
    grad_qkv = halving(own_rows(normed, grad_packed), order_y, bits)
    grad_normed = matmul(grad_packed, qkv_weight.T)
    _, norm_back_one = jax.vjp(layer_norm, stream, gain_one, shift_one)
    back_one, grad_gain_one, grad_shift_one = norm_back_one(grad_normed)
    grad_stream = (grad_stream_two + back_one).astype(jnp.bfloat16)
    grad_skip = halving(own_rows(joined, grad_stream), order_z, bits)
    grad_skip_bias = column_sum(grad_stream)
    grad_joined = matmul(grad_stream, skip_weight.T)

    vectors = (
        grad_skip_bias,
        grad_gain_one,
        grad_shift_one,
        grad_proj_bias,
        grad_gain_two,
        grad_shift_two,
        grad_fc1_bias,
        grad_fc2_bias,
    )
    chunks = dp_count * seq_count
    line = jnp.concatenate([v.reshape(chunks, -1) for v in vectors], axis=1)
    line = lax.psum_scatter(line, ("dp", "seq"), scatter_dimension=0, tiled=True)[0]
    pieces, start = [], 0
    for vector in vectors:
        size = vector.shape[0] // chunks
        pieces.append(line[start : start + size])
        start += size

    return (
        to_owner(block_output, 0),
        to_owner(grad_joined[:, :width], 0),
        to_owner(grad_joined[:, width:], 1),
        grad_skip,
        pieces[0],
        pieces[1],
        pieces[2],
        grad_qkv,
        grad_proj,
        pieces[3],
        pieces[4],
        pieces[5],
        grad_fc1,
        pieces[6],
        grad_fc2,
        pieces[7],
    )


def local_kernels(*arguments):
    arrays = Arguments(*arguments)
    items, half, width = arrays.inputs.shape
    hidden = arrays.fc1_weight.shape[1]
    dp_count = lax.axis_size("dp")
    bits = dp_count.bit_length() - 1
    seq_index = lax.axis_index("seq")
    device = lax.axis_index("dp") * 2 + seq_index
    first = seq_index == 0
    chunks = dp_count * 2
    skipped = arrays.skipped.reshape(items, 2, half, width // 2)
    plan = make_plan(width, hidden, chunks)
    feed = dict(
        inputs=arrays.inputs,
        skipped=skipped,
        cotangent=arrays.cotangent,
        lengths=arrays.lengths,
    )
    for name in Arguments._fields[4:]:
        feed[name] = getattr(arrays, name)
    found = run_block(feed, plan[0], width, hidden, half)
    weights, vectors, got = weight_gradients(
        [getattr(found, name) for name in LEFTS],
        [getattr(found, name) for name in RIGHTS],
        found.vectors,
        [found.block_send, found.grad_in_send, found.grad_skip_send],
        plan,
        bits,
    )
    block_got, grad_in_got, grad_skip_got = got

    def owner(own, other):
        other = other.astype(own.dtype)
        return jnp.where(first, jnp.stack([own, other]), jnp.stack([other, own]))

    share = width // chunks
    mine = lax.dynamic_slice(vectors, (0, device * share), (8, share))
    wide_share = hidden // chunks
    per_row = width // wide_share
    row = 8 + device // per_row
    bias = lax.dynamic_slice(vectors, (row, device % per_row * wide_share), (1, wide_share))[0]
    grad_fc2, grad_fc1, grad_proj, grad_qkv, grad_skip = weights
    grad_skip_own = found.grad_skip_own.reshape(2 * half, -1)
    return (
        owner(found.block_own, block_got),
        owner(found.grad_in_own, grad_in_got),
        owner(grad_skip_own, grad_skip_got.reshape(2 * half, -1)),
        grad_skip,
        mine[0],
        mine[1],
        mine[2],
        grad_qkv,
        grad_proj,
        mine[3],
        mine[4],
        mine[5],
        grad_fc1,
        bias,
        grad_fc2,
        mine[7],
    )


class Arguments(typing.NamedTuple):
    inputs: jax.Array
    skipped: jax.Array
    lengths: jax.Array
    cotangent: jax.Array
    skip_weight: jax.Array
    skip_bias: jax.Array
    gain_one: jax.Array
    shift_one: jax.Array
    qkv_weight: jax.Array
    proj_weight: jax.Array
    proj_bias: jax.Array
    gain_two: jax.Array
    shift_two: jax.Array
    fc1_weight: jax.Array
    fc1_bias: jax.Array
    fc2_weight: jax.Array
    fc2_bias: jax.Array


def solution(mesh):
    small = mesh.shape["dp"] == 16
    return jax.shard_map(
        local_kernels if small else local_permutes,
        mesh=mesh,
        in_specs=(
            P("dp", "seq", None),
            P("dp", None, "seq"),
            P("dp"),
            P("dp", "seq", None),
        )
        + (P(),) * 13,
        out_specs=(
            P("dp", "seq", None),
            P("dp", "seq", None),
            P("dp", None, "seq"),
            P(("dp", "seq"), None),
            P(("dp", "seq")),
            P(("dp", "seq")),
            P(("dp", "seq")),
            P(("dp", "seq"), None),
            P(("dp", "seq"), None),
            P(("dp", "seq")),
            P(("dp", "seq")),
            P(("dp", "seq")),
            P(("dp", "seq"), None),
            P(("dp", "seq")),
            P(("dp", "seq"), None),
            P(("dp", "seq")),
        ),
        check_vma=False,
    )
```

```python
import functools
import types
import typing

import jax
import jax.numpy as jnp
from jax import lax
from jax.experimental import pallas as pl
from jax.experimental.pallas import tpu as pltpu
from jax.sharding import PartitionSpec as P

HEADS = 16
HEAD_DIM = 72
CAPTION = 77
IMAGE = 256


epsilon = 1e-05
masked_score = -1e30


def layer_norm(stream, gain, shift):
    center = stream - jnp.mean(stream, axis=-1, keepdims=True)
    spread = jnp.mean(center * center, axis=-1, keepdims=True)
    return center * lax.rsqrt(spread + epsilon) * gain + shift


def gelu_exact(values):
    return jax.nn.gelu(values, approximate=False)


def column_sum(values):
    return jnp.sum(values.astype(jnp.float32), axis=0)


def matmul(left, right):
    return jnp.dot(left, right, preferred_element_type=jnp.float32)


def swap_seq(values):
    return lax.ppermute(values, "seq", [(0, 1), (1, 0)])


def swap_dp(values, bit):
    count = lax.axis_size("dp")
    return lax.ppermute(values, "dp", [(i, i ^ (1 << bit)) for i in range(count)])


def pick(values, index, axis):
    return lax.dynamic_index_in_dim(values, index, axis, keepdims=False)


def place(first, own, got, axis):
    return jnp.where(
        first, jnp.concatenate([own, got], axis=axis), jnp.concatenate([got, own], axis=axis)
    )


PAD = 192
ROWS = 2 * PAD


def matmul_t(left, right):
    return lax.dot_general(
        left, right, (((1,), (1,)), ((), ())), preferred_element_type=jnp.float32
    )


def t_matmul(left, right):
    return lax.dot_general(
        left, right, (((0,), (0,)), ((), ())), preferred_element_type=jnp.float32
    )


def tiles_of(width):
    starts = list(range(0, width - 255, 512))
    ends = starts[1:] + [width]
    return [pl.ds(a, b - a) for a, b in zip(starts, ends)]


def norm_parts(values):
    center = values - jnp.mean(values, axis=-1, keepdims=True)
    spread = jnp.mean(center * center, axis=-1, keepdims=True)
    scale = lax.rsqrt(spread + epsilon)
    return center * scale, scale


def fold_rows(values):
    rows, width = values.shape
    return jnp.sum(values.reshape(rows // 8, 8, width), axis=0)


def block_kernel(half, hidden, matrices, early, names, *refs):
    r = types.SimpleNamespace(**dict(zip(names, refs)))
    width = r.skip_weight.shape[1]
    seq = lax.axis_index("seq")
    core = lax.rem(lax.axis_index("dp"), 2)
    sems = r.sems
    low = jnp.bfloat16
    counter = iter(range(80))

    def copy(source, target):
        return pltpu.make_async_copy(source, target, sems.at[next(counter)])

    loads = types.SimpleNamespace(
        in0=copy(r.inputs.at[seq], r.raw_in.at[seq]),
        sk0=copy(r.skipped.at[seq], r.raw_skip.at[seq]),
        skip0=copy(r.skip_weight.at[pl.ds(0, width), :], r.feed.at[0]),
        skip1=copy(r.skip_weight.at[pl.ds(width, width), :], r.feed.at[1]),
        ct0=copy(r.cotangent.at[seq], r.raw_out.at[seq]),
        proj=copy(r.proj_weight, r.proj_buffer),
    )
    spare = r.spare

    def load_qkv():
        parts = [
            copy(r.qkv_weight.at[:, pl.ds(k * width, width)], spare.at[k]) for k in range(3)
        ]
        for load in parts:
            load.start()
        return parts

    dp = lax.axis_index("dp")
    neighbour = (dp, 1 - seq)

    def flip(name):
        if name == "seq":
            return neighbour
        return (dp + (1 - 2 * lax.rem(lax.div(dp, 1 << name), 2)) * (1 << name), seq)

    barrier = pltpu.get_barrier_semaphore()
    names_met = [0] + sorted({hop for _, hop in early}, key=str)
    for name in names_met:
        pl.semaphore_signal(barrier, inc=1, device_id=flip(name), device_id_type=MESH)
    for load in vars(loads).values():
        load.start()
    qkv_loads = load_qkv()
    pl.semaphore_wait(barrier, len(names_met))
    remotes = []

    def remote(source, target, name):
        k = len(remotes)
        item = pltpu.make_async_remote_copy(
            src_ref=source,
            dst_ref=target,
            send_sem=r.send_sem.at[k],
            recv_sem=r.recv_sem.at[k],
            device_id=flip(name),
            device_id_type=MESH,
        )
        item.start()
        remotes.append(item)
        return item

    gone, come = set(), set()

    def left_here(item):
        if id(item) not in gone:
            gone.add(id(item))
            item.wait_send()

    def got_here(item):
        if id(item) not in come:
            come.add(id(item))
            item.wait_recv()

    traded = [
        remote(r.inputs.at[1 - seq], r.raw_in.at[seq], "seq"),
        remote(r.skipped.at[1 - seq], r.raw_skip.at[seq], "seq"),
    ]
    chunk, feed = width, r.feed
    feeds = []
    for j in range(hidden // chunk):
        part = pl.ds(j * chunk, chunk)
        at = 2 - 2 * (j % 2)
        feeds.append(
            (
                copy(r.fc1_weight.at[:, part], feed.at[at]),
                copy(r.fc2_weight.at[part, :], feed.at[at + 1]),
            )
        )

    def start(copies):
        for item in copies:
            item.start()

    start(feeds[0])
    stores = {}

    def store(source, target):
        item = copy(source, target)
        item.start()
        stores[id(item)] = item
        return item

    def finish(item):
        stores.pop(id(item)).wait()

    joined, skips, grad_out = r.joined, r.skips, r.grad_out
    gap = PAD - half
    for load in (loads.in0, loads.sk0):
        load.wait()
    for item in traded:
        got_here(item)
    traded = remote(r.cotangent.at[1 - seq], r.raw_out.at[seq], "seq")
    for h in range(2):
        joined[pl.ds(h * PAD, PAD), :] = jnp.concatenate(
            [r.raw_in[h], jnp.zeros((gap, width), low)], axis=0
        )
        for f in range(2):
            skips[f, pl.ds(h * PAD, PAD), :] = jnp.concatenate(
                [r.raw_skip[f, h], jnp.zeros((gap, width // 2), low)], axis=0
            )
    loads.skip0.wait()
    loads.skip1.wait()
    stream = r.stream
    tiles = tiles_of(width)

    for columns in tiles:
        total = matmul(joined[...], feed[0, :, columns])
        total += matmul(skips[0], feed[1, pl.ds(0, width // 2), columns])
        total += matmul(skips[1], feed[1, pl.ds(width // 2, width // 2), columns])
        stream[:, columns] = total + r.skip_bias[columns]

    start(feeds[1])
    step = 128

    def norm(source, gain, shift, target):
        @pl.loop(0, ROWS // step)
        def _(i):
            rows = pl.ds(pl.multiple_of(i * step, step), step)
            unit, _ = norm_parts(source[rows, :])
            target[rows, :] = (unit * gain[...] + shift[...]).astype(low)

    normed, packed = r.normed, r.packed
    norm(stream, r.gain_one, r.shift_one, normed)
    for load in qkv_loads:
        load.wait()

    for k in range(3):
        for columns in tiles:
            target = pl.ds(k * width + columns.start, columns.size)
            packed[:, target] = matmul(normed[...], spare[k, :, columns]).astype(low)

    length = r.lengths[seq]
    at = lax.broadcasted_iota(jnp.int32, (1, ROWS), 1)
    inner = jnp.where(at >= PAD, at - PAD, at)
    position = jnp.where(at >= PAD, at - PAD + half, at)
    valid = (position == 0) | ((position >= 1) & (position <= length))
    valid = valid | ((position >= 1 + CAPTION) & (position < 1 + CAPTION + IMAGE))
    valid = valid & (inner < half)
    scale = HEAD_DIM ** (-0.5)
    window = 256

    def head_window(h):
        start = jnp.minimum(lax.div(h * HEAD_DIM, 128) * 128, width - window)
        start = pl.multiple_of(start, 128)
        lane = lax.broadcasted_iota(jnp.int32, (1, window), 1) + start
        mine = (lane >= h * HEAD_DIM) & (lane < (h + 1) * HEAD_DIM)
        return start, mine

    def part(which, start):
        return packed[:, pl.ds(pl.multiple_of(which * width + start, 128), window)]

    mixed_sum, probs = r.sum_a, r.probs

    def attend(h, carry):
        start, mine = head_window(h)
        query = jnp.where(mine, part(0, start), jnp.zeros((), low))
        scores = matmul_t(query, part(1, start)) * scale
        scores = jnp.where(valid, scores, masked_score)
        expo = jnp.exp(scores - jnp.max(scores, axis=-1, keepdims=True))
        share = expo * (1.0 / jnp.sum(expo, axis=-1, keepdims=True))
        share = share.astype(low)
        probs[h] = share
        found = matmul(share, part(2, start))
        columns = pl.ds(start, window)
        mixed_sum[:, columns] = jnp.where(mine, found, mixed_sum[:, columns])
        return carry

    lax.fori_loop(0, HEADS, attend, 0, unroll=4)
    mixed, stream_two = r.mixed, r.stream_two
    mixed[...] = mixed_sum[...].astype(low)
    loads.proj.wait()

    for columns in tiles:
        total = matmul(mixed[...], r.proj_buffer[:, columns]) + r.proj_bias[columns]
        stream_two[:, columns] = stream[:, columns] + total

    normed_two = r.normed_two
    norm(stream_two, r.gain_two, r.shift_two, normed_two)
    loads.ct0.wait()
    got_here(traded)
    for h in range(2):
        grad_out[pl.ds(h * PAD, PAD), :] = jnp.concatenate(
            [r.raw_out[h], jnp.zeros((gap, width), low)], axis=0
        )
    far_out = remote(grad_out, r.far_right_fc2, 0)
    sums = r.sums
    sums[7:8, :] = jnp.sum(grad_out[...].astype(jnp.float32), axis=0, keepdims=True)

    turned_ref = r.turned
    stages = {}

    def left(m, target, far, sources):
        matrix = matrices[m]
        stage = r.left_stage
        for item in stages.pop(0, ()):
            finish(item) if id(item) in stores else left_here(item)
        share, main, rest = matrix.share, matrix.main, matrix.rest
        folds, body = len(matrix.pieces), 16 * main
        first = 0
        for source in sources:
            turned_ref[pl.ds(32, width), :] = source.astype(jnp.float32).T
            for k in range(width // share):
                number = first + k
                c, block = number // 2 % 2, number // 4 * 2 + number % 2
                base = 32 + k * share
                place = c ^ core
                stage[place, pl.ds(block * main, main), :] = turned_ref[
                    pl.ds(base, main), :
                ].astype(low)
                row = lax.broadcasted_iota(jnp.int32, (16, 1), 0)
                for q in range(folds):
                    part = turned_ref[pl.ds(base + main - q * rest, 16), :]
                    part = jnp.where((row >= q * rest) & (row < (q + 1) * rest), part, 0.0)
                    stage[place, pl.ds(body + (q * 16 + block) * 16, 16), :] = part.astype(low)
            first += width // share
        rows = matrix.left_rows(16)
        stages[0] = [
            store(stage.at[0, pl.ds(0, rows), :], target),
            remote(stage.at[1, pl.ds(0, rows), :], far, 0),
        ]

    body = 16 * matrices[1].main
    left(1, r.left_fc1, r.far_left_fc1, [normed_two[...]])
    far_left = remotes[-1]
    near = copy(r.left_stage.at[0, pl.ds(0, body), :], spare.at[0, pl.ds(0, body), pl.ds(2 * ROWS, ROWS)])
    near.start()
    stores[id(near)] = near
    far_hidden = []
    opened, loading = [], []

    def fetch(source, target):
        item = copy(source, target)
        item.start()
        return item

    def launch():
        while opened:
            u, hop, item = opened.pop(0)
            finish(item)
            dims = [3, 2, 1, "seq"]
            bit = seq if hop == "seq" else lax.rem(lax.div(dp, 1 << hop), 2)
            index = tuple(1 - bit if name == hop else slice(None) for name in dims)
            remote(getattr(r, f"grad_{u}").at[index], getattr(r, f"far_grad_{u}"), hop)

    fetched = {}

    def prefetch(p):
        got_here(far_hidden[p])
        source = r.far_right_fc1.at[:, pl.ds(p * chunk, chunk)]
        fetched[p] = [fetch(source, spare.at[2, pl.ds(ROWS, ROWS), :])]
        if p == 0:
            got_here(far_left)
            target = spare.at[0, pl.ds(body, body), pl.ds(2 * ROWS, ROWS)]
            fetched[p].append(fetch(r.far_left_fc1.at[pl.ds(0, body), :], target))
            got_here(far_out)
            loading.append(fetch(r.far_right_fc2, spare.at[2, pl.ds(0, ROWS), :]))
        prefetch_left(p)

    def prefetch_left(p):
        got_here(far_acted[p])
        count = 4 * matrices[0].share
        source = r.far_left_fc2.at[pl.ds(p * count, count), :]
        target = spare.at[1, pl.ds(p % 2 * count, count), pl.ds(p // 2 * ROWS, ROWS)]
        loading.append(fetch(source, target))

    def early_hidden(p):
        for item in fetched.pop(p):
            item.wait()
        if p == 0:
            finish(near)
        launch()
        near_rows, far_rows = (spare[0, pl.ds(k * body, body), pl.ds(2 * ROWS, ROWS)] for k in range(2))
        for columns in tiles:
            value = matmul(near_rows, grad_hidden[p % 2, :, columns])
            value += matmul(far_rows, spare[2, pl.ds(ROWS, ROWS), columns])
            value = value.astype(low).reshape(2, 2, 2, 2, matrices[1].main, columns.size)
            r.wide_stage[:, :, :, :, :, columns] = value
        u, hop = early[3 + p]
        opened.append((u, hop, store(r.wide_stage, getattr(r, f"grad_{u}"))))

    forward, backward = r.sum_a, r.sum_b
    acted, grad_hidden, staged = r.acted, r.grad_hidden, r.left_fc2_stage
    pending, far_acted = {}, []
    for j, feeding in enumerate(feeds):
        slot = j % 2
        first, second = feed.at[2 - 2 * slot], feed.at[3 - 2 * slot]
        for load in feeding:
            load.wait()
        for item in pending.get(slot, ()):
            finish(item) if id(item) in stores else left_here(item)

        for columns in tiles:
            whole = pl.ds(j * chunk + columns.start, columns.size)
            value = matmul(normed_two[...], first[:, columns])
            value += r.fc1_bias[whole]
            phi = 0.5 + 0.5 * lax.erf(value * (0.5**0.5))
            bell = jnp.exp(-0.5 * value * value) * ((2 * jnp.pi) ** -0.5)
            acted[slot, :, columns] = (value * phi).astype(low)
            back = matmul_t(grad_out[...], second[columns, :])
            back = (back * (phi + value * bell)).astype(low)
            grad_hidden[slot, :, columns] = back
            sums[pl.ds(8 + j, 1), columns] = jnp.sum(
                back.astype(jnp.float32), axis=0, keepdims=True
            )

        if j >= 1:
            prefetch(j - 1)
        for columns in tiles:
            ahead = matmul(acted[slot], second[:, columns])
            back = matmul_t(grad_hidden[slot], first[columns, :])
            if j == 0:
                forward[:, columns] = ahead
                backward[:, columns] = back
            else:
                forward[:, columns] += ahead
                backward[:, columns] += back

        share = matrices[0].share
        turned = acted[slot].T
        groups = chunk // (4 * share)
        for g in range(groups):
            begin = g * 4 * share
            lower, upper = turned[begin : begin + 2 * share], turned[begin + 2 * share : begin + 4 * share]
            number = j * groups + g
            rows = pl.ds(number % 4 * 2 * share, 2 * share)
            spare[0, rows, pl.ds(number // 4 * ROWS, ROWS)] = jnp.where(core == 0, lower, upper)
            staged[slot, pl.ds(g * 2 * share, 2 * share), :] = jnp.where(core == 0, upper, lower)
        count = groups * 2 * share
        far_acted.append(remote(staged.at[slot], r.far_left_fc2.at[pl.ds(j * count, count), :], 0))
        part_columns = pl.ds(j * chunk, chunk)
        far_hidden.append(remote(grad_hidden.at[slot], r.far_right_fc1.at[:, part_columns], 0))
        pending[slot] = [
            far_acted[-1],
            far_hidden[-1],
            store(grad_hidden.at[slot], r.right_fc1.at[:, part_columns]),
        ]
        if j + 2 < len(feeds):
            start(feeds[j + 2])
        elif slot == 0:
            again = [copy(r.skip_weight.at[pl.ds(k * width, width), :], feed.at[2 + k]) for k in range(2)]
            start(again)
        if 1 <= j < 4:
            early_hidden(j - 1)

    left(2, r.left_proj, r.far_left_proj, [mixed[...]])
    launch()
    prefetch_left(3)
    left(3, r.left_qkv, r.far_left_qkv, [normed[...]])
    left(4, r.left_skip, r.far_left_skip, [joined[...], jnp.concatenate([skips[0], skips[1]], axis=1)])

    for item in loading:
        item.wait()
    share = matrices[0].share
    for p in range(3):
        start_column, size = matrices[0].pieces[p]
        columns = pl.ds(start_column, size)
        launch()
        for k in range(2):
            for g in range(2):
                rows, lanes = pl.ds(g * 4 * share, 4 * share), pl.ds(k * ROWS, ROWS)
                value = matmul(spare[0, rows, lanes], grad_out[:, columns])
                value += matmul(spare[1, rows, lanes], spare[2, pl.ds(0, ROWS), columns])
                r.tall_stage[k, g] = value.astype(low).reshape(2, 2, share, size)
        u, hop = early[p]
        opened.append((u, hop, store(r.tall_stage, getattr(r, f"grad_{u}"))))
    qkv_loads = load_qkv()

    grad_two = r.grad_two
    out_stage, grad_low = r.raw_out, r.grad_low
    for h in range(2):
        rows = pl.ds(h * PAD, half)
        value = stream_two[rows, :] + (forward[rows, :] + r.fc2_bias[...])
        out_stage[h] = value.astype(low)
    store(out_stage.at[seq], r.block_own)
    store(out_stage.at[1 - seq], r.block_send)
    launch()

    def norm_back(source, gain, back, extra, target, target_low, gain_row, shift_row):
        partial = r.partial
        partial[...] = jnp.zeros_like(partial)

        @pl.loop(0, ROWS // step)
        def _(i):
            rows = pl.ds(pl.multiple_of(i * step, step), step)
            unit, spread = norm_parts(source[rows, :])
            value = back[rows, :]
            partial[0] += fold_rows(value * unit)
            partial[1] += fold_rows(value)
            value = value * gain[...]
            mean = jnp.mean(value, axis=-1, keepdims=True)
            slope = jnp.mean(value * unit, axis=-1, keepdims=True)
            value = spread * (value - mean - unit * slope)
            value = value + extra[rows, :].astype(jnp.float32)
            if target is not None:
                target[rows, :] = value
            rounded = value.astype(low)
            target_low[rows, :] = rounded
            partial[2] += fold_rows(rounded.astype(jnp.float32))

        sums[gain_row : gain_row + 1, :] = jnp.sum(partial[0], axis=0, keepdims=True)
        sums[shift_row : shift_row + 1, :] = jnp.sum(partial[1], axis=0, keepdims=True)
        return jnp.sum(partial[2], axis=0, keepdims=True)

    sums[3:4, :] = norm_back(stream_two, r.gain_two, backward, grad_out, grad_two, grad_low, 4, 5)
    store(grad_low, r.right_proj)
    remote(grad_low, r.far_right_proj, 0)
    grad_mixed = r.grad_mixed

    for columns in tiles:
        grad_mixed[:, columns] = matmul_t(grad_low[...], r.proj_buffer[columns, :]).astype(low)

    grad_query, grad_key, grad_value = r.sum_a, r.sum_b, r.sum_c

    def attend_back(h, carry):
        start, mine = head_window(h)
        zero = jnp.zeros((), low)
        columns = pl.ds(start, window)
        query = jnp.where(mine, part(0, start), zero)
        back = jnp.where(mine, grad_mixed[:, columns], zero)
        share = probs[h]
        grad_share = matmul_t(back, part(2, start))
        wide = share.astype(jnp.float32)
        level = jnp.sum(wide * grad_share, axis=-1, keepdims=True)
        grad_score = (wide * (grad_share - level)).astype(low)
        found = t_matmul(share, back)
        grad_value[:, columns] = jnp.where(mine, found, grad_value[:, columns])
        found = matmul(grad_score, part(1, start)) * scale
        grad_query[:, columns] = jnp.where(mine, found, grad_query[:, columns])
        found = t_matmul(grad_score, query) * scale
        grad_key[:, columns] = jnp.where(mine, found, grad_key[:, columns])
        return carry

    lax.fori_loop(0, HEADS, attend_back, 0, unroll=4)
    for k, source in enumerate((grad_query, grad_key, grad_value)):
        packed[:, pl.ds(k * width, width)] = source[...].astype(low)
    store(packed, r.right_qkv)
    remote(packed, r.far_right_qkv, 0)
    for load in qkv_loads:
        load.wait()
    grad_normed = r.sum_a

    for columns in tiles:
        total = matmul_t(packed[:, pl.ds(0, width)], spare[0, columns, :])
        for k in range(1, 3):
            total += matmul_t(packed[:, pl.ds(k * width, width)], spare[k, columns, :])
        grad_normed[:, columns] = total

    grad_stream = r.grad_mixed
    sums[0:1, :] = norm_back(stream, r.gain_one, grad_normed, grad_two, None, grad_stream, 1, 2)
    store(grad_stream, r.right_skip)
    remote(grad_stream, r.far_right_skip, 0)
    sums[12:16, :] = jnp.zeros((4, width), jnp.float32)
    sums[6:7, :] = jnp.zeros((1, width), jnp.float32)
    store(sums, r.vectors)

    back_in = r.sum_b
    for load in again:
        load.wait()

    for columns in tiles:
        back_in[:, columns] = matmul_t(grad_stream[...], feed[2, columns, :])

    store(back_in.at[pl.ds(pl.multiple_of(seq * PAD, 64), half), :], r.grad_in_own)
    send_in = r.raw_in.at[0]
    send_in[...] = back_in[pl.ds(pl.multiple_of((1 - seq) * PAD, 64), half), :].astype(low)
    store(send_in, r.grad_in_send)
    feature = width // 2
    for f in range(2):
        value = matmul_t(grad_stream[...], feed[3, pl.ds(f * feature, feature), :])
        for h in range(2):
            piece = value[h * PAD : h * PAD + half]

            @pl.when(seq == f)
            def _():
                r.own_skip[h] = piece

            @pl.when(seq != f)
            def _():
                r.raw_skip[0, h] = piece.astype(low)

    store(r.own_skip, r.grad_skip_own)
    store(r.raw_skip.at[0], r.grad_skip_send)
    for item in stores.values():
        item.wait()
    for item in remotes:
        got_here(item)
        left_here(item)


WEIGHTS = ["fc1", "proj", "qkv", "skip"]


def run_block(arrays, matrices, units, width, hidden, half):
    low, wide = jnp.bfloat16, jnp.float32
    shape = jax.ShapeDtypeStruct
    outs = dict(
        block_own=shape((half, width), low),
        block_send=shape((half, width), low),
        grad_in_own=shape((half, width), wide),
        grad_in_send=shape((half, width), low),
        grad_skip_own=shape((2, half, width // 2), wide),
        grad_skip_send=shape((2, half, width // 2), low),
        vectors=shape((16, width), wide),
    )
    for name, matrix in zip(WEIGHTS, matrices[1:]):
        for prefix in ("", "far_"):
            outs[prefix + "left_" + name] = shape((matrix.left_rows(16), ROWS), low)
            outs[prefix + "right_" + name] = shape((ROWS, matrix.columns), low)
    outs.update(
        far_left_fc2=shape((matrices[0].left_rows(16), ROWS), low),
        far_right_fc2=shape((ROWS, width), low),
    )
    for u in EARLY:
        tail = (units[u].rows, units[u].columns)
        outs[f"grad_{u}"] = shape((2, 2, 2, 2) + tail, low)
        outs[f"far_grad_{u}"] = shape((2, 2, 2) + tail, low)
    early = [(u, units[u].hops[0]) for u in EARLY]
    staged = 16 * matrices[0].share // (hidden // width)
    square = (ROWS, width)
    scratch = dict(
        raw_in=((2, half, width), low),
        raw_skip=((2, 2, half, width // 2), low),
        raw_out=((2, half, width), low),
        spare=((3, width, width), low),
        proj_buffer=((width, width), low),
        feed=((4, width, width), low),
        joined=(square, low),
        skips=((2, ROWS, width // 2), low),
        grad_out=(square, low),
        stream=(square, wide),
        normed=(square, low),
        packed=((ROWS, 3 * width), low),
        probs=((HEADS, ROWS, ROWS), low),
        sum_a=(square, wide),
        sum_b=(square, wide),
        sum_c=(square, wide),
        mixed=(square, low),
        stream_two=(square, wide),
        normed_two=(square, low),
        acted=((2,) + square, low),
        grad_hidden=((2,) + square, low),
        left_fc2_stage=((2, staged, ROWS), low),
        tall_stage=((2, 2, 2, 2, matrices[0].share, 384), low),
        wide_stage=((2, 2, 2, 2, matrices[1].main, width), low),
        left_stage=((2, max(m.left_rows(16) for m in matrices[1:]), ROWS), low),
        turned=((width + 64, ROWS), wide),
        sums=((16, width), wide),
        partial=((3, 8, width), wide),
        grad_two=(square, wide),
        grad_low=(square, low),
        grad_mixed=(square, low),
        own_skip=((2, half, width // 2), wide),
    )
    anywhere = pl.BlockSpec(memory_space=pl.ANY)
    vmem = pl.BlockSpec(memory_space=pltpu.VMEM)
    smem = pl.BlockSpec(memory_space=pltpu.SMEM)
    small = {name for name, a in arrays.items() if a.dtype == wide}
    specs = [smem if n == "lengths" else vmem if n in small else anywhere for n in arrays]
    names = list(arrays) + list(outs) + list(scratch) + ["sems", "send_sem", "recv_sem"]
    results = pl.pallas_call(
        functools.partial(block_kernel, half, hidden, matrices, early, names),
        out_shape=list(outs.values()),
        in_specs=specs,
        out_specs=[anywhere] * len(outs),
        scratch_shapes=[pltpu.VMEM(*s) for s in scratch.values()]
        + [pltpu.SemaphoreType.DMA((n,)) for n in (80, 40, 40)],
        compiler_params=pltpu.CompilerParams(
            collective_id=1, has_side_effects=True, vmem_limit_bytes=63 * 2**20
        ),
        name="block",
    )(*arrays.values())
    return types.SimpleNamespace(**dict(zip(outs, results)))


MESH = pl.DeviceIdType.MESH
LANES = 384
SHIPS = 3
TWO = 2 * LANES


class Matrix:
    def __init__(self, share, columns, pieces, cuts):
        self.share, self.columns = share, columns
        self.main = share - share % 16
        self.rest = share % 16
        self.pieces, start = [], 0
        for width in pieces:
            self.pieces.append((start, width))
            start += width
        self.cuts = cuts
        self.fold = self.rest and 16
        self.fold_width = max(pieces)

    def left_rows(self, blocks):
        folds = len(self.pieces) if self.rest else 0
        return blocks * (self.main + folds * 16)


class Unit:
    def __init__(self, matrix, rows, start, columns, hops, folded):
        self.matrix, self.rows, self.start, self.columns = matrix, rows, start, columns
        self.hops, self.folded = hops, folded


def make_units(matrices, hops_of):
    units = []
    for m, matrix in enumerate(matrices):
        for start, columns in matrix.cuts:
            units.append(Unit(m, matrix.main, start, columns, hops_of[len(units)], False))
        if matrix.rest:
            units.append(Unit(m, 16, 0, matrix.fold_width, hops_of[len(units)], True))
    return units


def reduce_kernel(matrices, units, events, dims, *refs):
    count = len(matrices)
    lefts, far_lefts, rights, far_rights = ([None, *refs[k : 16 : 4]] for k in range(4))
    refs = refs[16:]
    whole_grads, refs = refs[: len(EARLY)], refs[len(EARLY) :]
    far_grads, refs = refs[: len(EARLY)], refs[len(EARLY) :]
    vector_ref, refs = refs[0], refs[1:]
    ships, refs = refs[:SHIPS], refs[SHIPS:]
    outs, refs = refs[: len(units)], refs[len(units) :]
    docks, refs = refs[:SHIPS], refs[SHIPS:]
    vector_out, refs = refs[0], refs[1:]
    grads, refs = refs[: len(units)], refs[len(units) :]
    hops = len(dims)
    landed = [refs[i * hops : (i + 1) * hops] for i in range(len(units))]
    refs = refs[len(units) * hops :]
    vector_land, vector_sum, refs = refs[0], refs[1], refs[2:]
    fold_sum, left_buffer, right_buffer, refs = refs[0], refs[1], refs[2], refs[3:]
    send_sem, recv_sem, vsend_sem, vrecv_sem, left_sem, right_sem, *refs = refs
    early_sem, ship_send, ship_recv = refs

    dp = lax.axis_index("dp")
    seq = lax.axis_index("seq")
    core = lax.rem(dp, 2)

    def bit(name):
        return seq if name == "seq" else lax.rem(lax.div(dp, 1 << name), 2)

    def partner(name):
        if name == "seq":
            return (dp, 1 - seq)
        return (dp + (1 - 2 * bit(name)) * (1 << name), seq)

    barrier = pltpu.get_barrier_semaphore()
    for name in [0] + list(dims):
        pl.semaphore_signal(barrier, inc=1, device_id=partner(name), device_id_type=MESH)
    pl.semaphore_wait(barrier, len(dims) + 1)

    sent = []

    def remote(source, target, send_at, recv_at, name):
        copy = pltpu.make_async_remote_copy(
            src_ref=source,
            dst_ref=target,
            send_sem=send_at,
            recv_sem=recv_at,
            device_id=partner(name),
            device_id_type=MESH,
        )
        copy.start()
        sent.append(copy)
        return copy

    early_copies = {}
    for k, u in enumerate(EARLY):
        hop = units[u].hops[0]
        index = tuple(bit(name) if name == hop else slice(None) for name in dims)
        early_copies[u] = [
            pltpu.make_async_copy(
                whole_grads[k].at[index], grads[u].at[index], early_sem.at[k, 0]
            ),
            pltpu.make_async_copy(far_grads[k], landed[u][0], early_sem.at[k, 1]),
        ]
        for copy in early_copies[u]:
            copy.start()

    def left_copies(m):
        rows = matrices[m].left_rows(2 ** len(dims))
        return [
            pltpu.make_async_copy(
                (lefts[m], far_lefts[m])[k],
                left_buffer.at[m % 2, pl.ds(0, rows), pl.ds(k * LANES, LANES)],
                left_sem.at[m % 2, k],
            )
            for k in range(2)
        ]

    all_pieces = [(m, p) for m in range(1, count) for p in range(len(matrices[m].pieces))]

    def right_copies(index):
        m, p = all_pieces[index]
        start, width = matrices[m].pieces[p]
        return [
            pltpu.make_async_copy(
                (rights[m], far_rights[m])[k].at[:, pl.ds(start, width)],
                right_buffer.at[index % 2, pl.ds(k * LANES, LANES), pl.ds(0, width)],
                right_sem.at[index % 2, k],
            )
            for k in range(2)
        ]

    def start(copies):
        for copy in copies:
            copy.start()

    def wait(copies):
        for copy in copies:
            copy.wait()

    start(left_copies(1))
    for index in range(2):
        start(right_copies(index))
    start(left_copies(2))

    def send(u, h):
        unit = units[u]
        index = []
        for name in dims:
            if name in unit.hops[:h]:
                index.append(bit(name))
            elif name == unit.hops[h]:
                index.append(1 - bit(name))
            else:
                index.append(slice(None))
        return remote(
            grads[u].at[tuple(index)],
            landed[u][h],
            send_sem.at[u, h],
            recv_sem.at[u, h],
            unit.hops[h],
        )

    flying = {}

    def add(u, h):
        unit = units[u]
        if h == 0 and u in EARLY:
            wait(early_copies[u])
        else:
            flying[u, h].wait_recv()
        done = unit.hops[: h + 1]
        free = [name for name in dims if name not in done]
        step = 16
        last = h + 1 == hops

        @pl.loop(0, 2 ** len(free) * (unit.rows // step))
        def _(i):
            block, row = lax.div(i, unit.rows // step), lax.rem(i, unit.rows // step) * step
            place = {
                name: lax.rem(lax.div(block, 1 << (len(free) - 1 - k)), 2)
                for k, name in enumerate(free)
            }
            rows = pl.ds(pl.multiple_of(row, step), step)
            own = tuple(place.get(name, bit(name)) for name in dims) + (rows,)
            got = tuple(place[name] for name in free) + (rows,)
            total = grads[u][own].astype(jnp.float32) + landed[u][h][got].astype(jnp.float32)
            if last:
                outs[u][rows] = total
            else:
                grads[u][own] = total.astype(jnp.bfloat16)

    def multiply(index):
        m, p = all_pieces[index]
        matrix = matrices[m]
        start_column, width = matrix.pieces[p]
        blocks = 2 ** len(dims)
        if p == 0:
            wait(left_copies(m))
        wait(right_copies(index))
        left, right = left_buffer.at[m % 2], right_buffer.at[index % 2]
        u = next(
            i
            for i, unit in enumerate(units)
            if unit.matrix == m
            and not unit.folded
            and unit.start <= start_column < unit.start + unit.columns
        )
        group = blocks
        while group * matrix.main > 640:
            group //= 2
        free = group.bit_length() - 1
        step = next(s for s in (384, 640, 512, 128) if width % s == 0)

        @pl.loop(0, 0 if u in EARLY else (blocks // group) * (width // step))
        def _(i):
            g, j = lax.div(i, width // step), lax.rem(i, width // step)
            rows = pl.ds(pl.multiple_of(g * (group * matrix.main), 16), group * matrix.main)
            columns = pl.ds(pl.multiple_of(j * step, 128), step)
            result = jnp.dot(left[rows, :], right[:, columns], preferred_element_type=jnp.float32)
            high = len(dims) - free
            where = tuple(lax.rem(lax.div(g, 1 << (high - 1 - k)), 2) for k in range(high))
            target = pl.ds(pl.multiple_of(start_column - units[u].start + j * step, 128), step)
            grads[u][where + (slice(None),) * (free + 1) + (target,)] = result.astype(
                jnp.bfloat16
            ).reshape((2,) * free + (matrix.main, step))

        if matrix.rest:
            offset = blocks * (matrix.main + 16 * p)

            @pl.loop(0, width // step)
            def _(j):
                columns = pl.ds(pl.multiple_of(j * step, 128), step)
                result = jnp.dot(
                    left[pl.ds(offset, blocks * 16), :],
                    right[:, columns],
                    preferred_element_type=jnp.float32,
                )
                if p == 0:
                    fold_sum[:, columns] = result
                else:
                    fold_sum[:, columns] += result

        if index + 2 < len(all_pieces):
            start(right_copies(index + 2))
        last = p + 1 == len(matrix.pieces)
        if last and m + 2 < count:
            start(left_copies(m + 2))
        if last and matrix.rest:
            f = next(i for i, unit in enumerate(units) if unit.matrix == m and unit.folded)
            folded = fold_sum[:, pl.ds(0, units[f].columns)].astype(jnp.bfloat16)
            grads[f][...] = folded.reshape((2,) * len(dims) + (16, units[f].columns))

    shipped = {}

    def ship(k):
        return remote(ships[k], docks[k], ship_send.at[k], ship_recv.at[k], "seq")

    path = [0] + list(dims)
    vector_flying = {}

    def vector_send(h):
        source = vector_ref if h == 0 else vector_sum.at[h - 1]
        return remote(source, vector_land.at[h], vsend_sem.at[h], vrecv_sem.at[h], path[h])

    def vector_add(h):
        vector_flying[h].wait_recv()
        before = vector_ref[...] if h == 0 else vector_sum[h - 1]
        total = before + vector_land[h]
        if h < hops:
            vector_sum[h] = total
            vector_flying[h + 1] = vector_send(h + 1)
        else:
            vector_out[...] = total

    vector_flying[0] = vector_send(0)
    vector_done, since = 0, 0
    for action, u, h in events:
        if action == COMPUTE:
            multiply(u)
        elif action == SEND and u == SHIP:
            shipped[h] = ship(h)
        elif action == SEND:
            flying[u, h] = send(u, h)
        elif u == SHIP:
            shipped[h].wait_recv()
        else:
            add(u, h)
            since += 1
            if since % 4 == 0 and vector_done <= hops:
                vector_add(vector_done)
                vector_done += 1
    while vector_done <= hops:
        vector_add(vector_done)
        vector_done += 1
    for copy in sent:
        copy.wait_send()


EARLY = (0, 1, 2, 3, 4, 5)
X, Y, Z, ZZ = "seq", 1, 2, 3
XYZ, YXZ, YZX = (X, Y, Z, ZZ), (Y, X, Z, ZZ), (Y, Z, ZZ, X)
ZXY, ZYX, XZY = (Z, ZZ, X, Y), (Z, ZZ, Y, X), (X, Z, ZZ, Y)
COMPUTE, SEND, TAKE, SHIP = 0, 1, 2, -1
HOP_PLAN = [XYZ, YZX, ZYX, XYZ, YZX, ZXY, XZY, YXZ, XYZ, XZY, YZX, YXZ, XYZ, YXZ, YXZ, YXZ, XZY]
EVENTS = [
    (SEND, SHIP, 0), (SEND, SHIP, 1), (TAKE, 0, 0), (SEND, 0, 1), (TAKE, 1, 0), (SEND, 1, 1),
    (COMPUTE, 0, 0), (TAKE, 2, 0), (SEND, 2, 1), (TAKE, 3, 0), (SEND, 3, 1), (TAKE, 4, 0),
    (SEND, 4, 1), (TAKE, 5, 0), (SEND, 5, 1), (COMPUTE, 1, 0), (COMPUTE, 2, 0), (COMPUTE, 3, 0),
    (TAKE, SHIP, 0), (SEND, 6, 0), (COMPUTE, 4, 0), (SEND, 7, 0), (TAKE, 0, 1), (SEND, 0, 2),
    (TAKE, 1, 1), (COMPUTE, 5, 0), (COMPUTE, 6, 0), (COMPUTE, 7, 0), (TAKE, SHIP, 1),
    (SEND, 8, 0), (SEND, 10, 0), (TAKE, 3, 1), (COMPUTE, 8, 0), (COMPUTE, 9, 0), (SEND, 11, 0),
    (TAKE, 7, 0), (SEND, 1, 2), (TAKE, 2, 1), (COMPUTE, 10, 0), (SEND, 3, 2), (TAKE, 4, 1),
    (SEND, 12, 0), (TAKE, 6, 0), (COMPUTE, 11, 0), (SEND, 14, 0), (TAKE, 10, 0), (SEND, 4, 2),
    (TAKE, 5, 1), (SEND, 6, 1), (TAKE, 0, 2), (SEND, 16, 0), (TAKE, 8, 0), (SEND, 0, 3),
    (TAKE, 1, 2), (SEND, 10, 1), (TAKE, 3, 2), (SEND, 15, 0), (TAKE, 11, 0), (SEND, 3, 3),
    (TAKE, 4, 2), (SEND, 11, 1), (TAKE, 12, 0), (TAKE, 6, 1), (SEND, 6, 2), (TAKE, 0, 3),
    (SEND, 7, 1), (TAKE, 16, 0), (SEND, 16, 1), (TAKE, 3, 3), (SEND, 13, 0), (TAKE, 14, 0),
    (TAKE, 10, 1), (SEND, 10, 2), (SEND, 14, 1), (TAKE, 11, 1), (SEND, 11, 2), (TAKE, 6, 2),
    (SEND, 5, 2), (TAKE, 7, 1), (SEND, 7, 2), (TAKE, 16, 1), (SEND, 16, 2), (TAKE, 10, 2),
    (SEND, 8, 1), (TAKE, 15, 0), (SEND, 15, 1), (TAKE, 14, 1), (SEND, 14, 2), (TAKE, 16, 2),
    (TAKE, 11, 2), (SEND, 11, 3), (SEND, 1, 3), (TAKE, 5, 2), (TAKE, 7, 2), (SEND, 7, 3),
    (SEND, 12, 1), (TAKE, 13, 0), (TAKE, 11, 3), (TAKE, 14, 2), (SEND, 14, 3), (SEND, 13, 1),
    (TAKE, 15, 1), (SEND, 15, 2), (TAKE, 7, 3), (SEND, 9, 0), (SEND, 4, 3), (TAKE, 1, 3),
    (SEND, 2, 2), (TAKE, 8, 1), (SEND, 8, 2), (SEND, 10, 3), (SEND, SHIP, 2), (TAKE, 13, 1),
    (TAKE, 14, 3), (SEND, 13, 2), (TAKE, 15, 2), (SEND, 15, 3), (TAKE, 9, 0), (SEND, 9, 1),
    (SEND, 6, 3), (TAKE, 12, 1), (TAKE, 4, 3), (SEND, 12, 2), (TAKE, 8, 2), (SEND, 8, 3),
    (TAKE, 10, 3), (TAKE, 13, 2), (SEND, 13, 3), (TAKE, 15, 3), (SEND, 5, 3), (SEND, 16, 3),
    (TAKE, 2, 2), (SEND, 2, 3), (TAKE, 9, 1), (SEND, 9, 2), (TAKE, 6, 3), (TAKE, 8, 3),
    (TAKE, 12, 2), (SEND, 12, 3), (TAKE, 5, 3), (TAKE, 13, 3), (TAKE, 16, 3), (TAKE, 9, 2),
    (SEND, 9, 3), (TAKE, SHIP, 2), (TAKE, 9, 3), (TAKE, 2, 3), (TAKE, 12, 3),
]


def weight_gradients(operands, vectors, ships, plan, bits):
    matrices, units, events = plan
    blocks = 2**bits
    dims = list(reversed(range(1, bits))) + ["seq"]
    given = len(operands)
    operands = [*operands, vectors, *ships]
    anywhere = pl.BlockSpec(memory_space=pl.ANY)
    vmem = pl.BlockSpec(memory_space=pltpu.VMEM)
    hops, count = len(dims), len(matrices)
    shape = jax.ShapeDtypeStruct
    outs = [shape((unit.rows, unit.columns), jnp.float32) for unit in units]
    outs += [shape(ship.shape, ship.dtype) for ship in ships]
    outs.append(shape(vectors.shape, jnp.float32))
    low = jnp.bfloat16
    scratch = [pltpu.VMEM((2,) * hops + (unit.rows, unit.columns), low) for unit in units]
    for unit in units:
        for h in range(hops):
            scratch.append(pltpu.VMEM((2,) * (hops - 1 - h) + (unit.rows, unit.columns), low))
    scratch.append(pltpu.VMEM((hops + 1,) + vectors.shape, jnp.float32))
    scratch.append(pltpu.VMEM((hops,) + vectors.shape, jnp.float32))
    folded = [matrix.fold_width for matrix in matrices if matrix.rest]
    scratch.append(pltpu.VMEM((blocks * 16, max(folded)), jnp.float32))
    scratch.append(pltpu.VMEM((2, max(m.left_rows(blocks) for m in matrices), TWO), low))
    scratch.append(pltpu.VMEM((2, TWO, max(max(w for _, w in m.pieces) for m in matrices)), low))
    scratch += [pltpu.SemaphoreType.DMA((len(units), hops))] * 2
    scratch += [pltpu.SemaphoreType.DMA((hops + 1,))] * 2
    scratch += [pltpu.SemaphoreType.DMA((2, 2))] * 2
    scratch += [pltpu.SemaphoreType.DMA((len(EARLY), 2))]
    scratch += [pltpu.SemaphoreType.DMA((SHIPS,))] * 2
    results = pl.pallas_call(
        functools.partial(reduce_kernel, matrices, units, events, dims),
        out_shape=outs,
        in_specs=[anywhere] * given + [vmem] + [anywhere] * SHIPS,
        out_specs=[vmem] * len(units) + [anywhere] * SHIPS + [vmem],
        scratch_shapes=scratch,
        compiler_params=pltpu.CompilerParams(
            collective_id=0, has_side_effects=True, vmem_limit_bytes=62 * 2**20
        ),
        name="reduce_weights",
    )(*operands)
    wholes = []
    for m, matrix in enumerate(matrices):
        mains = [r for r, u in zip(results, units) if u.matrix == m and not u.folded]
        whole = jnp.concatenate(mains, axis=1) if len(mains) > 1 else mains[0]
        if matrix.rest:
            fold = next(r for r, u in zip(results, units) if u.matrix == m and u.folded)
            parts = [
                fold[p * matrix.rest : (p + 1) * matrix.rest, :width]
                for p, (_, width) in enumerate(matrix.pieces)
            ]
            whole = jnp.concatenate([whole, jnp.concatenate(parts, axis=1)], axis=0)
        wholes.append(whole)
    return wholes, results[-1], results[len(units) : len(units) + SHIPS]


def even_cuts(columns, width):
    return [(start, width) for start in range(0, columns, width)]


def make_plan(width, hidden, chunks):
    matrices = [
        Matrix(hidden // chunks, width, [384] * 3, even_cuts(width, 384)),
        Matrix(width // chunks, hidden, [1152] * 4, even_cuts(hidden, 1152)),
        Matrix(width // chunks, width, [384] * 3, [(0, width)]),
        Matrix(width // chunks, 3 * width, [1152] * 3, even_cuts(3 * width, 1152)),
        Matrix(2 * width // chunks, width, [640, 512], [(0, 640), (640, 512)]),
    ]
    units = make_units(matrices, HOP_PLAN)
    return matrices, units, EVENTS


def halving(block, order, bits):
    dp_index = lax.axis_index("dp")
    seq_index = lax.axis_index("seq")
    dims = list(reversed(range(1, bits))) + ["seq"]
    for name in order:
        axis = dims.index(name)
        own = seq_index if name == "seq" else (dp_index >> name) & 1
        sent = pick(block, 1 - own, axis)
        kept = pick(block, own, axis)
        got = swap_seq(sent) if name == "seq" else swap_dp(sent, name)
        total = kept.astype(jnp.float32) + got.astype(jnp.float32)
        dims.pop(axis)
        block = total.astype(jnp.bfloat16) if dims else total
    return block


def local_permutes(
    inputs,
    skipped,
    lengths,
    cotangent,
    skip_weight,
    skip_bias,
    gain_one,
    shift_one,
    qkv_weight,
    proj_weight,
    proj_bias,
    gain_two,
    shift_two,
    fc1_weight,
    fc1_bias,
    fc2_weight,
    fc2_bias,
):
    items, half, width = inputs.shape
    seq_count = lax.axis_size("seq")
    dp_count = lax.axis_size("dp")
    bits = dp_count.bit_length() - 1
    seq_index = lax.axis_index("seq")
    core = lax.axis_index("dp") & 1
    first = seq_index == 0
    slots = half * seq_count

    def whole_item(values, axis):
        own = pick(values, seq_index, 0)
        got = swap_seq(pick(values, 1 - seq_index, 0))
        return place(first, own, got, axis)

    def to_owner(values, axis):
        parts = jnp.split(values, 2, axis=axis)
        own = jnp.where(first, parts[0], parts[1])
        other = jnp.where(first, parts[1], parts[0])
        got = swap_seq(other.astype(jnp.bfloat16)).astype(values.dtype)
        return place(first, own[None], got[None], 0)

    own_inputs = whole_item(inputs, 0)
    own_skip = whole_item(skipped, 1)
    grad_out = whole_item(cotangent, 0)
    length = pick(lengths, seq_index, 0)
    rows = slots

    joined = jnp.concatenate([own_inputs, own_skip], axis=-1)
    stream = matmul(joined, skip_weight) + skip_bias
    normed = layer_norm(stream, gain_one, shift_one).astype(jnp.bfloat16)
    packed = matmul(normed, qkv_weight).astype(jnp.bfloat16)
    heads = packed.reshape(rows, 3, HEADS, HEAD_DIM)
    query, keys, values = heads[:, 0], heads[:, 1], heads[:, 2]
    scale = HEAD_DIM ** (-0.5)
    positions = jnp.arange(slots, dtype=jnp.int32)
    caption = (positions >= 1) & (positions <= length)
    image = (positions >= 1 + CAPTION) & (positions < 1 + CAPTION + IMAGE)
    valid = (positions == 0) | caption | image

    def product(spec, left, right):
        return jnp.einsum(spec, left, right, preferred_element_type=jnp.float32)

    scores = product("qhd,khd->hqk", query, keys) * scale
    scores = jnp.where(valid[None, None, :], scores, masked_score)
    top = jnp.max(scores, axis=-1, keepdims=True)
    expo = jnp.exp(scores - top)
    probs = expo / jnp.sum(expo, axis=-1, keepdims=True)
    probs_low = probs.astype(jnp.bfloat16)
    mixed = product("hqk,khd->qhd", probs_low, values)
    mixed = mixed.astype(jnp.bfloat16).reshape(rows, width)
    attended = matmul(mixed, proj_weight) + proj_bias
    stream_two = stream + attended
    normed_two = layer_norm(stream_two, gain_two, shift_two).astype(jnp.bfloat16)
    hidden = matmul(normed_two, fc1_weight) + fc1_bias
    acted, gelu_back = jax.vjp(gelu_exact, hidden)
    acted_low = acted.astype(jnp.bfloat16)
    block_output = (stream_two + (matmul(acted_low, fc2_weight) + fc2_bias)).astype(jnp.bfloat16)

    blocks = dp_count // 2

    def own_rows(left, right):
        parts = left.reshape(rows, blocks, 2, -1)
        kept = pick(parts, core, 2).reshape(rows, -1)
        sent = pick(parts, 1 - core, 2).reshape(rows, -1)
        left_both = jnp.concatenate([kept, swap_dp(sent, 0)], axis=0)
        right_both = jnp.concatenate([right, swap_dp(right, 0)], axis=0)
        total = matmul(left_both.T, right_both).astype(jnp.bfloat16)
        share = total.shape[0] // (blocks * 2)
        return total.reshape((2,) * bits + (share, right.shape[1]))

    above = list(range(1, bits))
    order_x = ["seq"] + above
    order_y = above + ["seq"]
    order_z = above[1:] + ["seq"] + above[:1]

    grad_fc2 = halving(own_rows(acted_low, grad_out), order_x, bits)
    grad_fc2_bias = column_sum(grad_out)
    grad_acted = matmul(grad_out, fc2_weight.T)
    grad_hidden = gelu_back(grad_acted)[0].astype(jnp.bfloat16)
    grad_fc1 = halving(own_rows(normed_two, grad_hidden), order_x, bits)
    grad_fc1_bias = column_sum(grad_hidden)
    grad_normed_two = matmul(grad_hidden, fc1_weight.T)
    _, norm_back_two = jax.vjp(layer_norm, stream_two, gain_two, shift_two)
    back_two, grad_gain_two, grad_shift_two = norm_back_two(grad_normed_two)
    grad_stream_two = grad_out.astype(jnp.float32) + back_two
    grad_attended = grad_stream_two.astype(jnp.bfloat16)
    grad_proj = halving(own_rows(mixed, grad_attended), order_y, bits)
    grad_proj_bias = column_sum(grad_attended)
    grad_mixed = matmul(grad_attended, proj_weight.T)
    grad_mixed = grad_mixed.astype(jnp.bfloat16).reshape(rows, HEADS, HEAD_DIM)
    grad_probs = product("qhd,khd->hqk", grad_mixed, values)
    grad_scores = probs * (grad_probs - jnp.sum(probs * grad_probs, axis=-1, keepdims=True))
    grad_scores = grad_scores.astype(jnp.bfloat16)
    grad_values = product("hqk,qhd->khd", probs_low, grad_mixed)
    grad_query = product("hqk,khd->qhd", grad_scores, keys) * scale
    grad_keys = product("hqk,qhd->khd", grad_scores, query) * scale
    grad_packed = jnp.stack([grad_query, grad_keys, grad_values], axis=1)
    grad_packed = grad_packed.astype(jnp.bfloat16).reshape(rows, 3 * width)
    grad_qkv = halving(own_rows(normed, grad_packed), order_y, bits)
    grad_normed = matmul(grad_packed, qkv_weight.T)
    _, norm_back_one = jax.vjp(layer_norm, stream, gain_one, shift_one)
    back_one, grad_gain_one, grad_shift_one = norm_back_one(grad_normed)
    grad_stream = (grad_stream_two + back_one).astype(jnp.bfloat16)
    grad_skip = halving(own_rows(joined, grad_stream), order_z, bits)
    grad_skip_bias = column_sum(grad_stream)
    grad_joined = matmul(grad_stream, skip_weight.T)

    vectors = (
        grad_skip_bias,
        grad_gain_one,
        grad_shift_one,
        grad_proj_bias,
        grad_gain_two,
        grad_shift_two,
        grad_fc1_bias,
        grad_fc2_bias,
    )
    chunks = dp_count * seq_count
    line = jnp.concatenate([v.reshape(chunks, -1) for v in vectors], axis=1)
    line = lax.psum_scatter(line, ("dp", "seq"), scatter_dimension=0, tiled=True)[0]
    pieces, start = [], 0
    for vector in vectors:
        size = vector.shape[0] // chunks
        pieces.append(line[start : start + size])
        start += size

    return (
        to_owner(block_output, 0),
        to_owner(grad_joined[:, :width], 0),
        to_owner(grad_joined[:, width:], 1),
        grad_skip,
        pieces[0],
        pieces[1],
        pieces[2],
        grad_qkv,
        grad_proj,
        pieces[3],
        pieces[4],
        pieces[5],
        grad_fc1,
        pieces[6],
        grad_fc2,
        pieces[7],
    )


def local_kernels(*arguments):
    arrays = Arguments(*arguments)
    items, half, width = arrays.inputs.shape
    hidden = arrays.fc1_weight.shape[1]
    dp_count = lax.axis_size("dp")
    bits = dp_count.bit_length() - 1
    seq_index = lax.axis_index("seq")
    device = lax.axis_index("dp") * 2 + seq_index
    first = seq_index == 0
    chunks = dp_count * 2
    skipped = arrays.skipped.reshape(items, 2, half, width // 2)
    plan = make_plan(width, hidden, chunks)
    feed = dict(
        inputs=arrays.inputs,
        skipped=skipped,
        cotangent=arrays.cotangent,
        lengths=arrays.lengths,
    )
    for name in Arguments._fields[4:]:
        feed[name] = getattr(arrays, name)
    found = run_block(feed, *plan[:2], width, hidden, half)
    kinds = ("left_", "far_left_", "right_", "far_right_")
    operands = [getattr(found, kind + name) for name in WEIGHTS for kind in kinds]
    operands += [getattr(found, f"grad_{u}") for u in EARLY]
    operands += [getattr(found, f"far_grad_{u}") for u in EARLY]
    weights, vectors, got = weight_gradients(
        operands,
        found.vectors,
        [found.block_send, found.grad_in_send, found.grad_skip_send],
        plan,
        bits,
    )
    block_got, grad_in_got, grad_skip_got = got

    def owner(own, other):
        other = other.astype(own.dtype)
        return jnp.where(first, jnp.stack([own, other]), jnp.stack([other, own]))

    share = width // chunks
    mine = lax.dynamic_slice(vectors, (0, device * share), (8, share))
    wide_share = hidden // chunks
    per_row = width // wide_share
    row = 8 + device // per_row
    bias = lax.dynamic_slice(vectors, (row, device % per_row * wide_share), (1, wide_share))[0]
    grad_fc2, grad_fc1, grad_proj, grad_qkv, grad_skip = weights
    grad_skip_own = found.grad_skip_own.reshape(2 * half, -1)
    return (
        owner(found.block_own, block_got),
        owner(found.grad_in_own, grad_in_got),
        owner(grad_skip_own, grad_skip_got.reshape(2 * half, -1)),
        grad_skip,
        mine[0],
        mine[1],
        mine[2],
        grad_qkv,
        grad_proj,
        mine[3],
        mine[4],
        mine[5],
        grad_fc1,
        bias,
        grad_fc2,
        mine[7],
    )


class Arguments(typing.NamedTuple):
    inputs: jax.Array
    skipped: jax.Array
    lengths: jax.Array
    cotangent: jax.Array
    skip_weight: jax.Array
    skip_bias: jax.Array
    gain_one: jax.Array
    shift_one: jax.Array
    qkv_weight: jax.Array
    proj_weight: jax.Array
    proj_bias: jax.Array
    gain_two: jax.Array
    shift_two: jax.Array
    fc1_weight: jax.Array
    fc1_bias: jax.Array
    fc2_weight: jax.Array
    fc2_bias: jax.Array


def solution(mesh):
    small = mesh.shape["dp"] == 16
    return jax.shard_map(
        local_kernels if small else local_permutes,
        mesh=mesh,
        in_specs=(
            P("dp", "seq", None),
            P("dp", None, "seq"),
            P("dp"),
            P("dp", "seq", None),
        )
        + (P(),) * 13,
        out_specs=(
            P("dp", "seq", None),
            P("dp", "seq", None),
            P("dp", None, "seq"),
            P(("dp", "seq"), None),
            P(("dp", "seq")),
            P(("dp", "seq")),
            P(("dp", "seq")),
            P(("dp", "seq"), None),
            P(("dp", "seq"), None),
            P(("dp", "seq")),
            P(("dp", "seq")),
            P(("dp", "seq")),
            P(("dp", "seq"), None),
            P(("dp", "seq")),
            P(("dp", "seq"), None),
            P(("dp", "seq")),
        ),
        check_vma=False,
    )
```

```python
import functools
import types
import typing

import jax
import jax.numpy as jnp
from jax import lax
from jax.experimental import pallas as pl
from jax.experimental.pallas import tpu as pltpu
from jax.sharding import PartitionSpec as P

HEADS = 16
HEAD_DIM = 72
CAPTION = 77
IMAGE = 256


epsilon = 1e-05
masked_score = -1e30


def layer_norm(stream, gain, shift):
    center = stream - jnp.mean(stream, axis=-1, keepdims=True)
    spread = jnp.mean(center * center, axis=-1, keepdims=True)
    return center * lax.rsqrt(spread + epsilon) * gain + shift


def gelu_exact(values):
    return jax.nn.gelu(values, approximate=False)


def column_sum(values):
    return jnp.sum(values.astype(jnp.float32), axis=0)


def matmul(left, right):
    return jnp.dot(left, right, preferred_element_type=jnp.float32)


def swap_seq(values):
    return lax.ppermute(values, "seq", [(0, 1), (1, 0)])


def swap_dp(values, bit):
    count = lax.axis_size("dp")
    return lax.ppermute(values, "dp", [(i, i ^ (1 << bit)) for i in range(count)])


def pick(values, index, axis):
    return lax.dynamic_index_in_dim(values, index, axis, keepdims=False)


def place(first, own, got, axis):
    return jnp.where(
        first, jnp.concatenate([own, got], axis=axis), jnp.concatenate([got, own], axis=axis)
    )


PAD = 192
ROWS = 2 * PAD


def matmul_t(left, right):
    return lax.dot_general(
        left, right, (((1,), (1,)), ((), ())), preferred_element_type=jnp.float32
    )


def t_matmul(left, right):
    return lax.dot_general(
        left, right, (((0,), (0,)), ((), ())), preferred_element_type=jnp.float32
    )


def tiles_of(width):
    starts = list(range(0, width - 255, 512))
    ends = starts[1:] + [width]
    return [pl.ds(a, b - a) for a, b in zip(starts, ends)]


def norm_parts(values):
    center = values - jnp.mean(values, axis=-1, keepdims=True)
    spread = jnp.mean(center * center, axis=-1, keepdims=True)
    scale = lax.rsqrt(spread + epsilon)
    return center * scale, scale


def fold_rows(values):
    rows, width = values.shape
    return jnp.sum(values.reshape(rows // 8, 8, width), axis=0)


def block_kernel(half, hidden, matrices, early, names, *refs):
    r = types.SimpleNamespace(**dict(zip(names, refs)))
    width = r.skip_weight.shape[1]
    seq = lax.axis_index("seq")
    core = lax.rem(lax.axis_index("dp"), 2)
    sems = r.sems
    low = jnp.bfloat16
    counter = iter(range(80))

    def copy(source, target):
        return pltpu.make_async_copy(source, target, sems.at[next(counter)])

    loads = types.SimpleNamespace(
        in0=copy(r.inputs.at[seq], r.raw_in.at[seq]),
        sk0=copy(r.skipped.at[seq], r.raw_skip.at[seq]),
        skip0=copy(r.skip_weight.at[pl.ds(0, width), :], r.feed.at[0]),
        skip1=copy(r.skip_weight.at[pl.ds(width, width), :], r.feed.at[1]),
        ct0=copy(r.cotangent.at[seq], r.raw_out.at[seq]),
        proj=copy(r.proj_weight, r.proj_buffer),
    )
    spare = r.spare

    def load_qkv():
        parts = [
            copy(r.qkv_weight.at[:, pl.ds(k * width, width)], spare.at[k]) for k in range(3)
        ]
        for load in parts:
            load.start()
        return parts

    dp = lax.axis_index("dp")
    neighbour = (dp, 1 - seq)

    def flip(name):
        if name == "seq":
            return neighbour
        return (dp + (1 - 2 * lax.rem(lax.div(dp, 1 << name), 2)) * (1 << name), seq)

    barrier = pltpu.get_barrier_semaphore()
    names_met = [0] + sorted({hop for _, hop in early}, key=str)
    for name in names_met:
        pl.semaphore_signal(barrier, inc=1, device_id=flip(name), device_id_type=MESH)
    for load in vars(loads).values():
        load.start()
    qkv_loads = load_qkv()
    pl.semaphore_wait(barrier, len(names_met))
    remotes = []

    def remote(source, target, name):
        k = len(remotes)
        item = pltpu.make_async_remote_copy(
            src_ref=source,
            dst_ref=target,
            send_sem=r.send_sem.at[k],
            recv_sem=r.recv_sem.at[k],
            device_id=flip(name),
            device_id_type=MESH,
        )
        item.start()
        remotes.append(item)
        return item

    gone, come = set(), set()

    def left_here(item):
        if id(item) not in gone:
            gone.add(id(item))
            item.wait_send()

    def got_here(item):
        if id(item) not in come:
            come.add(id(item))
            item.wait_recv()

    traded = [
        remote(r.inputs.at[1 - seq], r.raw_in.at[seq], "seq"),
        remote(r.skipped.at[1 - seq], r.raw_skip.at[seq], "seq"),
    ]
    chunk, feed = width, r.feed
    feeds = []
    for j in range(hidden // chunk):
        part = pl.ds(j * chunk, chunk)
        at = 2 - 2 * (j % 2)
        feeds.append(
            (
                copy(r.fc1_weight.at[:, part], feed.at[at]),
                copy(r.fc2_weight.at[part, :], feed.at[at + 1]),
            )
        )

    def start(copies):
        for item in copies:
            item.start()

    start(feeds[0])
    stores = {}

    def store(source, target):
        item = copy(source, target)
        item.start()
        stores[id(item)] = item
        return item

    def finish(item):
        stores.pop(id(item)).wait()

    joined, skips, grad_out = r.joined, r.skips, r.grad_out
    gap = PAD - half
    for load in (loads.in0, loads.sk0):
        load.wait()
    for item in traded:
        got_here(item)
    traded = remote(r.cotangent.at[1 - seq], r.raw_out.at[seq], "seq")
    for h in range(2):
        joined[pl.ds(h * PAD, PAD), :] = jnp.concatenate(
            [r.raw_in[h], jnp.zeros((gap, width), low)], axis=0
        )
        for f in range(2):
            skips[f, pl.ds(h * PAD, PAD), :] = jnp.concatenate(
                [r.raw_skip[f, h], jnp.zeros((gap, width // 2), low)], axis=0
            )
    loads.skip0.wait()
    loads.skip1.wait()
    stream = r.stream
    tiles = tiles_of(width)

    for columns in tiles:
        total = matmul(joined[...], feed[0, :, columns])
        total += matmul(skips[0], feed[1, pl.ds(0, width // 2), columns])
        total += matmul(skips[1], feed[1, pl.ds(width // 2, width // 2), columns])
        stream[:, columns] = total + r.skip_bias[columns]

    start(feeds[1])
    step = 128

    def norm(source, gain, shift, target):
        @pl.loop(0, ROWS // step)
        def _(i):
            rows = pl.ds(pl.multiple_of(i * step, step), step)
            unit, _ = norm_parts(source[rows, :])
            target[rows, :] = (unit * gain[...] + shift[...]).astype(low)

    normed, packed = r.normed, r.packed
    norm(stream, r.gain_one, r.shift_one, normed)
    for load in qkv_loads:
        load.wait()

    for k in range(3):
        for columns in tiles:
            target = pl.ds(k * width + columns.start, columns.size)
            packed[:, target] = matmul(normed[...], spare[k, :, columns]).astype(low)

    length = r.lengths[seq]
    at = lax.broadcasted_iota(jnp.int32, (1, ROWS), 1)
    inner = jnp.where(at >= PAD, at - PAD, at)
    position = jnp.where(at >= PAD, at - PAD + half, at)
    valid = (position == 0) | ((position >= 1) & (position <= length))
    valid = valid | ((position >= 1 + CAPTION) & (position < 1 + CAPTION + IMAGE))
    valid = valid & (inner < half)
    scale = HEAD_DIM ** (-0.5)
    window = 256

    def head_window(h):
        start = jnp.minimum(lax.div(h * HEAD_DIM, 128) * 128, width - window)
        start = pl.multiple_of(start, 128)
        lane = lax.broadcasted_iota(jnp.int32, (1, window), 1) + start
        mine = (lane >= h * HEAD_DIM) & (lane < (h + 1) * HEAD_DIM)
        return start, mine

    def part(which, start):
        return packed[:, pl.ds(pl.multiple_of(which * width + start, 128), window)]

    mixed_sum, probs = r.sum_a, r.probs

    def attend(h, carry):
        start, mine = head_window(h)
        query = jnp.where(mine, part(0, start), jnp.zeros((), low))
        scores = matmul_t(query, part(1, start)) * scale
        scores = jnp.where(valid, scores, masked_score)
        expo = jnp.exp(scores - jnp.max(scores, axis=-1, keepdims=True))
        share = expo * (1.0 / jnp.sum(expo, axis=-1, keepdims=True))
        share = share.astype(low)
        probs[h] = share
        found = matmul(share, part(2, start))
        columns = pl.ds(start, window)
        mixed_sum[:, columns] = jnp.where(mine, found, mixed_sum[:, columns])
        return carry

    lax.fori_loop(0, HEADS, attend, 0, unroll=4)
    mixed, stream_two = r.mixed, r.stream_two
    mixed[...] = mixed_sum[...].astype(low)
    loads.proj.wait()

    for columns in tiles:
        total = matmul(mixed[...], r.proj_buffer[:, columns]) + r.proj_bias[columns]
        stream_two[:, columns] = stream[:, columns] + total

    normed_two = r.normed_two
    norm(stream_two, r.gain_two, r.shift_two, normed_two)
    loads.ct0.wait()
    got_here(traded)
    for h in range(2):
        grad_out[pl.ds(h * PAD, PAD), :] = jnp.concatenate(
            [r.raw_out[h], jnp.zeros((gap, width), low)], axis=0
        )
    far_out = remote(grad_out, r.far_right_fc2, 0)
    sums = r.sums
    sums[7:8, :] = jnp.sum(grad_out[...].astype(jnp.float32), axis=0, keepdims=True)

    turned_ref = r.turned
    stages = {}

    def left(m, target, far, sources):
        matrix = matrices[m]
        stage = r.left_stage
        for item in stages.pop(0, ()):
            finish(item) if id(item) in stores else left_here(item)
        share, main, rest = matrix.share, matrix.main, matrix.rest
        folds, body = len(matrix.pieces), 16 * main
        first = 0
        for source in sources:
            turned_ref[pl.ds(32, width), :] = source.T.astype(jnp.float32)
            for k in range(width // share):
                number = first + k
                c, block = number // 2 % 2, number // 4 * 2 + number % 2
                base = 32 + k * share
                place = c ^ core
                stage[place, pl.ds(block * main, main), :] = turned_ref[
                    pl.ds(base, main), :
                ].astype(low)
                row = lax.broadcasted_iota(jnp.int32, (16, 1), 0)
                for q in range(folds):
                    part = turned_ref[pl.ds(base + main - q * rest, 16), :]
                    part = jnp.where((row >= q * rest) & (row < (q + 1) * rest), part, 0.0)
                    stage[place, pl.ds(body + (q * 16 + block) * 16, 16), :] = part.astype(low)
            first += width // share
        rows = matrix.left_rows(16)
        stages[0] = [
            store(stage.at[0, pl.ds(0, rows), :], target),
            remote(stage.at[1, pl.ds(0, rows), :], far, 0),
        ]

    body = 16 * matrices[1].main
    left(1, r.left_fc1, r.far_left_fc1, [normed_two[...]])
    far_left = remotes[-1]
    near = copy(r.left_stage.at[0, pl.ds(0, body), :], spare.at[0, pl.ds(0, body), pl.ds(2 * ROWS, ROWS)])
    near.start()
    stores[id(near)] = near
    far_hidden = []
    opened, loading = [], []

    def fetch(source, target):
        item = copy(source, target)
        item.start()
        return item

    def launch():
        while opened:
            u, hop, item = opened.pop(0)
            finish(item)
            dims = [3, 2, 1, "seq"]
            bit = seq if hop == "seq" else lax.rem(lax.div(dp, 1 << hop), 2)
            index = tuple(1 - bit if name == hop else slice(None) for name in dims)
            remote(getattr(r, f"grad_{u}").at[index], getattr(r, f"far_grad_{u}"), hop)

    fetched = {}

    def prefetch(p):
        got_here(far_hidden[p])
        source = r.far_right_fc1.at[:, pl.ds(p * chunk, chunk)]
        fetched[p] = [fetch(source, spare.at[2, pl.ds(ROWS, ROWS), :])]
        if p == 0:
            got_here(far_left)
            target = spare.at[0, pl.ds(body, body), pl.ds(2 * ROWS, ROWS)]
            fetched[p].append(fetch(r.far_left_fc1.at[pl.ds(0, body), :], target))
            got_here(far_out)
            loading.append(fetch(r.far_right_fc2, spare.at[2, pl.ds(0, ROWS), :]))
        prefetch_left(p)

    def prefetch_left(p):
        got_here(far_acted[p])
        count = 4 * matrices[0].share
        source = r.far_left_fc2.at[pl.ds(p * count, count), :]
        target = spare.at[1, pl.ds(p % 2 * count, count), pl.ds(p // 2 * ROWS, ROWS)]
        loading.append(fetch(source, target))

    def early_hidden(p):
        for item in fetched.pop(p):
            item.wait()
        if p == 0:
            finish(near)
        launch()
        near_rows, far_rows = (spare[0, pl.ds(k * body, body), pl.ds(2 * ROWS, ROWS)] for k in range(2))
        for columns in tiles:
            value = matmul(near_rows, grad_hidden[p % 2, :, columns])
            value += matmul(far_rows, spare[2, pl.ds(ROWS, ROWS), columns])
            value = value.astype(low).reshape(2, 2, 2, 2, matrices[1].main, columns.size)
            r.wide_stage[:, :, :, :, :, columns] = value
        u, hop = early[3 + p]
        opened.append((u, hop, store(r.wide_stage, getattr(r, f"grad_{u}"))))

    forward, backward = r.sum_a, r.sum_b
    acted, grad_hidden, staged = r.acted, r.grad_hidden, r.left_fc2_stage
    pending, far_acted = {}, []
    for j, feeding in enumerate(feeds):
        slot = j % 2
        first, second = feed.at[2 - 2 * slot], feed.at[3 - 2 * slot]
        for load in feeding:
            load.wait()
        for item in pending.get(slot, ()):
            finish(item) if id(item) in stores else left_here(item)

        for columns in tiles:
            whole = pl.ds(j * chunk + columns.start, columns.size)
            value = matmul(normed_two[...], first[:, columns])
            value += r.fc1_bias[whole]
            phi = 0.5 + 0.5 * lax.erf(value * (0.5**0.5))
            bell = jnp.exp(-0.5 * value * value) * ((2 * jnp.pi) ** -0.5)
            acted[slot, :, columns] = (value * phi).astype(low)
            back = matmul_t(grad_out[...], second[columns, :])
            back = (back * (phi + value * bell)).astype(low)
            grad_hidden[slot, :, columns] = back
            sums[pl.ds(8 + j, 1), columns] = jnp.sum(
                back.astype(jnp.float32), axis=0, keepdims=True
            )

        if j >= 1:
            prefetch(j - 1)
        for columns in tiles:
            ahead = matmul(acted[slot], second[:, columns])
            back = matmul_t(grad_hidden[slot], first[columns, :])
            if j == 0:
                forward[:, columns] = ahead
                backward[:, columns] = back
            else:
                forward[:, columns] += ahead
                backward[:, columns] += back

        share = matrices[0].share
        turned = acted[slot].T
        groups = chunk // (4 * share)
        for g in range(groups):
            begin = g * 4 * share
            lower, upper = turned[begin : begin + 2 * share], turned[begin + 2 * share : begin + 4 * share]
            number = j * groups + g
            rows = pl.ds(number % 4 * 2 * share, 2 * share)
            spare[0, rows, pl.ds(number // 4 * ROWS, ROWS)] = jnp.where(core == 0, lower, upper)
            staged[slot, pl.ds(g * 2 * share, 2 * share), :] = jnp.where(core == 0, upper, lower)
        count = groups * 2 * share
        far_acted.append(remote(staged.at[slot], r.far_left_fc2.at[pl.ds(j * count, count), :], 0))
        part_columns = pl.ds(j * chunk, chunk)
        far_hidden.append(remote(grad_hidden.at[slot], r.far_right_fc1.at[:, part_columns], 0))
        pending[slot] = [
            far_acted[-1],
            far_hidden[-1],
            store(grad_hidden.at[slot], r.right_fc1.at[:, part_columns]),
        ]
        if j + 2 < len(feeds):
            start(feeds[j + 2])
        if 1 <= j < 4:
            early_hidden(j - 1)

    left(2, r.left_proj, r.far_left_proj, [mixed[...]])
    launch()
    prefetch_left(3)
    left(3, r.left_qkv, r.far_left_qkv, [normed[...]])
    left(4, r.left_skip, r.far_left_skip, [joined[...], jnp.concatenate([skips[0], skips[1]], axis=1)])

    for item in loading:
        item.wait()
    share = matrices[0].share
    for p in range(3):
        start_column, size = matrices[0].pieces[p]
        columns = pl.ds(start_column, size)
        launch()
        for k in range(2):
            for g in range(2):
                rows, lanes = pl.ds(g * 4 * share, 4 * share), pl.ds(k * ROWS, ROWS)
                value = matmul(spare[0, rows, lanes], grad_out[:, columns])
                value += matmul(spare[1, rows, lanes], spare[2, pl.ds(0, ROWS), columns])
                r.tall_stage[k, g] = value.astype(low).reshape(2, 2, share, size)
        u, hop = early[p]
        opened.append((u, hop, store(r.tall_stage, getattr(r, f"grad_{u}"))))
    qkv_loads = load_qkv()

    grad_two = r.grad_two
    out_stage, grad_low = r.raw_out, r.grad_low
    for h in range(2):
        rows = pl.ds(h * PAD, half)
        value = stream_two[rows, :] + (forward[rows, :] + r.fc2_bias[...])
        out_stage[h] = value.astype(low)
    store(out_stage.at[seq], r.block_own)
    remote(out_stage.at[1 - seq], r.block_got, "seq")
    launch()

    def norm_back(source, gain, back, extra, target, target_low, gain_row, shift_row):
        partial = r.partial
        partial[...] = jnp.zeros_like(partial)

        @pl.loop(0, ROWS // step)
        def _(i):
            rows = pl.ds(pl.multiple_of(i * step, step), step)
            unit, spread = norm_parts(source[rows, :])
            value = back[rows, :]
            partial[0] += fold_rows(value * unit)
            partial[1] += fold_rows(value)
            value = value * gain[...]
            mean = jnp.mean(value, axis=-1, keepdims=True)
            slope = jnp.mean(value * unit, axis=-1, keepdims=True)
            value = spread * (value - mean - unit * slope)
            value = value + extra[rows, :].astype(jnp.float32)
            if target is not None:
                target[rows, :] = value
            rounded = value.astype(low)
            target_low[rows, :] = rounded
            partial[2] += fold_rows(rounded.astype(jnp.float32))

        sums[gain_row : gain_row + 1, :] = jnp.sum(partial[0], axis=0, keepdims=True)
        sums[shift_row : shift_row + 1, :] = jnp.sum(partial[1], axis=0, keepdims=True)
        return jnp.sum(partial[2], axis=0, keepdims=True)

    sums[3:4, :] = norm_back(stream_two, r.gain_two, backward, grad_out, grad_two, grad_low, 4, 5)
    store(grad_low, r.right_proj)
    remote(grad_low, r.far_right_proj, 0)
    grad_mixed = r.grad_mixed

    for columns in tiles:
        grad_mixed[:, columns] = matmul_t(grad_low[...], r.proj_buffer[columns, :]).astype(low)

    grad_query, grad_key, grad_value = r.sum_a, r.sum_b, r.sum_c

    def attend_back(h, carry):
        start, mine = head_window(h)
        zero = jnp.zeros((), low)
        columns = pl.ds(start, window)
        query = jnp.where(mine, part(0, start), zero)
        back = jnp.where(mine, grad_mixed[:, columns], zero)
        share = probs[h]
        grad_share = matmul_t(back, part(2, start))
        wide = share.astype(jnp.float32)
        level = jnp.sum(wide * grad_share, axis=-1, keepdims=True)
        grad_score = (wide * (grad_share - level)).astype(low)
        found = t_matmul(share, back)
        grad_value[:, columns] = jnp.where(mine, found, grad_value[:, columns])
        found = matmul(grad_score, part(1, start)) * scale
        grad_query[:, columns] = jnp.where(mine, found, grad_query[:, columns])
        found = t_matmul(grad_score, query) * scale
        grad_key[:, columns] = jnp.where(mine, found, grad_key[:, columns])
        return carry

    lax.fori_loop(0, HEADS, attend_back, 0, unroll=4)
    for k, source in enumerate((grad_query, grad_key, grad_value)):
        packed[:, pl.ds(k * width, width)] = source[...].astype(low)
    store(packed, r.right_qkv)
    remote(packed, r.far_right_qkv, 0)
    for load in qkv_loads:
        load.wait()
    grad_normed = r.sum_a

    for columns in tiles:
        total = matmul_t(packed[:, pl.ds(0, width)], spare[0, columns, :])
        for k in range(1, 3):
            total += matmul_t(packed[:, pl.ds(k * width, width)], spare[k, columns, :])
        grad_normed[:, columns] = total

    grad_stream = r.grad_mixed
    sums[0:1, :] = norm_back(stream, r.gain_one, grad_normed, grad_two, None, grad_stream, 1, 2)
    store(grad_stream, r.right_skip)
    remote(grad_stream, r.far_right_skip, 0)
    sums[12:16, :] = jnp.zeros((4, width), jnp.float32)
    sums[6:7, :] = jnp.zeros((1, width), jnp.float32)
    store(sums, r.vectors)

    for item in stores.values():
        item.wait()
    for item in remotes:
        got_here(item)
        left_here(item)


WEIGHTS = ["fc1", "proj", "qkv", "skip"]


def run_block(arrays, matrices, units, width, hidden, half):
    low, wide = jnp.bfloat16, jnp.float32
    shape = jax.ShapeDtypeStruct
    outs = dict(
        block_own=shape((half, width), low),
        block_got=shape((half, width), low),
        vectors=shape((16, width), wide),
    )
    for name, matrix in zip(WEIGHTS, matrices[1:]):
        for prefix in ("", "far_"):
            outs[prefix + "left_" + name] = shape((matrix.left_rows(16), ROWS), low)
            outs[prefix + "right_" + name] = shape((ROWS, matrix.columns), low)
    outs.update(
        far_left_fc2=shape((matrices[0].left_rows(16), ROWS), low),
        far_right_fc2=shape((ROWS, width), low),
    )
    for u in EARLY:
        tail = (units[u].rows, units[u].columns)
        outs[f"grad_{u}"] = shape((2, 2, 2, 2) + tail, low)
        outs[f"far_grad_{u}"] = shape((2, 2, 2) + tail, low)
    early = [(u, units[u].hops[0]) for u in EARLY]
    staged = 16 * matrices[0].share // (hidden // width)
    square = (ROWS, width)
    scratch = dict(
        raw_in=((2, half, width), low),
        raw_skip=((2, 2, half, width // 2), low),
        raw_out=((2, half, width), low),
        spare=((3, width, width), low),
        proj_buffer=((width, width), low),
        feed=((4, width, width), low),
        joined=(square, low),
        skips=((2, ROWS, width // 2), low),
        grad_out=(square, low),
        stream=(square, wide),
        normed=(square, low),
        packed=((ROWS, 3 * width), low),
        probs=((HEADS, ROWS, ROWS), low),
        sum_a=(square, wide),
        sum_b=(square, wide),
        sum_c=(square, wide),
        mixed=(square, low),
        stream_two=(square, wide),
        normed_two=(square, low),
        acted=((2,) + square, low),
        grad_hidden=((2,) + square, low),
        left_fc2_stage=((2, staged, ROWS), low),
        tall_stage=((2, 2, 2, 2, matrices[0].share, 384), low),
        wide_stage=((2, 2, 2, 2, matrices[1].main, width), low),
        left_stage=((2, max(m.left_rows(16) for m in matrices[1:]), ROWS), low),
        turned=((width + 64, ROWS), wide),
        sums=((16, width), wide),
        partial=((3, 8, width), wide),
        grad_two=(square, wide),
        grad_low=(square, low),
        grad_mixed=(square, low),
    )
    anywhere = pl.BlockSpec(memory_space=pl.ANY)
    vmem = pl.BlockSpec(memory_space=pltpu.VMEM)
    smem = pl.BlockSpec(memory_space=pltpu.SMEM)
    small = {name for name, a in arrays.items() if a.dtype == wide}
    specs = [smem if n == "lengths" else vmem if n in small else anywhere for n in arrays]
    names = list(arrays) + list(outs) + list(scratch) + ["sems", "send_sem", "recv_sem"]
    results = pl.pallas_call(
        functools.partial(block_kernel, half, hidden, matrices, early, names),
        out_shape=list(outs.values()),
        in_specs=specs,
        out_specs=[anywhere] * len(outs),
        scratch_shapes=[pltpu.VMEM(*s) for s in scratch.values()]
        + [pltpu.SemaphoreType.DMA((n,)) for n in (80, 40, 40)],
        compiler_params=pltpu.CompilerParams(
            collective_id=1, has_side_effects=True, vmem_limit_bytes=63 * 2**20
        ),
        name="block",
    )(*arrays.values())
    return types.SimpleNamespace(**dict(zip(outs, results)))


MESH = pl.DeviceIdType.MESH
LANES = 384
SHIPS = 2
TWO = 2 * LANES


class Matrix:
    def __init__(self, share, columns, pieces, cuts):
        self.share, self.columns = share, columns
        self.main = share - share % 16
        self.rest = share % 16
        self.pieces, start = [], 0
        for width in pieces:
            self.pieces.append((start, width))
            start += width
        self.cuts = cuts
        self.fold = self.rest and 16
        self.fold_width = max(pieces)

    def left_rows(self, blocks):
        folds = len(self.pieces) if self.rest else 0
        return blocks * (self.main + folds * 16)


class Unit:
    def __init__(self, matrix, rows, start, columns, hops, folded):
        self.matrix, self.rows, self.start, self.columns = matrix, rows, start, columns
        self.hops, self.folded = hops, folded


def make_units(matrices, hops_of):
    units = []
    for m, matrix in enumerate(matrices):
        for start, columns in matrix.cuts:
            units.append(Unit(m, matrix.main, start, columns, hops_of[len(units)], False))
        if matrix.rest:
            units.append(Unit(m, 16, 0, matrix.fold_width, hops_of[len(units)], True))
    return units


def reduce_kernel(matrices, units, events, dims, *refs):
    count = len(matrices)
    lefts, far_lefts, rights, far_rights = ([None, *refs[k : 16 : 4]] for k in range(4))
    refs = refs[16:]
    whole_grads, refs = refs[: len(EARLY)], refs[len(EARLY) :]
    far_grads, refs = refs[: len(EARLY)], refs[len(EARLY) :]
    vector_ref, skip_ref, refs = refs[0], refs[1], refs[2:]
    outs, refs = refs[: len(units)], refs[len(units) :]
    docks, refs = refs[:SHIPS], refs[SHIPS:]
    own_in, own_skip, refs = refs[0], refs[1], refs[2:]
    vector_out, refs = refs[0], refs[1:]
    grads, refs = refs[: len(units)], refs[len(units) :]
    hops = len(dims)
    landed = [refs[i * hops : (i + 1) * hops] for i in range(len(units))]
    refs = refs[len(units) * hops :]
    vector_land, vector_sum, refs = refs[0], refs[1], refs[2:]
    fold_sum, left_buffer, right_buffer, refs = refs[0], refs[1], refs[2], refs[3:]
    send_sem, recv_sem, vsend_sem, vrecv_sem, left_sem, right_sem, *refs = refs
    early_sem, ship_send, ship_recv, skip_buffer, grad_stream, *refs = refs
    back_in, back_skip, send_in, send_skip, skip_sem = refs
    ships = [send_in, send_skip]

    dp = lax.axis_index("dp")
    seq = lax.axis_index("seq")
    core = lax.rem(dp, 2)

    def bit(name):
        return seq if name == "seq" else lax.rem(lax.div(dp, 1 << name), 2)

    def partner(name):
        if name == "seq":
            return (dp, 1 - seq)
        return (dp + (1 - 2 * bit(name)) * (1 << name), seq)

    barrier = pltpu.get_barrier_semaphore()
    for name in [0] + list(dims):
        pl.semaphore_signal(barrier, inc=1, device_id=partner(name), device_id_type=MESH)
    pl.semaphore_wait(barrier, len(dims) + 1)

    sent = []

    def remote(source, target, send_at, recv_at, name):
        copy = pltpu.make_async_remote_copy(
            src_ref=source,
            dst_ref=target,
            send_sem=send_at,
            recv_sem=recv_at,
            device_id=partner(name),
            device_id_type=MESH,
        )
        copy.start()
        sent.append(copy)
        return copy

    early_copies = {}
    for k, u in enumerate(EARLY):
        hop = units[u].hops[0]
        index = tuple(bit(name) if name == hop else slice(None) for name in dims)
        early_copies[u] = [
            pltpu.make_async_copy(
                whole_grads[k].at[index], grads[u].at[index], early_sem.at[k, 0]
            ),
            pltpu.make_async_copy(far_grads[k], landed[u][0], early_sem.at[k, 1]),
        ]
        for copy in early_copies[u]:
            copy.start()

    width = skip_buffer.shape[2]
    skip_copies = [
        pltpu.make_async_copy(
            skip_ref.at[pl.ds(k * width, width), :], skip_buffer.at[k], skip_sem.at[k]
        )
        for k in range(2)
    ]
    skip_copies.append(pltpu.make_async_copy(rights[4], grad_stream, skip_sem.at[2]))
    kept = []

    def finish_inputs():
        wait(skip_copies)
        half, feature = send_in.shape[0], width // 2
        for columns in tiles_of(width):
            value = matmul_t(grad_stream[...], skip_buffer[0, columns, :])
            lower, upper = value[:half], value[PAD : PAD + half]
            back_in[:, columns] = jnp.where(seq == 0, lower, upper)
            send_in[:, columns] = jnp.where(seq == 0, upper, lower).astype(jnp.bfloat16)
        parts = [
            matmul_t(grad_stream[...], skip_buffer[1, pl.ds(f * feature, feature), :])
            for f in range(2)
        ]
        for h in range(2):
            lower, upper = (part[h * PAD : h * PAD + half] for part in parts)
            back_skip[h] = jnp.where(seq == 0, lower, upper)
            send_skip[h] = jnp.where(seq == 0, upper, lower).astype(jnp.bfloat16)
        kept.append(pltpu.make_async_copy(back_in, own_in, skip_sem.at[3]))
        kept.append(pltpu.make_async_copy(back_skip, own_skip, skip_sem.at[4]))
        start(kept)

    def left_copies(m):
        rows = matrices[m].left_rows(2 ** len(dims))
        return [
            pltpu.make_async_copy(
                (lefts[m], far_lefts[m])[k],
                left_buffer.at[m % 2, pl.ds(0, rows), pl.ds(k * LANES, LANES)],
                left_sem.at[m % 2, k],
            )
            for k in range(2)
        ]

    all_pieces = [(m, p) for m in range(1, count) for p in range(len(matrices[m].pieces))]

    def right_copies(index):
        m, p = all_pieces[index]
        start, width = matrices[m].pieces[p]
        return [
            pltpu.make_async_copy(
                (rights[m], far_rights[m])[k].at[:, pl.ds(start, width)],
                right_buffer.at[index % 2, pl.ds(k * LANES, LANES), pl.ds(0, width)],
                right_sem.at[index % 2, k],
            )
            for k in range(2)
        ]

    def start(copies):
        for copy in copies:
            copy.start()

    def wait(copies):
        for copy in copies:
            copy.wait()

    start(left_copies(1))
    for index in range(2):
        start(right_copies(index))
    start(left_copies(2))
    start(skip_copies)

    def send(u, h):
        unit = units[u]
        index = []
        for name in dims:
            if name in unit.hops[:h]:
                index.append(bit(name))
            elif name == unit.hops[h]:
                index.append(1 - bit(name))
            else:
                index.append(slice(None))
        return remote(
            grads[u].at[tuple(index)],
            landed[u][h],
            send_sem.at[u, h],
            recv_sem.at[u, h],
            unit.hops[h],
        )

    flying = {}

    def add(u, h):
        unit = units[u]
        if h == 0 and u in EARLY:
            wait(early_copies[u])
        else:
            flying[u, h].wait_recv()
        done = unit.hops[: h + 1]
        free = [name for name in dims if name not in done]
        step = next(n for n in (48, 32, 16) if unit.rows % n == 0)
        last = h + 1 == hops

        @pl.loop(0, 2 ** len(free) * (unit.rows // step))
        def _(i):
            block, row = lax.div(i, unit.rows // step), lax.rem(i, unit.rows // step) * step
            place = {
                name: lax.rem(lax.div(block, 1 << (len(free) - 1 - k)), 2)
                for k, name in enumerate(free)
            }
            rows = pl.ds(pl.multiple_of(row, step), step)
            own = tuple(place.get(name, bit(name)) for name in dims) + (rows,)
            got = tuple(place[name] for name in free) + (rows,)
            total = grads[u][own].astype(jnp.float32) + landed[u][h][got].astype(jnp.float32)
            if last:
                outs[u][rows] = total
            else:
                grads[u][own] = total.astype(jnp.bfloat16)

    def multiply(index):
        m, p = all_pieces[index]
        matrix = matrices[m]
        start_column, width = matrix.pieces[p]
        blocks = 2 ** len(dims)
        if p == 0:
            wait(left_copies(m))
        wait(right_copies(index))
        left, right = left_buffer.at[m % 2], right_buffer.at[index % 2]
        u = next(
            i
            for i, unit in enumerate(units)
            if unit.matrix == m
            and not unit.folded
            and unit.start <= start_column < unit.start + unit.columns
        )
        group = blocks
        while group * matrix.main > 640:
            group //= 2
        free = group.bit_length() - 1
        step = next(s for s in (384, 640, 512, 128) if width % s == 0)

        @pl.loop(0, 0 if u in EARLY else (blocks // group) * (width // step))
        def _(i):
            g, j = lax.div(i, width // step), lax.rem(i, width // step)
            rows = pl.ds(pl.multiple_of(g * (group * matrix.main), 16), group * matrix.main)
            columns = pl.ds(pl.multiple_of(j * step, 128), step)
            result = jnp.dot(left[rows, :], right[:, columns], preferred_element_type=jnp.float32)
            high = len(dims) - free
            where = tuple(lax.rem(lax.div(g, 1 << (high - 1 - k)), 2) for k in range(high))
            target = pl.ds(pl.multiple_of(start_column - units[u].start + j * step, 128), step)
            grads[u][where + (slice(None),) * (free + 1) + (target,)] = result.astype(
                jnp.bfloat16
            ).reshape((2,) * free + (matrix.main, step))

        if matrix.rest:
            offset = blocks * (matrix.main + 16 * p)

            @pl.loop(0, width // step)
            def _(j):
                columns = pl.ds(pl.multiple_of(j * step, 128), step)
                result = jnp.dot(
                    left[pl.ds(offset, blocks * 16), :],
                    right[:, columns],
                    preferred_element_type=jnp.float32,
                )
                if p == 0:
                    fold_sum[:, columns] = result
                else:
                    fold_sum[:, columns] += result

        if index + 2 < len(all_pieces):
            start(right_copies(index + 2))
        last = p + 1 == len(matrix.pieces)
        if last and m + 2 < count:
            start(left_copies(m + 2))
        if last and matrix.rest:
            f = next(i for i, unit in enumerate(units) if unit.matrix == m and unit.folded)
            folded = fold_sum[:, pl.ds(0, units[f].columns)].astype(jnp.bfloat16)
            grads[f][...] = folded.reshape((2,) * len(dims) + (16, units[f].columns))

    shipped = {}

    def ship(k):
        return remote(ships[k], docks[k], ship_send.at[k], ship_recv.at[k], "seq")

    path = [0] + list(dims)
    vector_flying = {}

    def vector_send(h):
        source = vector_ref if h == 0 else vector_sum.at[h - 1]
        return remote(source, vector_land.at[h], vsend_sem.at[h], vrecv_sem.at[h], path[h])

    def vector_add(h):
        vector_flying[h].wait_recv()
        before = vector_ref[...] if h == 0 else vector_sum[h - 1]
        total = before + vector_land[h]
        if h < hops:
            vector_sum[h] = total
            vector_flying[h + 1] = vector_send(h + 1)
        else:
            vector_out[...] = total

    vector_flying[0] = vector_send(0)
    vector_done, since = 0, 0
    for action, u, h in events:
        if action == COMPUTE and u == SHIP:
            finish_inputs()
        elif action == COMPUTE:
            multiply(u)
        elif action == SEND and u == SHIP:
            shipped[h] = ship(h)
        elif action == SEND:
            flying[u, h] = send(u, h)
        elif u == SHIP:
            shipped[h].wait_recv()
        else:
            add(u, h)
            since += 1
            if since % 12 == 0 and vector_done <= hops:
                vector_add(vector_done)
                vector_done += 1
    while vector_done <= hops:
        vector_add(vector_done)
        vector_done += 1
    wait(kept)
    for copy in sent:
        copy.wait_send()


EARLY = (0, 1, 2, 3, 4, 5)
X, Y, Z, ZZ = "seq", 1, 2, 3
XYZ, YXZ, YZX = (X, Y, Z, ZZ), (Y, X, Z, ZZ), (Y, Z, ZZ, X)
ZXY, ZYX, XZY = (Z, ZZ, X, Y), (Z, ZZ, Y, X), (X, Z, ZZ, Y)
COMPUTE, SEND, TAKE, SHIP = 0, 1, 2, -1
HOP_PLAN = [XZY, YXZ, ZYX, XYZ, YXZ, ZXY, YXZ, XYZ, YZX, XZY, YXZ, YXZ, YXZ, YXZ, XZY, XYZ, ZXY]
EVENTS = [
    (TAKE, 0, 0), (SEND, 0, 1), (TAKE, 1, 0), (SEND, 1, 1), (TAKE, 2, 0), (SEND, 2, 1),
    (TAKE, 3, 0), (SEND, 3, 1), (TAKE, 4, 0), (SEND, 4, 1), (TAKE, 5, 0), (SEND, 5, 1),
    (COMPUTE, 0, 0), (COMPUTE, 1, 0), (COMPUTE, 2, 0), (COMPUTE, 3, 0), (SEND, 6, 0),
    (TAKE, 3, 1), (SEND, 3, 2), (COMPUTE, SHIP, 0), (TAKE, 0, 1), (SEND, 7, 0), (TAKE, 1, 1),
    (SEND, 1, 2), (COMPUTE, 4, 0), (SEND, SHIP, 0), (TAKE, 4, 1), (COMPUTE, 5, 0),
    (COMPUTE, 6, 0), (SEND, 8, 0), (COMPUTE, 7, 0), (SEND, 0, 2), (TAKE, 2, 1), (SEND, 9, 0),
    (TAKE, 7, 0), (SEND, 10, 0), (TAKE, 6, 0), (COMPUTE, 8, 0), (COMPUTE, 9, 0), (SEND, 4, 2),
    (TAKE, 3, 2), (TAKE, SHIP, 0), (SEND, 6, 1), (COMPUTE, 10, 0), (SEND, 3, 3), (TAKE, 5, 1),
    (SEND, 14, 0), (TAKE, 9, 0), (SEND, 9, 1), (TAKE, 1, 2), (COMPUTE, 11, 0), (SEND, 16, 0),
    (SEND, 11, 0), (TAKE, 8, 0), (SEND, 15, 0), (TAKE, 6, 1), (SEND, 8, 1), (TAKE, 4, 2),
    (SEND, 1, 3), (SEND, 4, 3), (TAKE, 0, 2), (TAKE, 9, 1), (SEND, 9, 2), (TAKE, 3, 3),
    (SEND, 6, 2), (TAKE, 16, 0), (SEND, 16, 1), (SEND, 12, 0), (TAKE, 10, 0), (TAKE, 1, 3),
    (TAKE, 4, 3), (TAKE, 8, 1), (SEND, 8, 2), (TAKE, 9, 2), (SEND, 10, 1), (TAKE, 14, 0),
    (SEND, 14, 1), (TAKE, 16, 1), (SEND, 13, 0), (TAKE, 11, 0), (TAKE, 6, 2), (SEND, 6, 3),
    (TAKE, 8, 2), (SEND, 11, 1), (TAKE, 15, 0), (TAKE, 6, 3), (SEND, 5, 2), (TAKE, 10, 1),
    (SEND, 10, 2), (TAKE, 14, 1), (SEND, 14, 2), (SEND, 15, 1), (TAKE, 12, 0), (SEND, 12, 1),
    (TAKE, 11, 1), (SEND, 11, 2), (TAKE, 10, 2), (SEND, 10, 3), (SEND, 2, 2), (TAKE, 13, 0),
    (SEND, 13, 1), (TAKE, 5, 2), (TAKE, 14, 2), (TAKE, 11, 2), (SEND, 11, 3), (SEND, 7, 1),
    (TAKE, 15, 1), (SEND, 15, 2), (TAKE, 10, 3), (SEND, 8, 3), (SEND, 16, 2), (TAKE, 12, 1),
    (SEND, 12, 2), (SEND, 0, 3), (TAKE, 2, 2), (SEND, 2, 3), (SEND, SHIP, 1), (TAKE, 13, 1),
    (TAKE, 11, 3), (SEND, 13, 2), (TAKE, 15, 2), (SEND, 15, 3), (TAKE, 8, 3), (TAKE, 16, 2),
    (SEND, 14, 3), (SEND, 5, 3), (TAKE, 7, 1), (SEND, 7, 2), (TAKE, 12, 2), (SEND, 12, 3),
    (TAKE, 2, 3), (SEND, 16, 3), (SEND, 9, 3), (TAKE, 0, 3), (TAKE, 13, 2), (SEND, 13, 3),
    (TAKE, 15, 3), (TAKE, 14, 3), (TAKE, 5, 3), (TAKE, 7, 2), (SEND, 7, 3), (TAKE, 16, 3),
    (TAKE, 9, 3), (TAKE, 12, 3), (TAKE, 13, 3), (TAKE, 7, 3), (TAKE, SHIP, 1),
]


def weight_gradients(operands, vectors, skip_weight, half, plan, bits):
    matrices, units, events = plan
    blocks = 2**bits
    dims = list(reversed(range(1, bits))) + ["seq"]
    given = len(operands)
    operands = [*operands, vectors, skip_weight]
    width = skip_weight.shape[1]
    ends = [(half, width), (2, half, width // 2)]
    anywhere = pl.BlockSpec(memory_space=pl.ANY)
    vmem = pl.BlockSpec(memory_space=pltpu.VMEM)
    hops, count = len(dims), len(matrices)
    shape = jax.ShapeDtypeStruct
    outs = [shape((unit.rows, unit.columns), jnp.float32) for unit in units]
    outs += [shape(end, jnp.bfloat16) for end in ends]
    outs += [shape(end, jnp.float32) for end in ends]
    outs.append(shape(vectors.shape, jnp.float32))
    low = jnp.bfloat16
    scratch = [pltpu.VMEM((2,) * hops + (unit.rows, unit.columns), low) for unit in units]
    for unit in units:
        for h in range(hops):
            scratch.append(pltpu.VMEM((2,) * (hops - 1 - h) + (unit.rows, unit.columns), low))
    scratch.append(pltpu.VMEM((hops + 1,) + vectors.shape, jnp.float32))
    scratch.append(pltpu.VMEM((hops,) + vectors.shape, jnp.float32))
    folded = [matrix.fold_width for matrix in matrices if matrix.rest]
    scratch.append(pltpu.VMEM((blocks * 16, max(folded)), jnp.float32))
    scratch.append(pltpu.VMEM((2, max(m.left_rows(blocks) for m in matrices), TWO), low))
    scratch.append(pltpu.VMEM((2, TWO, max(max(w for _, w in m.pieces) for m in matrices)), low))
    scratch += [pltpu.SemaphoreType.DMA((len(units), hops))] * 2
    scratch += [pltpu.SemaphoreType.DMA((hops + 1,))] * 2
    scratch += [pltpu.SemaphoreType.DMA((2, 2))] * 2
    scratch += [pltpu.SemaphoreType.DMA((len(EARLY), 2))]
    scratch += [pltpu.SemaphoreType.DMA((SHIPS,))] * 2
    scratch += [pltpu.VMEM((2, width, width), low), pltpu.VMEM((LANES, width), low)]
    scratch += [pltpu.VMEM(end, jnp.float32) for end in ends]
    scratch += [pltpu.VMEM(end, low) for end in ends]
    scratch.append(pltpu.SemaphoreType.DMA((5,)))
    results = pl.pallas_call(
        functools.partial(reduce_kernel, matrices, units, events, dims),
        out_shape=outs,
        in_specs=[anywhere] * given + [vmem, anywhere],
        out_specs=[vmem] * len(units) + [anywhere] * (2 * SHIPS) + [vmem],
        scratch_shapes=scratch,
        compiler_params=pltpu.CompilerParams(
            collective_id=0, has_side_effects=True, vmem_limit_bytes=62 * 2**20
        ),
        name="reduce_weights",
    )(*operands)
    wholes = []
    for m, matrix in enumerate(matrices):
        mains = [r for r, u in zip(results, units) if u.matrix == m and not u.folded]
        whole = jnp.concatenate(mains, axis=1) if len(mains) > 1 else mains[0]
        if matrix.rest:
            fold = next(r for r, u in zip(results, units) if u.matrix == m and u.folded)
            parts = [
                fold[p * matrix.rest : (p + 1) * matrix.rest, :width]
                for p, (_, width) in enumerate(matrix.pieces)
            ]
            whole = jnp.concatenate([whole, jnp.concatenate(parts, axis=1)], axis=0)
        wholes.append(whole)
    return wholes, results[-1], results[len(units) : -1]


def even_cuts(columns, width):
    return [(start, width) for start in range(0, columns, width)]


def make_plan(width, hidden, chunks):
    matrices = [
        Matrix(hidden // chunks, width, [384] * 3, even_cuts(width, 384)),
        Matrix(width // chunks, hidden, [1152] * 4, even_cuts(hidden, 1152)),
        Matrix(width // chunks, width, [384] * 3, [(0, width)]),
        Matrix(width // chunks, 3 * width, [1152] * 3, even_cuts(3 * width, 1152)),
        Matrix(2 * width // chunks, width, [640, 512], [(0, 640), (640, 512)]),
    ]
    units = make_units(matrices, HOP_PLAN)
    return matrices, units, EVENTS


def halving(block, order, bits):
    dp_index = lax.axis_index("dp")
    seq_index = lax.axis_index("seq")
    dims = list(reversed(range(1, bits))) + ["seq"]
    for name in order:
        axis = dims.index(name)
        own = seq_index if name == "seq" else (dp_index >> name) & 1
        sent = pick(block, 1 - own, axis)
        kept = pick(block, own, axis)
        got = swap_seq(sent) if name == "seq" else swap_dp(sent, name)
        total = kept.astype(jnp.float32) + got.astype(jnp.float32)
        dims.pop(axis)
        block = total.astype(jnp.bfloat16) if dims else total
    return block


def local_permutes(
    inputs,
    skipped,
    lengths,
    cotangent,
    skip_weight,
    skip_bias,
    gain_one,
    shift_one,
    qkv_weight,
    proj_weight,
    proj_bias,
    gain_two,
    shift_two,
    fc1_weight,
    fc1_bias,
    fc2_weight,
    fc2_bias,
):
    items, half, width = inputs.shape
    seq_count = lax.axis_size("seq")
    dp_count = lax.axis_size("dp")
    bits = dp_count.bit_length() - 1
    seq_index = lax.axis_index("seq")
    core = lax.axis_index("dp") & 1
    first = seq_index == 0
    slots = half * seq_count

    def whole_item(values, axis):
        own = pick(values, seq_index, 0)
        got = swap_seq(pick(values, 1 - seq_index, 0))
        return place(first, own, got, axis)

    def to_owner(values, axis):
        parts = jnp.split(values, 2, axis=axis)
        own = jnp.where(first, parts[0], parts[1])
        other = jnp.where(first, parts[1], parts[0])
        got = swap_seq(other.astype(jnp.bfloat16)).astype(values.dtype)
        return place(first, own[None], got[None], 0)

    own_inputs = whole_item(inputs, 0)
    own_skip = whole_item(skipped, 1)
    grad_out = whole_item(cotangent, 0)
    length = pick(lengths, seq_index, 0)
    rows = slots

    joined = jnp.concatenate([own_inputs, own_skip], axis=-1)
    stream = matmul(joined, skip_weight) + skip_bias
    normed = layer_norm(stream, gain_one, shift_one).astype(jnp.bfloat16)
    packed = matmul(normed, qkv_weight).astype(jnp.bfloat16)
    heads = packed.reshape(rows, 3, HEADS, HEAD_DIM)
    query, keys, values = heads[:, 0], heads[:, 1], heads[:, 2]
    scale = HEAD_DIM ** (-0.5)
    positions = jnp.arange(slots, dtype=jnp.int32)
    caption = (positions >= 1) & (positions <= length)
    image = (positions >= 1 + CAPTION) & (positions < 1 + CAPTION + IMAGE)
    valid = (positions == 0) | caption | image

    def product(spec, left, right):
        return jnp.einsum(spec, left, right, preferred_element_type=jnp.float32)

    scores = product("qhd,khd->hqk", query, keys) * scale
    scores = jnp.where(valid[None, None, :], scores, masked_score)
    top = jnp.max(scores, axis=-1, keepdims=True)
    expo = jnp.exp(scores - top)
    probs = expo / jnp.sum(expo, axis=-1, keepdims=True)
    probs_low = probs.astype(jnp.bfloat16)
    mixed = product("hqk,khd->qhd", probs_low, values)
    mixed = mixed.astype(jnp.bfloat16).reshape(rows, width)
    attended = matmul(mixed, proj_weight) + proj_bias
    stream_two = stream + attended
    normed_two = layer_norm(stream_two, gain_two, shift_two).astype(jnp.bfloat16)
    hidden = matmul(normed_two, fc1_weight) + fc1_bias
    acted, gelu_back = jax.vjp(gelu_exact, hidden)
    acted_low = acted.astype(jnp.bfloat16)
    block_output = (stream_two + (matmul(acted_low, fc2_weight) + fc2_bias)).astype(jnp.bfloat16)

    blocks = dp_count // 2

    def own_rows(left, right):
        parts = left.reshape(rows, blocks, 2, -1)
        kept = pick(parts, core, 2).reshape(rows, -1)
        sent = pick(parts, 1 - core, 2).reshape(rows, -1)
        left_both = jnp.concatenate([kept, swap_dp(sent, 0)], axis=0)
        right_both = jnp.concatenate([right, swap_dp(right, 0)], axis=0)
        total = matmul(left_both.T, right_both).astype(jnp.bfloat16)
        share = total.shape[0] // (blocks * 2)
        return total.reshape((2,) * bits + (share, right.shape[1]))

    above = list(range(1, bits))
    order_x = ["seq"] + above
    order_y = above + ["seq"]
    order_z = above[1:] + ["seq"] + above[:1]

    grad_fc2 = halving(own_rows(acted_low, grad_out), order_x, bits)
    grad_fc2_bias = column_sum(grad_out)
    grad_acted = matmul(grad_out, fc2_weight.T)
    grad_hidden = gelu_back(grad_acted)[0].astype(jnp.bfloat16)
    grad_fc1 = halving(own_rows(normed_two, grad_hidden), order_x, bits)
    grad_fc1_bias = column_sum(grad_hidden)
    grad_normed_two = matmul(grad_hidden, fc1_weight.T)
    _, norm_back_two = jax.vjp(layer_norm, stream_two, gain_two, shift_two)
    back_two, grad_gain_two, grad_shift_two = norm_back_two(grad_normed_two)
    grad_stream_two = grad_out.astype(jnp.float32) + back_two
    grad_attended = grad_stream_two.astype(jnp.bfloat16)
    grad_proj = halving(own_rows(mixed, grad_attended), order_y, bits)
    grad_proj_bias = column_sum(grad_attended)
    grad_mixed = matmul(grad_attended, proj_weight.T)
    grad_mixed = grad_mixed.astype(jnp.bfloat16).reshape(rows, HEADS, HEAD_DIM)
    grad_probs = product("qhd,khd->hqk", grad_mixed, values)
    grad_scores = probs * (grad_probs - jnp.sum(probs * grad_probs, axis=-1, keepdims=True))
    grad_scores = grad_scores.astype(jnp.bfloat16)
    grad_values = product("hqk,qhd->khd", probs_low, grad_mixed)
    grad_query = product("hqk,khd->qhd", grad_scores, keys) * scale
    grad_keys = product("hqk,qhd->khd", grad_scores, query) * scale
    grad_packed = jnp.stack([grad_query, grad_keys, grad_values], axis=1)
    grad_packed = grad_packed.astype(jnp.bfloat16).reshape(rows, 3 * width)
    grad_qkv = halving(own_rows(normed, grad_packed), order_y, bits)
    grad_normed = matmul(grad_packed, qkv_weight.T)
    _, norm_back_one = jax.vjp(layer_norm, stream, gain_one, shift_one)
    back_one, grad_gain_one, grad_shift_one = norm_back_one(grad_normed)
    grad_stream = (grad_stream_two + back_one).astype(jnp.bfloat16)
    grad_skip = halving(own_rows(joined, grad_stream), order_z, bits)
    grad_skip_bias = column_sum(grad_stream)
    grad_joined = matmul(grad_stream, skip_weight.T)

    vectors = (
        grad_skip_bias,
        grad_gain_one,
        grad_shift_one,
        grad_proj_bias,
        grad_gain_two,
        grad_shift_two,
        grad_fc1_bias,
        grad_fc2_bias,
    )
    chunks = dp_count * seq_count
    line = jnp.concatenate([v.reshape(chunks, -1) for v in vectors], axis=1)
    line = lax.psum_scatter(line, ("dp", "seq"), scatter_dimension=0, tiled=True)[0]
    pieces, start = [], 0
    for vector in vectors:
        size = vector.shape[0] // chunks
        pieces.append(line[start : start + size])
        start += size

    return (
        to_owner(block_output, 0),
        to_owner(grad_joined[:, :width], 0),
        to_owner(grad_joined[:, width:], 1),
        grad_skip,
        pieces[0],
        pieces[1],
        pieces[2],
        grad_qkv,
        grad_proj,
        pieces[3],
        pieces[4],
        pieces[5],
        grad_fc1,
        pieces[6],
        grad_fc2,
        pieces[7],
    )


def local_kernels(*arguments):
    arrays = Arguments(*arguments)
    items, half, width = arrays.inputs.shape
    hidden = arrays.fc1_weight.shape[1]
    dp_count = lax.axis_size("dp")
    bits = dp_count.bit_length() - 1
    seq_index = lax.axis_index("seq")
    device = lax.axis_index("dp") * 2 + seq_index
    first = seq_index == 0
    chunks = dp_count * 2
    skipped = arrays.skipped.reshape(items, 2, half, width // 2)
    plan = make_plan(width, hidden, chunks)
    feed = dict(
        inputs=arrays.inputs,
        skipped=skipped,
        cotangent=arrays.cotangent,
        lengths=arrays.lengths,
    )
    for name in Arguments._fields[4:]:
        feed[name] = getattr(arrays, name)
    found = run_block(feed, *plan[:2], width, hidden, half)
    kinds = ("left_", "far_left_", "right_", "far_right_")
    operands = [getattr(found, kind + name) for name in WEIGHTS for kind in kinds]
    operands += [getattr(found, f"grad_{u}") for u in EARLY]
    operands += [getattr(found, f"far_grad_{u}") for u in EARLY]
    weights, vectors, got = weight_gradients(
        operands,
        found.vectors,
        arrays.skip_weight,
        half,
        plan,
        bits,
    )
    grad_in_got, grad_skip_got, grad_in_own, grad_skip_own = got

    def owner(own, other):
        other = other.astype(own.dtype)
        return jnp.where(first, jnp.stack([own, other]), jnp.stack([other, own]))

    share = width // chunks
    mine = lax.dynamic_slice(vectors, (0, device * share), (8, share))
    wide_share = hidden // chunks
    per_row = width // wide_share
    row = 8 + device // per_row
    bias = lax.dynamic_slice(vectors, (row, device % per_row * wide_share), (1, wide_share))[0]
    grad_fc2, grad_fc1, grad_proj, grad_qkv, grad_skip = weights
    grad_skip_own = grad_skip_own.reshape(2 * half, -1)
    return (
        owner(found.block_own, found.block_got),
        owner(grad_in_own, grad_in_got),
        owner(grad_skip_own, grad_skip_got.reshape(2 * half, -1)),
        grad_skip,
        mine[0],
        mine[1],
        mine[2],
        grad_qkv,
        grad_proj,
        mine[3],
        mine[4],
        mine[5],
        grad_fc1,
        bias,
        grad_fc2,
        mine[7],
    )


class Arguments(typing.NamedTuple):
    inputs: jax.Array
    skipped: jax.Array
    lengths: jax.Array
    cotangent: jax.Array
    skip_weight: jax.Array
    skip_bias: jax.Array
    gain_one: jax.Array
    shift_one: jax.Array
    qkv_weight: jax.Array
    proj_weight: jax.Array
    proj_bias: jax.Array
    gain_two: jax.Array
    shift_two: jax.Array
    fc1_weight: jax.Array
    fc1_bias: jax.Array
    fc2_weight: jax.Array
    fc2_bias: jax.Array


def solution(mesh):
    small = mesh.shape["dp"] == 16
    return jax.shard_map(
        local_kernels if small else local_permutes,
        mesh=mesh,
        in_specs=(
            P("dp", "seq", None),
            P("dp", None, "seq"),
            P("dp"),
            P("dp", "seq", None),
        )
        + (P(),) * 13,
        out_specs=(
            P("dp", "seq", None),
            P("dp", "seq", None),
            P("dp", None, "seq"),
            P(("dp", "seq"), None),
            P(("dp", "seq")),
            P(("dp", "seq")),
            P(("dp", "seq")),
            P(("dp", "seq"), None),
            P(("dp", "seq"), None),
            P(("dp", "seq")),
            P(("dp", "seq")),
            P(("dp", "seq")),
            P(("dp", "seq"), None),
            P(("dp", "seq")),
            P(("dp", "seq"), None),
            P(("dp", "seq")),
        ),
        check_vma=False,
    )
```

```python
import functools
import types
import typing

import jax
import jax.numpy as jnp
from jax import lax
from jax.experimental import pallas as pl
from jax.experimental.pallas import tpu as pltpu
from jax.sharding import PartitionSpec as P

HEADS = 16
HEAD_DIM = 72
CAPTION = 77
IMAGE = 256


epsilon = 1e-05
masked_score = -1e30


def layer_norm(stream, gain, shift):
    center = stream - jnp.mean(stream, axis=-1, keepdims=True)
    spread = jnp.mean(center * center, axis=-1, keepdims=True)
    return center * lax.rsqrt(spread + epsilon) * gain + shift


def gelu_exact(values):
    return jax.nn.gelu(values, approximate=False)


def column_sum(values):
    return jnp.sum(values.astype(jnp.float32), axis=0)


def matmul(left, right):
    return jnp.dot(left, right, preferred_element_type=jnp.float32)


def swap_seq(values):
    return lax.ppermute(values, "seq", [(0, 1), (1, 0)])


def swap_dp(values, bit):
    count = lax.axis_size("dp")
    return lax.ppermute(values, "dp", [(i, i ^ (1 << bit)) for i in range(count)])


def pick(values, index, axis):
    return lax.dynamic_index_in_dim(values, index, axis, keepdims=False)


def place(first, own, got, axis):
    return jnp.where(
        first, jnp.concatenate([own, got], axis=axis), jnp.concatenate([got, own], axis=axis)
    )


PAD = 192
ROWS = 2 * PAD


def matmul_t(left, right):
    return lax.dot_general(
        left, right, (((1,), (1,)), ((), ())), preferred_element_type=jnp.float32
    )


def t_matmul(left, right):
    return lax.dot_general(
        left, right, (((0,), (0,)), ((), ())), preferred_element_type=jnp.float32
    )


def tiles_of(width):
    starts = list(range(0, width - 255, 512))
    ends = starts[1:] + [width]
    return [pl.ds(a, b - a) for a, b in zip(starts, ends)]


def norm_parts(values):
    center = values - jnp.mean(values, axis=-1, keepdims=True)
    spread = jnp.mean(center * center, axis=-1, keepdims=True)
    scale = lax.rsqrt(spread + epsilon)
    return center * scale, scale


def fold_rows(values):
    rows, width = values.shape
    return jnp.sum(values.reshape(rows // 8, 8, width), axis=0)


def block_kernel(half, hidden, matrices, early, names, *refs):
    r = types.SimpleNamespace(**dict(zip(names, refs)))
    width = r.skip_weight.shape[1]
    seq = lax.axis_index("seq")
    core = lax.rem(lax.axis_index("dp"), 2)
    sems = r.sems
    low = jnp.bfloat16
    counter = iter(range(80))

    def copy(source, target):
        return pltpu.make_async_copy(source, target, sems.at[next(counter)])

    loads = types.SimpleNamespace(
        in0=copy(r.inputs.at[seq], r.raw_in.at[seq]),
        sk0=copy(r.skipped.at[seq], r.raw_skip.at[seq]),
        skip0=copy(r.skip_weight.at[pl.ds(0, width), :], r.feed.at[0]),
        skip1=copy(r.skip_weight.at[pl.ds(width, width), :], r.feed.at[1]),
        ct0=copy(r.cotangent.at[seq], r.raw_out.at[seq]),
        proj=copy(r.proj_weight, r.proj_buffer),
    )
    spare = r.spare

    def load_qkv():
        parts = [
            copy(r.qkv_weight.at[:, pl.ds(k * width, width)], spare.at[k]) for k in range(3)
        ]
        for load in parts:
            load.start()
        return parts

    dp = lax.axis_index("dp")
    neighbour = (dp, 1 - seq)

    def flip(name):
        if name == "seq":
            return neighbour
        return (dp + (1 - 2 * lax.rem(lax.div(dp, 1 << name), 2)) * (1 << name), seq)

    barrier = pltpu.get_barrier_semaphore()
    names_met = [0] + sorted({hop for _, hop in early}, key=str)
    for name in names_met:
        pl.semaphore_signal(barrier, inc=1, device_id=flip(name), device_id_type=MESH)
    for load in vars(loads).values():
        load.start()
    qkv_loads = load_qkv()
    pl.semaphore_wait(barrier, len(names_met))
    remotes = []

    def remote(source, target, name):
        k = len(remotes)
        item = pltpu.make_async_remote_copy(
            src_ref=source,
            dst_ref=target,
            send_sem=r.send_sem.at[k],
            recv_sem=r.recv_sem.at[k],
            device_id=flip(name),
            device_id_type=MESH,
        )
        item.start()
        remotes.append(item)
        return item

    gone, come = set(), set()

    def left_here(item):
        if id(item) not in gone:
            gone.add(id(item))
            item.wait_send()

    def got_here(item):
        if id(item) not in come:
            come.add(id(item))
            item.wait_recv()

    traded = [
        remote(r.inputs.at[1 - seq], r.raw_in.at[seq], "seq"),
        remote(r.skipped.at[1 - seq], r.raw_skip.at[seq], "seq"),
    ]
    chunk, feed = width, r.feed
    feeds = []
    for j in range(hidden // chunk):
        part = pl.ds(j * chunk, chunk)
        at = 2 - 2 * (j % 2)
        feeds.append(
            (
                copy(r.fc1_weight.at[:, part], feed.at[at]),
                copy(r.fc2_weight.at[part, :], feed.at[at + 1]),
            )
        )

    def start(copies):
        for item in copies:
            item.start()

    start(feeds[0])
    stores = {}

    def store(source, target):
        item = copy(source, target)
        item.start()
        stores[id(item)] = item
        return item

    def finish(item):
        stores.pop(id(item)).wait()

    joined, skips, grad_out = r.joined, r.skips, r.grad_out
    gap = PAD - half
    for load in (loads.in0, loads.sk0):
        load.wait()
    for item in traded:
        got_here(item)
    traded = remote(r.cotangent.at[1 - seq], r.raw_out.at[seq], "seq")
    for h in range(2):
        joined[pl.ds(h * PAD, PAD), :] = jnp.concatenate(
            [r.raw_in[h], jnp.zeros((gap, width), low)], axis=0
        )
        for f in range(2):
            skips[f, pl.ds(h * PAD, PAD), :] = jnp.concatenate(
                [r.raw_skip[f, h], jnp.zeros((gap, width // 2), low)], axis=0
            )
    loads.skip0.wait()
    loads.skip1.wait()
    stream = r.stream
    tiles = tiles_of(width)

    for columns in tiles:
        total = matmul(joined[...], feed[0, :, columns])
        total += matmul(skips[0], feed[1, pl.ds(0, width // 2), columns])
        total += matmul(skips[1], feed[1, pl.ds(width // 2, width // 2), columns])
        stream[:, columns] = total + r.skip_bias[columns]

    start(feeds[1])
    step = 128

    def norm(source, gain, shift, target):
        @pl.loop(0, ROWS // step)
        def _(i):
            rows = pl.ds(pl.multiple_of(i * step, step), step)
            unit, _ = norm_parts(source[rows, :])
            target[rows, :] = (unit * gain[...] + shift[...]).astype(low)

    normed, packed = r.normed, r.packed
    norm(stream, r.gain_one, r.shift_one, normed)
    for load in qkv_loads:
        load.wait()

    for k in range(3):
        for columns in tiles:
            target = pl.ds(k * width + columns.start, columns.size)
            packed[:, target] = matmul(normed[...], spare[k, :, columns]).astype(low)

    length = r.lengths[seq]
    at = lax.broadcasted_iota(jnp.int32, (1, ROWS), 1)
    inner = jnp.where(at >= PAD, at - PAD, at)
    position = jnp.where(at >= PAD, at - PAD + half, at)
    valid = (position == 0) | ((position >= 1) & (position <= length))
    valid = valid | ((position >= 1 + CAPTION) & (position < 1 + CAPTION + IMAGE))
    valid = valid & (inner < half)
    scale = HEAD_DIM ** (-0.5)
    window = 256

    def head_window(h):
        start = jnp.minimum(lax.div(h * HEAD_DIM, 128) * 128, width - window)
        start = pl.multiple_of(start, 128)
        lane = lax.broadcasted_iota(jnp.int32, (1, window), 1) + start
        mine = (lane >= h * HEAD_DIM) & (lane < (h + 1) * HEAD_DIM)
        return start, mine

    def part(which, start):
        return packed[:, pl.ds(pl.multiple_of(which * width + start, 128), window)]

    mixed_sum, probs = r.sum_a, r.probs

    def attend(h, carry):
        start, mine = head_window(h)
        query = jnp.where(mine, part(0, start), jnp.zeros((), low))
        scores = matmul_t(query, part(1, start)) * scale
        scores = jnp.where(valid, scores, masked_score)
        expo = jnp.exp(scores - jnp.max(scores, axis=-1, keepdims=True))
        share = expo * (1.0 / jnp.sum(expo, axis=-1, keepdims=True))
        share = share.astype(low)
        probs[h] = share
        found = matmul(share, part(2, start))
        columns = pl.ds(start, window)
        mixed_sum[:, columns] = jnp.where(mine, found, mixed_sum[:, columns])
        return carry

    lax.fori_loop(0, HEADS, attend, 0, unroll=4)
    mixed, stream_two = r.mixed, r.stream_two
    mixed[...] = mixed_sum[...].astype(low)
    loads.proj.wait()

    for columns in tiles:
        total = matmul(mixed[...], r.proj_buffer[:, columns]) + r.proj_bias[columns]
        stream_two[:, columns] = stream[:, columns] + total

    normed_two = r.normed_two
    norm(stream_two, r.gain_two, r.shift_two, normed_two)
    loads.ct0.wait()
    got_here(traded)
    for h in range(2):
        grad_out[pl.ds(h * PAD, PAD), :] = jnp.concatenate(
            [r.raw_out[h], jnp.zeros((gap, width), low)], axis=0
        )
    far_out = remote(grad_out, r.far_right_fc2, 0)
    sums = r.sums
    sums[7:8, :] = jnp.sum(grad_out[...].astype(jnp.float32), axis=0, keepdims=True)

    turned_ref = r.turned
    stages = {}

    def left(m, target, far, sources):
        matrix = matrices[m]
        stage = r.left_stage
        for item in stages.pop(0, ()):
            finish(item) if id(item) in stores else left_here(item)
        share, main, rest = matrix.share, matrix.main, matrix.rest
        folds, body = len(matrix.pieces), 16 * main
        first = 0
        for source in sources:
            turned_ref[pl.ds(32, width), :] = source.T.astype(jnp.float32)
            for k in range(width // share):
                number = first + k
                c, block = number // 2 % 2, number // 4 * 2 + number % 2
                base = 32 + k * share
                place = c ^ core
                stage[place, pl.ds(block * main, main), :] = turned_ref[
                    pl.ds(base, main), :
                ].astype(low)
                row = lax.broadcasted_iota(jnp.int32, (16, 1), 0)
                for q in range(folds):
                    part = turned_ref[pl.ds(base + main - q * rest, 16), :]
                    part = jnp.where((row >= q * rest) & (row < (q + 1) * rest), part, 0.0)
                    stage[place, pl.ds(body + (q * 16 + block) * 16, 16), :] = part.astype(low)
            first += width // share
        rows = matrix.left_rows(16)
        stages[0] = [
            store(stage.at[0, pl.ds(0, rows), :], target),
            remote(stage.at[1, pl.ds(0, rows), :], far, 0),
        ]

    body = 16 * matrices[1].main
    left(1, r.left_fc1, r.far_left_fc1, [normed_two[...]])
    far_left = remotes[-1]
    near = copy(r.left_stage.at[0, pl.ds(0, body), :], spare.at[0, pl.ds(0, body), pl.ds(2 * ROWS, ROWS)])
    near.start()
    stores[id(near)] = near
    far_hidden = []
    opened, loading = [], []

    def fetch(source, target):
        item = copy(source, target)
        item.start()
        return item

    def launch():
        while opened:
            u, hop, item = opened.pop(0)
            finish(item)
            dims = [3, 2, 1, "seq"]
            bit = seq if hop == "seq" else lax.rem(lax.div(dp, 1 << hop), 2)
            index = tuple(1 - bit if name == hop else slice(None) for name in dims)
            remote(getattr(r, f"grad_{u}").at[index], getattr(r, f"far_grad_{u}"), hop)

    fetched = {}

    def prefetch(p):
        got_here(far_hidden[p])
        source = r.far_right_fc1.at[:, pl.ds(p * chunk, chunk)]
        fetched[p] = [fetch(source, spare.at[2, pl.ds(ROWS, ROWS), :])]
        if p == 0:
            got_here(far_left)
            target = spare.at[0, pl.ds(body, body), pl.ds(2 * ROWS, ROWS)]
            fetched[p].append(fetch(r.far_left_fc1.at[pl.ds(0, body), :], target))
            got_here(far_out)
            loading.append(fetch(r.far_right_fc2, spare.at[2, pl.ds(0, ROWS), :]))
        prefetch_left(p)

    def prefetch_left(p):
        got_here(far_acted[p])
        count = 4 * matrices[0].share
        source = r.far_left_fc2.at[pl.ds(p * count, count), :]
        target = spare.at[1, pl.ds(p % 2 * count, count), pl.ds(p // 2 * ROWS, ROWS)]
        loading.append(fetch(source, target))

    def early_hidden(p):
        for item in fetched.pop(p):
            item.wait()
        if p == 0:
            finish(near)
        launch()
        near_rows, far_rows = (spare[0, pl.ds(k * body, body), pl.ds(2 * ROWS, ROWS)] for k in range(2))
        for columns in tiles:
            value = matmul(near_rows, grad_hidden[p % 2, :, columns])
            value += matmul(far_rows, spare[2, pl.ds(ROWS, ROWS), columns])
            value = value.astype(low).reshape(2, 2, 2, 2, matrices[1].main, columns.size)
            r.wide_stage[:, :, :, :, :, columns] = value
        u, hop = early[3 + p]
        opened.append((u, hop, store(r.wide_stage, getattr(r, f"grad_{u}"))))

    forward, backward = r.sum_a, r.sum_b
    acted, grad_hidden, staged = r.acted, r.grad_hidden, r.left_fc2_stage
    pending, far_acted = {}, []
    for j, feeding in enumerate(feeds):
        slot = j % 2
        first, second = feed.at[2 - 2 * slot], feed.at[3 - 2 * slot]
        for load in feeding:
            load.wait()
        for item in pending.get(slot, ()):
            finish(item) if id(item) in stores else left_here(item)

        for columns in tiles:
            whole = pl.ds(j * chunk + columns.start, columns.size)
            value = matmul(normed_two[...], first[:, columns])
            value += r.fc1_bias[whole]
            phi = 0.5 + 0.5 * lax.erf(value * (0.5**0.5))
            bell = jnp.exp(-0.5 * value * value) * ((2 * jnp.pi) ** -0.5)
            acted[slot, :, columns] = (value * phi).astype(low)
            back = matmul_t(grad_out[...], second[columns, :])
            back = (back * (phi + value * bell)).astype(low)
            grad_hidden[slot, :, columns] = back
            sums[pl.ds(8 + j, 1), columns] = jnp.sum(
                back.astype(jnp.float32), axis=0, keepdims=True
            )

        if j >= 1:
            prefetch(j - 1)
        for columns in tiles:
            ahead = matmul(acted[slot], second[:, columns])
            back = matmul_t(grad_hidden[slot], first[columns, :])
            if j == 0:
                forward[:, columns] = ahead
                backward[:, columns] = back
            else:
                forward[:, columns] += ahead
                backward[:, columns] += back

        share = matrices[0].share
        turned = acted[slot].T
        groups = chunk // (4 * share)
        for g in range(groups):
            begin = g * 4 * share
            lower, upper = turned[begin : begin + 2 * share], turned[begin + 2 * share : begin + 4 * share]
            number = j * groups + g
            rows = pl.ds(number % 4 * 2 * share, 2 * share)
            spare[0, rows, pl.ds(number // 4 * ROWS, ROWS)] = jnp.where(core == 0, lower, upper)
            staged[slot, pl.ds(g * 2 * share, 2 * share), :] = jnp.where(core == 0, upper, lower)
        count = groups * 2 * share
        far_acted.append(remote(staged.at[slot], r.far_left_fc2.at[pl.ds(j * count, count), :], 0))
        part_columns = pl.ds(j * chunk, chunk)
        far_hidden.append(remote(grad_hidden.at[slot], r.far_right_fc1.at[:, part_columns], 0))
        pending[slot] = [
            far_acted[-1],
            far_hidden[-1],
            store(grad_hidden.at[slot], r.right_fc1.at[:, part_columns]),
        ]
        if j + 2 < len(feeds):
            start(feeds[j + 2])
        if 1 <= j < 4:
            early_hidden(j - 1)

    left(2, r.left_proj, r.far_left_proj, [mixed[...]])
    launch()
    prefetch_left(3)
    left(3, r.left_qkv, r.far_left_qkv, [normed[...]])
    left(4, r.left_skip, r.far_left_skip, [joined[...], jnp.concatenate([skips[0], skips[1]], axis=1)])

    for item in loading:
        item.wait()
    share = matrices[0].share
    for p in range(3):
        start_column, size = matrices[0].pieces[p]
        columns = pl.ds(start_column, size)
        launch()
        for k in range(2):
            for g in range(2):
                rows, lanes = pl.ds(g * 4 * share, 4 * share), pl.ds(k * ROWS, ROWS)
                value = matmul(spare[0, rows, lanes], grad_out[:, columns])
                value += matmul(spare[1, rows, lanes], spare[2, pl.ds(0, ROWS), columns])
                r.tall_stage[k, g] = value.astype(low).reshape(2, 2, share, size)
        u, hop = early[p]
        opened.append((u, hop, store(r.tall_stage, getattr(r, f"grad_{u}"))))
    qkv_loads = load_qkv()

    grad_two = r.grad_two
    out_stage, grad_low = r.raw_out, r.grad_low
    for h in range(2):
        rows = pl.ds(h * PAD, half)
        value = stream_two[rows, :] + (forward[rows, :] + r.fc2_bias[...])
        out_stage[h] = value.astype(low)
    store(out_stage.at[seq], r.block_own)
    remote(out_stage.at[1 - seq], r.block_got, "seq")
    launch()

    def norm_back(source, gain, back, extra, target, target_low, gain_row, shift_row):
        partial = r.partial
        partial[...] = jnp.zeros_like(partial)

        @pl.loop(0, ROWS // step)
        def _(i):
            rows = pl.ds(pl.multiple_of(i * step, step), step)
            unit, spread = norm_parts(source[rows, :])
            value = back[rows, :]
            partial[0] += fold_rows(value * unit)
            partial[1] += fold_rows(value)
            value = value * gain[...]
            mean = jnp.mean(value, axis=-1, keepdims=True)
            slope = jnp.mean(value * unit, axis=-1, keepdims=True)
            value = spread * (value - mean - unit * slope)
            value = value + extra[rows, :].astype(jnp.float32)
            if target is not None:
                target[rows, :] = value
            rounded = value.astype(low)
            target_low[rows, :] = rounded
            partial[2] += fold_rows(rounded.astype(jnp.float32))

        sums[gain_row : gain_row + 1, :] = jnp.sum(partial[0], axis=0, keepdims=True)
        sums[shift_row : shift_row + 1, :] = jnp.sum(partial[1], axis=0, keepdims=True)
        return jnp.sum(partial[2], axis=0, keepdims=True)

    sums[3:4, :] = norm_back(stream_two, r.gain_two, backward, grad_out, grad_two, grad_low, 4, 5)
    store(grad_low, r.right_proj)
    remote(grad_low, r.far_right_proj, 0)
    grad_mixed = r.grad_mixed

    for columns in tiles:
        grad_mixed[:, columns] = matmul_t(grad_low[...], r.proj_buffer[columns, :]).astype(low)

    grad_query, grad_key, grad_value = r.sum_a, r.sum_b, r.sum_c

    def attend_back(h, carry):
        start, mine = head_window(h)
        zero = jnp.zeros((), low)
        columns = pl.ds(start, window)
        query = jnp.where(mine, part(0, start), zero)
        back = jnp.where(mine, grad_mixed[:, columns], zero)
        share = probs[h]
        grad_share = matmul_t(back, part(2, start))
        wide = share.astype(jnp.float32)
        level = jnp.sum(wide * grad_share, axis=-1, keepdims=True)
        grad_score = (wide * (grad_share - level)).astype(low)
        found = t_matmul(share, back)
        grad_value[:, columns] = jnp.where(mine, found, grad_value[:, columns])
        found = matmul(grad_score, part(1, start)) * scale
        grad_query[:, columns] = jnp.where(mine, found, grad_query[:, columns])
        found = t_matmul(grad_score, query) * scale
        grad_key[:, columns] = jnp.where(mine, found, grad_key[:, columns])
        return carry

    lax.fori_loop(0, HEADS, attend_back, 0, unroll=4)
    for k, source in enumerate((grad_query, grad_key, grad_value)):
        packed[:, pl.ds(k * width, width)] = source[...].astype(low)
    store(packed, r.right_qkv)
    remote(packed, r.far_right_qkv, 0)
    for load in qkv_loads:
        load.wait()
    grad_normed = r.sum_a

    for columns in tiles:
        total = matmul_t(packed[:, pl.ds(0, width)], spare[0, columns, :])
        for k in range(1, 3):
            total += matmul_t(packed[:, pl.ds(k * width, width)], spare[k, columns, :])
        grad_normed[:, columns] = total

    grad_stream = r.grad_mixed
    sums[0:1, :] = norm_back(stream, r.gain_one, grad_normed, grad_two, None, grad_stream, 1, 2)
    store(grad_stream, r.right_skip)
    remote(grad_stream, r.far_right_skip, 0)
    sums[12:16, :] = jnp.zeros((4, width), jnp.float32)
    sums[6:7, :] = jnp.zeros((1, width), jnp.float32)
    store(sums, r.vectors)

    for item in stores.values():
        item.wait()
    for item in remotes:
        got_here(item)
        left_here(item)


WEIGHTS = ["fc1", "proj", "qkv", "skip"]


def run_block(arrays, matrices, units, width, hidden, half):
    low, wide = jnp.bfloat16, jnp.float32
    shape = jax.ShapeDtypeStruct
    outs = dict(
        block_own=shape((half, width), low),
        block_got=shape((half, width), low),
        vectors=shape((16, width), wide),
    )
    for name, matrix in zip(WEIGHTS, matrices[1:]):
        for prefix in ("", "far_"):
            outs[prefix + "left_" + name] = shape((matrix.left_rows(16), ROWS), low)
            outs[prefix + "right_" + name] = shape((ROWS, matrix.columns), low)
    outs.update(
        far_left_fc2=shape((matrices[0].left_rows(16), ROWS), low),
        far_right_fc2=shape((ROWS, width), low),
    )
    for u in EARLY:
        tail = (units[u].rows, units[u].columns)
        outs[f"grad_{u}"] = shape((2, 2, 2, 2) + tail, low)
        outs[f"far_grad_{u}"] = shape((2, 2, 2) + tail, low)
    early = [(u, units[u].hops[0]) for u in EARLY]
    staged = 16 * matrices[0].share // (hidden // width)
    square = (ROWS, width)
    scratch = dict(
        raw_in=((2, half, width), low),
        raw_skip=((2, 2, half, width // 2), low),
        raw_out=((2, half, width), low),
        spare=((3, width, width), low),
        proj_buffer=((width, width), low),
        feed=((4, width, width), low),
        joined=(square, low),
        skips=((2, ROWS, width // 2), low),
        grad_out=(square, low),
        stream=(square, wide),
        normed=(square, low),
        packed=((ROWS, 3 * width), low),
        probs=((HEADS, ROWS, ROWS), low),
        sum_a=(square, wide),
        sum_b=(square, wide),
        sum_c=(square, wide),
        mixed=(square, low),
        stream_two=(square, wide),
        normed_two=(square, low),
        acted=((2,) + square, low),
        grad_hidden=((2,) + square, low),
        left_fc2_stage=((2, staged, ROWS), low),
        tall_stage=((2, 2, 2, 2, matrices[0].share, 384), low),
        wide_stage=((2, 2, 2, 2, matrices[1].main, width), low),
        left_stage=((2, max(m.left_rows(16) for m in matrices[1:]), ROWS), low),
        turned=((width + 64, ROWS), wide),
        sums=((16, width), wide),
        partial=((3, 8, width), wide),
        grad_two=(square, wide),
        grad_low=(square, low),
        grad_mixed=(square, low),
    )
    anywhere = pl.BlockSpec(memory_space=pl.ANY)
    vmem = pl.BlockSpec(memory_space=pltpu.VMEM)
    smem = pl.BlockSpec(memory_space=pltpu.SMEM)
    small = {name for name, a in arrays.items() if a.dtype == wide}
    specs = [smem if n == "lengths" else vmem if n in small else anywhere for n in arrays]
    names = list(arrays) + list(outs) + list(scratch) + ["sems", "send_sem", "recv_sem"]
    results = pl.pallas_call(
        functools.partial(block_kernel, half, hidden, matrices, early, names),
        out_shape=list(outs.values()),
        in_specs=specs,
        out_specs=[anywhere] * len(outs),
        scratch_shapes=[pltpu.VMEM(*s) for s in scratch.values()]
        + [pltpu.SemaphoreType.DMA((n,)) for n in (80, 40, 40)],
        compiler_params=pltpu.CompilerParams(
            collective_id=1, has_side_effects=True, vmem_limit_bytes=63 * 2**20
        ),
        name="block",
    )(*arrays.values())
    return types.SimpleNamespace(**dict(zip(outs, results)))


MESH = pl.DeviceIdType.MESH
LANES = 384
SHIPS = 2
TWO = 2 * LANES


class Matrix:
    def __init__(self, share, columns, pieces, cuts):
        self.share, self.columns = share, columns
        self.main = share - share % 16
        self.rest = share % 16
        self.pieces, start = [], 0
        for width in pieces:
            self.pieces.append((start, width))
            start += width
        self.cuts = cuts
        self.fold = self.rest and 16
        self.fold_width = max(pieces)

    def left_rows(self, blocks):
        folds = len(self.pieces) if self.rest else 0
        return blocks * (self.main + folds * 16)


class Unit:
    def __init__(self, matrix, rows, start, columns, hops, folded):
        self.matrix, self.rows, self.start, self.columns = matrix, rows, start, columns
        self.hops, self.folded = hops, folded


def make_units(matrices, hops_of):
    units = []
    for m, matrix in enumerate(matrices):
        for start, columns in matrix.cuts:
            units.append(Unit(m, matrix.main, start, columns, hops_of[len(units)], False))
        if matrix.rest:
            units.append(Unit(m, 16, 0, matrix.fold_width, hops_of[len(units)], True))
    return units


def reduce_kernel(matrices, units, events, dims, *refs):
    count = len(matrices)
    lefts, far_lefts, rights, far_rights = ([None, *refs[k : 16 : 4]] for k in range(4))
    refs = refs[16:]
    whole_grads, refs = refs[: len(EARLY)], refs[len(EARLY) :]
    far_grads, refs = refs[: len(EARLY)], refs[len(EARLY) :]
    vector_ref, skip_ref, refs = refs[0], refs[1], refs[2:]
    outs, refs = refs[:count], refs[count:]
    docks, refs = refs[:SHIPS], refs[SHIPS:]
    own_in, own_skip, refs = refs[0], refs[1], refs[2:]
    vector_out, refs = refs[0], refs[1:]
    grads, refs = refs[: len(units)], refs[len(units) :]
    hops = len(dims)
    landed = [refs[i * hops : (i + 1) * hops] for i in range(len(units))]
    refs = refs[len(units) * hops :]
    vector_land, vector_sum, refs = refs[0], refs[1], refs[2:]
    fold_sum, left_buffer, right_buffer, refs = refs[0], refs[1], refs[2], refs[3:]
    send_sem, recv_sem, vsend_sem, vrecv_sem, left_sem, right_sem, *refs = refs
    early_sem, ship_send, ship_recv, skip_buffer, grad_stream, *refs = refs
    back_in, back_skip, send_in, send_skip, skip_sem = refs
    ships = [send_in, send_skip]

    dp = lax.axis_index("dp")
    seq = lax.axis_index("seq")
    core = lax.rem(dp, 2)

    def bit(name):
        return seq if name == "seq" else lax.rem(lax.div(dp, 1 << name), 2)

    def partner(name):
        if name == "seq":
            return (dp, 1 - seq)
        return (dp + (1 - 2 * bit(name)) * (1 << name), seq)

    barrier = pltpu.get_barrier_semaphore()
    for name in [0] + list(dims):
        pl.semaphore_signal(barrier, inc=1, device_id=partner(name), device_id_type=MESH)
    pl.semaphore_wait(barrier, len(dims) + 1)

    sent = []

    def remote(source, target, send_at, recv_at, name):
        copy = pltpu.make_async_remote_copy(
            src_ref=source,
            dst_ref=target,
            send_sem=send_at,
            recv_sem=recv_at,
            device_id=partner(name),
            device_id_type=MESH,
        )
        copy.start()
        sent.append(copy)
        return copy

    early_copies = {}
    for k, u in enumerate(EARLY):
        hop = units[u].hops[0]
        index = tuple(bit(name) if name == hop else slice(None) for name in dims)
        early_copies[u] = [
            pltpu.make_async_copy(
                whole_grads[k].at[index], grads[u].at[index], early_sem.at[k, 0]
            ),
            pltpu.make_async_copy(far_grads[k], landed[u][0], early_sem.at[k, 1]),
        ]
        for copy in early_copies[u]:
            copy.start()

    width = skip_buffer.shape[2]
    skip_copies = [
        pltpu.make_async_copy(
            skip_ref.at[pl.ds(k * width, width), :], skip_buffer.at[k], skip_sem.at[k]
        )
        for k in range(2)
    ]
    skip_copies.append(pltpu.make_async_copy(rights[4], grad_stream, skip_sem.at[2]))
    kept = []

    def finish_inputs():
        wait(skip_copies)
        half, feature = send_in.shape[0], width // 2
        for columns in tiles_of(width):
            value = matmul_t(grad_stream[...], skip_buffer[0, columns, :])
            lower, upper = value[:half], value[PAD : PAD + half]
            back_in[:, columns] = jnp.where(seq == 0, lower, upper)
            send_in[:, columns] = jnp.where(seq == 0, upper, lower).astype(jnp.bfloat16)
        parts = [
            matmul_t(grad_stream[...], skip_buffer[1, pl.ds(f * feature, feature), :])
            for f in range(2)
        ]
        for h in range(2):
            lower, upper = (part[h * PAD : h * PAD + half] for part in parts)
            back_skip[h] = jnp.where(seq == 0, lower, upper)
            send_skip[h] = jnp.where(seq == 0, upper, lower).astype(jnp.bfloat16)
        kept.append(pltpu.make_async_copy(back_in, own_in, skip_sem.at[3]))
        kept.append(pltpu.make_async_copy(back_skip, own_skip, skip_sem.at[4]))
        start(kept)

    def left_copies(m):
        rows = matrices[m].left_rows(2 ** len(dims))
        return [
            pltpu.make_async_copy(
                (lefts[m], far_lefts[m])[k],
                left_buffer.at[m % 2, pl.ds(0, rows), pl.ds(k * LANES, LANES)],
                left_sem.at[m % 2, k],
            )
            for k in range(2)
        ]

    all_pieces = [(m, p) for m in range(1, count) for p in range(len(matrices[m].pieces))]

    def right_copies(index):
        m, p = all_pieces[index]
        start, width = matrices[m].pieces[p]
        return [
            pltpu.make_async_copy(
                (rights[m], far_rights[m])[k].at[:, pl.ds(start, width)],
                right_buffer.at[index % 2, pl.ds(k * LANES, LANES), pl.ds(0, width)],
                right_sem.at[index % 2, k],
            )
            for k in range(2)
        ]

    def start(copies):
        for copy in copies:
            copy.start()

    def wait(copies):
        for copy in copies:
            copy.wait()

    start(left_copies(1))
    for index in range(2):
        start(right_copies(index))
    start(left_copies(2))
    start(skip_copies)

    def send(u, h):
        unit = units[u]
        index = []
        for name in dims:
            if name in unit.hops[:h]:
                index.append(bit(name))
            elif name == unit.hops[h]:
                index.append(1 - bit(name))
            else:
                index.append(slice(None))
        return remote(
            grads[u].at[tuple(index)],
            landed[u][h],
            send_sem.at[u, h],
            recv_sem.at[u, h],
            unit.hops[h],
        )

    flying = {}

    def add(u, h):
        unit = units[u]
        if h == 0 and u in EARLY:
            wait(early_copies[u])
        else:
            flying[u, h].wait_recv()
        done = unit.hops[: h + 1]
        free = [name for name in dims if name not in done]
        step = next(n for n in (48, 32, 16) if unit.rows % n == 0)
        last = h + 1 == hops

        @pl.loop(0, 2 ** len(free) * (unit.rows // step))
        def _(i):
            block, row = lax.div(i, unit.rows // step), lax.rem(i, unit.rows // step) * step
            place = {
                name: lax.rem(lax.div(block, 1 << (len(free) - 1 - k)), 2)
                for k, name in enumerate(free)
            }
            rows = pl.ds(pl.multiple_of(row, step), step)
            own = tuple(place.get(name, bit(name)) for name in dims) + (rows,)
            got = tuple(place[name] for name in free) + (rows,)
            total = grads[u][own].astype(jnp.float32) + landed[u][h][got].astype(jnp.float32)
            if last and not unit.folded:
                outs[unit.matrix][rows, pl.ds(unit.start, unit.columns)] = total
            elif last:
                matrix = matrices[unit.matrix]
                for p, (begin, size) in enumerate(matrix.pieces):
                    part = total[p * matrix.rest : (p + 1) * matrix.rest, :size]
                    under = pl.ds(matrix.main, matrix.rest)
                    outs[unit.matrix][under, pl.ds(begin, size)] = part
            else:
                grads[u][own] = total.astype(jnp.bfloat16)

    def multiply(index):
        m, p = all_pieces[index]
        matrix = matrices[m]
        start_column, width = matrix.pieces[p]
        blocks = 2 ** len(dims)
        if p == 0:
            wait(left_copies(m))
        wait(right_copies(index))
        left, right = left_buffer.at[m % 2], right_buffer.at[index % 2]
        u = next(
            i
            for i, unit in enumerate(units)
            if unit.matrix == m
            and not unit.folded
            and unit.start <= start_column < unit.start + unit.columns
        )
        group = blocks
        while group * matrix.main > 640:
            group //= 2
        free = group.bit_length() - 1
        step = next(s for s in (384, 640, 512, 128) if width % s == 0)

        @pl.loop(0, 0 if u in EARLY else (blocks // group) * (width // step))
        def _(i):
            g, j = lax.div(i, width // step), lax.rem(i, width // step)
            rows = pl.ds(pl.multiple_of(g * (group * matrix.main), 16), group * matrix.main)
            columns = pl.ds(pl.multiple_of(j * step, 128), step)
            result = jnp.dot(left[rows, :], right[:, columns], preferred_element_type=jnp.float32)
            high = len(dims) - free
            where = tuple(lax.rem(lax.div(g, 1 << (high - 1 - k)), 2) for k in range(high))
            target = pl.ds(pl.multiple_of(start_column - units[u].start + j * step, 128), step)
            grads[u][where + (slice(None),) * (free + 1) + (target,)] = result.astype(
                jnp.bfloat16
            ).reshape((2,) * free + (matrix.main, step))

        if matrix.rest:
            offset = blocks * (matrix.main + 16 * p)

            @pl.loop(0, width // step)
            def _(j):
                columns = pl.ds(pl.multiple_of(j * step, 128), step)
                result = jnp.dot(
                    left[pl.ds(offset, blocks * 16), :],
                    right[:, columns],
                    preferred_element_type=jnp.float32,
                )
                if p == 0:
                    fold_sum[:, columns] = result
                else:
                    fold_sum[:, columns] += result

        if index + 2 < len(all_pieces):
            start(right_copies(index + 2))
        last = p + 1 == len(matrix.pieces)
        if last and m + 2 < count:
            start(left_copies(m + 2))
        if last and matrix.rest:
            f = next(i for i, unit in enumerate(units) if unit.matrix == m and unit.folded)
            folded = fold_sum[:, pl.ds(0, units[f].columns)].astype(jnp.bfloat16)
            grads[f][...] = folded.reshape((2,) * len(dims) + (16, units[f].columns))

    shipped = {}

    def ship(k):
        return remote(ships[k], docks[k], ship_send.at[k], ship_recv.at[k], "seq")

    path = [0] + list(dims)
    vector_flying = {}

    def vector_send(h):
        source = vector_ref if h == 0 else vector_sum.at[h - 1]
        return remote(source, vector_land.at[h], vsend_sem.at[h], vrecv_sem.at[h], path[h])

    def vector_add(h):
        vector_flying[h].wait_recv()
        before = vector_ref[...] if h == 0 else vector_sum[h - 1]
        total = before + vector_land[h]
        if h < hops:
            vector_sum[h] = total
            vector_flying[h + 1] = vector_send(h + 1)
        else:
            vector_out[...] = total

    vector_flying[0] = vector_send(0)
    vector_done, since = 0, 0
    for action, u, h in events:
        if action == COMPUTE and u == SHIP:
            finish_inputs()
        elif action == COMPUTE:
            multiply(u)
        elif action == SEND and u == SHIP:
            shipped[h] = ship(h)
        elif action == SEND:
            flying[u, h] = send(u, h)
        elif u == SHIP:
            shipped[h].wait_recv()
        else:
            add(u, h)
            since += 1
            if since % 12 == 0 and vector_done <= hops:
                vector_add(vector_done)
                vector_done += 1
    while vector_done <= hops:
        vector_add(vector_done)
        vector_done += 1
    wait(kept)
    for copy in sent:
        copy.wait_send()


EARLY = (0, 1, 2, 3, 4, 5)
X, Y, Z, ZZ = "seq", 1, 2, 3
XYZ, YXZ, YZX = (X, Y, Z, ZZ), (Y, X, Z, ZZ), (Y, Z, ZZ, X)
ZXY, ZYX, XZY = (Z, ZZ, X, Y), (Z, ZZ, Y, X), (X, Z, ZZ, Y)
COMPUTE, SEND, TAKE, SHIP = 0, 1, 2, -1
HOP_PLAN = [XZY, YXZ, ZYX, XYZ, YXZ, ZXY, YXZ, XYZ, YZX, XZY, YXZ, YXZ, YXZ, YXZ, XZY, XYZ, ZXY]
EVENTS = [
    (TAKE, 0, 0), (SEND, 0, 1), (TAKE, 1, 0), (SEND, 1, 1), (TAKE, 2, 0), (SEND, 2, 1),
    (TAKE, 3, 0), (SEND, 3, 1), (TAKE, 4, 0), (SEND, 4, 1), (TAKE, 5, 0), (SEND, 5, 1),
    (COMPUTE, 0, 0), (COMPUTE, 1, 0), (COMPUTE, 2, 0), (COMPUTE, 3, 0), (SEND, 6, 0),
    (TAKE, 3, 1), (SEND, 3, 2), (COMPUTE, SHIP, 0), (TAKE, 0, 1), (SEND, 7, 0), (TAKE, 1, 1),
    (SEND, 1, 2), (COMPUTE, 4, 0), (SEND, SHIP, 0), (TAKE, 4, 1), (COMPUTE, 5, 0),
    (COMPUTE, 6, 0), (SEND, 8, 0), (COMPUTE, 7, 0), (SEND, 0, 2), (TAKE, 2, 1), (SEND, 9, 0),
    (TAKE, 7, 0), (SEND, 10, 0), (TAKE, 6, 0), (COMPUTE, 8, 0), (COMPUTE, 9, 0), (SEND, 4, 2),
    (TAKE, 3, 2), (TAKE, SHIP, 0), (SEND, 6, 1), (COMPUTE, 10, 0), (SEND, 3, 3), (TAKE, 5, 1),
    (SEND, 14, 0), (TAKE, 9, 0), (SEND, 9, 1), (TAKE, 1, 2), (COMPUTE, 11, 0), (SEND, 16, 0),
    (SEND, 11, 0), (TAKE, 8, 0), (SEND, 15, 0), (TAKE, 6, 1), (SEND, 8, 1), (TAKE, 4, 2),
    (SEND, 1, 3), (SEND, 4, 3), (TAKE, 0, 2), (TAKE, 9, 1), (SEND, 9, 2), (TAKE, 3, 3),
    (SEND, 6, 2), (TAKE, 16, 0), (SEND, 16, 1), (SEND, 12, 0), (TAKE, 10, 0), (TAKE, 1, 3),
    (TAKE, 4, 3), (TAKE, 8, 1), (SEND, 8, 2), (TAKE, 9, 2), (SEND, 10, 1), (TAKE, 14, 0),
    (SEND, 14, 1), (TAKE, 16, 1), (SEND, 13, 0), (TAKE, 11, 0), (TAKE, 6, 2), (SEND, 6, 3),
    (TAKE, 8, 2), (SEND, 11, 1), (TAKE, 15, 0), (TAKE, 6, 3), (SEND, 5, 2), (TAKE, 10, 1),
    (SEND, 10, 2), (TAKE, 14, 1), (SEND, 14, 2), (SEND, 15, 1), (TAKE, 12, 0), (SEND, 12, 1),
    (TAKE, 11, 1), (SEND, 11, 2), (TAKE, 10, 2), (SEND, 10, 3), (SEND, 2, 2), (TAKE, 13, 0),
    (SEND, 13, 1), (TAKE, 5, 2), (TAKE, 14, 2), (TAKE, 11, 2), (SEND, 11, 3), (SEND, 7, 1),
    (TAKE, 15, 1), (SEND, 15, 2), (TAKE, 10, 3), (SEND, 8, 3), (SEND, 16, 2), (TAKE, 12, 1),
    (SEND, 12, 2), (SEND, 0, 3), (TAKE, 2, 2), (SEND, 2, 3), (SEND, SHIP, 1), (TAKE, 13, 1),
    (TAKE, 11, 3), (SEND, 13, 2), (TAKE, 15, 2), (SEND, 15, 3), (TAKE, 8, 3), (TAKE, 16, 2),
    (SEND, 14, 3), (SEND, 5, 3), (TAKE, 7, 1), (SEND, 7, 2), (TAKE, 12, 2), (SEND, 12, 3),
    (TAKE, 2, 3), (SEND, 16, 3), (SEND, 9, 3), (TAKE, 0, 3), (TAKE, 13, 2), (SEND, 13, 3),
    (TAKE, 15, 3), (TAKE, 14, 3), (TAKE, 5, 3), (TAKE, 7, 2), (SEND, 7, 3), (TAKE, 16, 3),
    (TAKE, 9, 3), (TAKE, 12, 3), (TAKE, 13, 3), (TAKE, 7, 3), (TAKE, SHIP, 1),
]


def weight_gradients(operands, vectors, skip_weight, half, plan, bits):
    matrices, units, events = plan
    blocks = 2**bits
    dims = list(reversed(range(1, bits))) + ["seq"]
    given = len(operands)
    operands = [*operands, vectors, skip_weight]
    width = skip_weight.shape[1]
    ends = [(half, width), (2, half, width // 2)]
    anywhere = pl.BlockSpec(memory_space=pl.ANY)
    vmem = pl.BlockSpec(memory_space=pltpu.VMEM)
    hops, count = len(dims), len(matrices)
    shape = jax.ShapeDtypeStruct
    outs = [shape((m.share, m.columns), jnp.float32) for m in matrices]
    outs += [shape(end, jnp.bfloat16) for end in ends]
    outs += [shape(end, jnp.float32) for end in ends]
    outs.append(shape(vectors.shape, jnp.float32))
    low = jnp.bfloat16
    scratch = [pltpu.VMEM((2,) * hops + (unit.rows, unit.columns), low) for unit in units]
    for unit in units:
        for h in range(hops):
            scratch.append(pltpu.VMEM((2,) * (hops - 1 - h) + (unit.rows, unit.columns), low))
    scratch.append(pltpu.VMEM((hops + 1,) + vectors.shape, jnp.float32))
    scratch.append(pltpu.VMEM((hops,) + vectors.shape, jnp.float32))
    folded = [matrix.fold_width for matrix in matrices if matrix.rest]
    scratch.append(pltpu.VMEM((blocks * 16, max(folded)), jnp.float32))
    scratch.append(pltpu.VMEM((2, max(m.left_rows(blocks) for m in matrices), TWO), low))
    scratch.append(pltpu.VMEM((2, TWO, max(max(w for _, w in m.pieces) for m in matrices)), low))
    scratch += [pltpu.SemaphoreType.DMA((len(units), hops))] * 2
    scratch += [pltpu.SemaphoreType.DMA((hops + 1,))] * 2
    scratch += [pltpu.SemaphoreType.DMA((2, 2))] * 2
    scratch += [pltpu.SemaphoreType.DMA((len(EARLY), 2))]
    scratch += [pltpu.SemaphoreType.DMA((SHIPS,))] * 2
    scratch += [pltpu.VMEM((2, width, width), low), pltpu.VMEM((LANES, width), low)]
    scratch += [pltpu.VMEM(end, jnp.float32) for end in ends]
    scratch += [pltpu.VMEM(end, low) for end in ends]
    scratch.append(pltpu.SemaphoreType.DMA((5,)))
    results = pl.pallas_call(
        functools.partial(reduce_kernel, matrices, units, events, dims),
        out_shape=outs,
        in_specs=[anywhere] * given + [vmem, anywhere],
        out_specs=[vmem] * count + [anywhere] * (2 * SHIPS) + [vmem],
        scratch_shapes=scratch,
        compiler_params=pltpu.CompilerParams(
            collective_id=0, has_side_effects=True, vmem_limit_bytes=62 * 2**20
        ),
        name="reduce_weights",
    )(*operands)
    return results[:count], results[-1], results[count:-1]


def even_cuts(columns, width):
    return [(start, width) for start in range(0, columns, width)]


def make_plan(width, hidden, chunks):
    matrices = [
        Matrix(hidden // chunks, width, [384] * 3, even_cuts(width, 384)),
        Matrix(width // chunks, hidden, [1152] * 4, even_cuts(hidden, 1152)),
        Matrix(width // chunks, width, [384] * 3, [(0, width)]),
        Matrix(width // chunks, 3 * width, [1152] * 3, even_cuts(3 * width, 1152)),
        Matrix(2 * width // chunks, width, [640, 512], [(0, 640), (640, 512)]),
    ]
    units = make_units(matrices, HOP_PLAN)
    return matrices, units, EVENTS


def halving(block, order, bits):
    dp_index = lax.axis_index("dp")
    seq_index = lax.axis_index("seq")
    dims = list(reversed(range(1, bits))) + ["seq"]
    for name in order:
        axis = dims.index(name)
        own = seq_index if name == "seq" else (dp_index >> name) & 1
        sent = pick(block, 1 - own, axis)
        kept = pick(block, own, axis)
        got = swap_seq(sent) if name == "seq" else swap_dp(sent, name)
        total = kept.astype(jnp.float32) + got.astype(jnp.float32)
        dims.pop(axis)
        block = total.astype(jnp.bfloat16) if dims else total
    return block


def local_permutes(
    inputs,
    skipped,
    lengths,
    cotangent,
    skip_weight,
    skip_bias,
    gain_one,
    shift_one,
    qkv_weight,
    proj_weight,
    proj_bias,
    gain_two,
    shift_two,
    fc1_weight,
    fc1_bias,
    fc2_weight,
    fc2_bias,
):
    items, half, width = inputs.shape
    seq_count = lax.axis_size("seq")
    dp_count = lax.axis_size("dp")
    bits = dp_count.bit_length() - 1
    seq_index = lax.axis_index("seq")
    core = lax.axis_index("dp") & 1
    first = seq_index == 0
    slots = half * seq_count

    def whole_item(values, axis):
        own = pick(values, seq_index, 0)
        got = swap_seq(pick(values, 1 - seq_index, 0))
        return place(first, own, got, axis)

    def to_owner(values, axis):
        parts = jnp.split(values, 2, axis=axis)
        own = jnp.where(first, parts[0], parts[1])
        other = jnp.where(first, parts[1], parts[0])
        got = swap_seq(other.astype(jnp.bfloat16)).astype(values.dtype)
        return place(first, own[None], got[None], 0)

    own_inputs = whole_item(inputs, 0)
    own_skip = whole_item(skipped, 1)
    grad_out = whole_item(cotangent, 0)
    length = pick(lengths, seq_index, 0)
    rows = slots

    joined = jnp.concatenate([own_inputs, own_skip], axis=-1)
    stream = matmul(joined, skip_weight) + skip_bias
    normed = layer_norm(stream, gain_one, shift_one).astype(jnp.bfloat16)
    packed = matmul(normed, qkv_weight).astype(jnp.bfloat16)
    heads = packed.reshape(rows, 3, HEADS, HEAD_DIM)
    query, keys, values = heads[:, 0], heads[:, 1], heads[:, 2]
    scale = HEAD_DIM ** (-0.5)
    positions = jnp.arange(slots, dtype=jnp.int32)
    caption = (positions >= 1) & (positions <= length)
    image = (positions >= 1 + CAPTION) & (positions < 1 + CAPTION + IMAGE)
    valid = (positions == 0) | caption | image

    def product(spec, left, right):
        return jnp.einsum(spec, left, right, preferred_element_type=jnp.float32)

    scores = product("qhd,khd->hqk", query, keys) * scale
    scores = jnp.where(valid[None, None, :], scores, masked_score)
    top = jnp.max(scores, axis=-1, keepdims=True)
    expo = jnp.exp(scores - top)
    probs = expo / jnp.sum(expo, axis=-1, keepdims=True)
    probs_low = probs.astype(jnp.bfloat16)
    mixed = product("hqk,khd->qhd", probs_low, values)
    mixed = mixed.astype(jnp.bfloat16).reshape(rows, width)
    attended = matmul(mixed, proj_weight) + proj_bias
    stream_two = stream + attended
    normed_two = layer_norm(stream_two, gain_two, shift_two).astype(jnp.bfloat16)
    hidden = matmul(normed_two, fc1_weight) + fc1_bias
    acted, gelu_back = jax.vjp(gelu_exact, hidden)
    acted_low = acted.astype(jnp.bfloat16)
    block_output = (stream_two + (matmul(acted_low, fc2_weight) + fc2_bias)).astype(jnp.bfloat16)

    blocks = dp_count // 2

    def own_rows(left, right):
        parts = left.reshape(rows, blocks, 2, -1)
        kept = pick(parts, core, 2).reshape(rows, -1)
        sent = pick(parts, 1 - core, 2).reshape(rows, -1)
        left_both = jnp.concatenate([kept, swap_dp(sent, 0)], axis=0)
        right_both = jnp.concatenate([right, swap_dp(right, 0)], axis=0)
        total = matmul(left_both.T, right_both).astype(jnp.bfloat16)
        share = total.shape[0] // (blocks * 2)
        return total.reshape((2,) * bits + (share, right.shape[1]))

    above = list(range(1, bits))
    order_x = ["seq"] + above
    order_y = above + ["seq"]
    order_z = above[1:] + ["seq"] + above[:1]

    grad_fc2 = halving(own_rows(acted_low, grad_out), order_x, bits)
    grad_fc2_bias = column_sum(grad_out)
    grad_acted = matmul(grad_out, fc2_weight.T)
    grad_hidden = gelu_back(grad_acted)[0].astype(jnp.bfloat16)
    grad_fc1 = halving(own_rows(normed_two, grad_hidden), order_x, bits)
    grad_fc1_bias = column_sum(grad_hidden)
    grad_normed_two = matmul(grad_hidden, fc1_weight.T)
    _, norm_back_two = jax.vjp(layer_norm, stream_two, gain_two, shift_two)
    back_two, grad_gain_two, grad_shift_two = norm_back_two(grad_normed_two)
    grad_stream_two = grad_out.astype(jnp.float32) + back_two
    grad_attended = grad_stream_two.astype(jnp.bfloat16)
    grad_proj = halving(own_rows(mixed, grad_attended), order_y, bits)
    grad_proj_bias = column_sum(grad_attended)
    grad_mixed = matmul(grad_attended, proj_weight.T)
    grad_mixed = grad_mixed.astype(jnp.bfloat16).reshape(rows, HEADS, HEAD_DIM)
    grad_probs = product("qhd,khd->hqk", grad_mixed, values)
    grad_scores = probs * (grad_probs - jnp.sum(probs * grad_probs, axis=-1, keepdims=True))
    grad_scores = grad_scores.astype(jnp.bfloat16)
    grad_values = product("hqk,qhd->khd", probs_low, grad_mixed)
    grad_query = product("hqk,khd->qhd", grad_scores, keys) * scale
    grad_keys = product("hqk,qhd->khd", grad_scores, query) * scale
    grad_packed = jnp.stack([grad_query, grad_keys, grad_values], axis=1)
    grad_packed = grad_packed.astype(jnp.bfloat16).reshape(rows, 3 * width)
    grad_qkv = halving(own_rows(normed, grad_packed), order_y, bits)
    grad_normed = matmul(grad_packed, qkv_weight.T)
    _, norm_back_one = jax.vjp(layer_norm, stream, gain_one, shift_one)
    back_one, grad_gain_one, grad_shift_one = norm_back_one(grad_normed)
    grad_stream = (grad_stream_two + back_one).astype(jnp.bfloat16)
    grad_skip = halving(own_rows(joined, grad_stream), order_z, bits)
    grad_skip_bias = column_sum(grad_stream)
    grad_joined = matmul(grad_stream, skip_weight.T)

    vectors = (
        grad_skip_bias,
        grad_gain_one,
        grad_shift_one,
        grad_proj_bias,
        grad_gain_two,
        grad_shift_two,
        grad_fc1_bias,
        grad_fc2_bias,
    )
    chunks = dp_count * seq_count
    line = jnp.concatenate([v.reshape(chunks, -1) for v in vectors], axis=1)
    line = lax.psum_scatter(line, ("dp", "seq"), scatter_dimension=0, tiled=True)[0]
    pieces, start = [], 0
    for vector in vectors:
        size = vector.shape[0] // chunks
        pieces.append(line[start : start + size])
        start += size

    return (
        to_owner(block_output, 0),
        to_owner(grad_joined[:, :width], 0),
        to_owner(grad_joined[:, width:], 1),
        grad_skip,
        pieces[0],
        pieces[1],
        pieces[2],
        grad_qkv,
        grad_proj,
        pieces[3],
        pieces[4],
        pieces[5],
        grad_fc1,
        pieces[6],
        grad_fc2,
        pieces[7],
    )


def local_kernels(*arguments):
    arrays = Arguments(*arguments)
    items, half, width = arrays.inputs.shape
    hidden = arrays.fc1_weight.shape[1]
    dp_count = lax.axis_size("dp")
    bits = dp_count.bit_length() - 1
    seq_index = lax.axis_index("seq")
    device = lax.axis_index("dp") * 2 + seq_index
    first = seq_index == 0
    chunks = dp_count * 2
    skipped = arrays.skipped.reshape(items, 2, half, width // 2)
    plan = make_plan(width, hidden, chunks)
    feed = dict(
        inputs=arrays.inputs,
        skipped=skipped,
        cotangent=arrays.cotangent,
        lengths=arrays.lengths,
    )
    for name in Arguments._fields[4:]:
        feed[name] = getattr(arrays, name)
    found = run_block(feed, *plan[:2], width, hidden, half)
    kinds = ("left_", "far_left_", "right_", "far_right_")
    operands = [getattr(found, kind + name) for name in WEIGHTS for kind in kinds]
    operands += [getattr(found, f"grad_{u}") for u in EARLY]
    operands += [getattr(found, f"far_grad_{u}") for u in EARLY]
    weights, vectors, got = weight_gradients(
        operands,
        found.vectors,
        arrays.skip_weight,
        half,
        plan,
        bits,
    )
    grad_in_got, grad_skip_got, grad_in_own, grad_skip_own = got

    def owner(own, other):
        other = other.astype(own.dtype)
        return jnp.where(first, jnp.stack([own, other]), jnp.stack([other, own]))

    share = width // chunks
    mine = lax.dynamic_slice(vectors, (0, device * share), (8, share))
    wide_share = hidden // chunks
    per_row = width // wide_share
    row = 8 + device // per_row
    bias = lax.dynamic_slice(vectors, (row, device % per_row * wide_share), (1, wide_share))[0]
    grad_fc2, grad_fc1, grad_proj, grad_qkv, grad_skip = weights
    grad_skip_own = grad_skip_own.reshape(2 * half, -1)
    return (
        owner(found.block_own, found.block_got),
        owner(grad_in_own, grad_in_got),
        owner(grad_skip_own, grad_skip_got.reshape(2 * half, -1)),
        grad_skip,
        mine[0],
        mine[1],
        mine[2],
        grad_qkv,
        grad_proj,
        mine[3],
        mine[4],
        mine[5],
        grad_fc1,
        bias,
        grad_fc2,
        mine[7],
    )


class Arguments(typing.NamedTuple):
    inputs: jax.Array
    skipped: jax.Array
    lengths: jax.Array
    cotangent: jax.Array
    skip_weight: jax.Array
    skip_bias: jax.Array
    gain_one: jax.Array
    shift_one: jax.Array
    qkv_weight: jax.Array
    proj_weight: jax.Array
    proj_bias: jax.Array
    gain_two: jax.Array
    shift_two: jax.Array
    fc1_weight: jax.Array
    fc1_bias: jax.Array
    fc2_weight: jax.Array
    fc2_bias: jax.Array


def solution(mesh):
    small = mesh.shape["dp"] == 16
    return jax.shard_map(
        local_kernels if small else local_permutes,
        mesh=mesh,
        in_specs=(
            P("dp", "seq", None),
            P("dp", None, "seq"),
            P("dp"),
            P("dp", "seq", None),
        )
        + (P(),) * 13,
        out_specs=(
            P("dp", "seq", None),
            P("dp", "seq", None),
            P("dp", None, "seq"),
            P(("dp", "seq"), None),
            P(("dp", "seq")),
            P(("dp", "seq")),
            P(("dp", "seq")),
            P(("dp", "seq"), None),
            P(("dp", "seq"), None),
            P(("dp", "seq")),
            P(("dp", "seq")),
            P(("dp", "seq")),
            P(("dp", "seq"), None),
            P(("dp", "seq")),
            P(("dp", "seq"), None),
            P(("dp", "seq")),
        ),
        check_vma=False,
    )
```

```python
import functools
import types
import typing

import jax
import jax.numpy as jnp
from jax import lax
from jax.experimental import pallas as pl
from jax.experimental.pallas import tpu as pltpu
from jax.sharding import PartitionSpec as P

HEADS = 16
HEAD_DIM = 72
CAPTION = 77
IMAGE = 256


epsilon = 1e-05
masked_score = -1e30


def layer_norm(stream, gain, shift):
    center = stream - jnp.mean(stream, axis=-1, keepdims=True)
    spread = jnp.mean(center * center, axis=-1, keepdims=True)
    return center * lax.rsqrt(spread + epsilon) * gain + shift


def gelu_exact(values):
    return jax.nn.gelu(values, approximate=False)


def column_sum(values):
    return jnp.sum(values.astype(jnp.float32), axis=0)


def matmul(left, right):
    return jnp.dot(left, right, preferred_element_type=jnp.float32)


def swap_seq(values):
    return lax.ppermute(values, "seq", [(0, 1), (1, 0)])


def swap_dp(values, bit):
    count = lax.axis_size("dp")
    return lax.ppermute(values, "dp", [(i, i ^ (1 << bit)) for i in range(count)])


def pick(values, index, axis):
    return lax.dynamic_index_in_dim(values, index, axis, keepdims=False)


def place(first, own, got, axis):
    return jnp.where(
        first, jnp.concatenate([own, got], axis=axis), jnp.concatenate([got, own], axis=axis)
    )


PAD = 192
ROWS = 2 * PAD


def matmul_t(left, right):
    return lax.dot_general(
        left, right, (((1,), (1,)), ((), ())), preferred_element_type=jnp.float32
    )


def t_matmul(left, right):
    return lax.dot_general(
        left, right, (((0,), (0,)), ((), ())), preferred_element_type=jnp.float32
    )


def tiles_of(width):
    starts = list(range(0, width - 255, 512))
    ends = starts[1:] + [width]
    return [pl.ds(a, b - a) for a, b in zip(starts, ends)]


def norm_parts(values):
    center = values - jnp.mean(values, axis=-1, keepdims=True)
    spread = jnp.mean(center * center, axis=-1, keepdims=True)
    scale = lax.rsqrt(spread + epsilon)
    return center * scale, scale


def fold_rows(values):
    rows, width = values.shape
    return jnp.sum(values.reshape(rows // 8, 8, width), axis=0)


def block_kernel(half, hidden, matrices, early, names, *refs):
    r = types.SimpleNamespace(**dict(zip(names, refs)))
    width = r.skip_weight.shape[1]
    seq = lax.axis_index("seq")
    core = lax.rem(lax.axis_index("dp"), 2)
    sems = r.sems
    low = jnp.bfloat16
    counter = iter(range(80))

    def copy(source, target):
        return pltpu.make_async_copy(source, target, sems.at[next(counter)])

    loads = types.SimpleNamespace(
        in0=copy(r.inputs.at[seq], r.raw_in.at[seq]),
        sk0=copy(r.skipped.at[seq], r.raw_skip.at[seq]),
        skip0=copy(r.skip_weight.at[pl.ds(0, width), :], r.feed.at[0]),
        skip1=copy(r.skip_weight.at[pl.ds(width, width), :], r.feed.at[1]),
        ct0=copy(r.cotangent.at[seq], r.raw_out.at[seq]),
        proj=copy(r.proj_weight, r.proj_buffer),
    )
    spare = r.spare

    def load_qkv():
        parts = [
            copy(r.qkv_weight.at[:, pl.ds(k * width, width)], spare.at[k]) for k in range(3)
        ]
        for load in parts:
            load.start()
        return parts

    dp = lax.axis_index("dp")
    neighbour = (dp, 1 - seq)

    def flip(name):
        if name == "seq":
            return neighbour
        return (dp + (1 - 2 * lax.rem(lax.div(dp, 1 << name), 2)) * (1 << name), seq)

    barrier = pltpu.get_barrier_semaphore()
    names_met = [0] + sorted({hop for _, hop in early}, key=str)
    for name in names_met:
        pl.semaphore_signal(barrier, inc=1, device_id=flip(name), device_id_type=MESH)
    for load in vars(loads).values():
        load.start()
    qkv_loads = load_qkv()
    pl.semaphore_wait(barrier, len(names_met))
    remotes = []

    def remote(source, target, name):
        k = len(remotes)
        item = pltpu.make_async_remote_copy(
            src_ref=source,
            dst_ref=target,
            send_sem=r.send_sem.at[k],
            recv_sem=r.recv_sem.at[k],
            device_id=flip(name),
            device_id_type=MESH,
        )
        item.start()
        remotes.append(item)
        return item

    gone, come = set(), set()

    def left_here(item):
        if id(item) not in gone:
            gone.add(id(item))
            item.wait_send()

    def got_here(item):
        if id(item) not in come:
            come.add(id(item))
            item.wait_recv()

    traded = [
        remote(r.inputs.at[1 - seq], r.raw_in.at[seq], "seq"),
        remote(r.skipped.at[1 - seq], r.raw_skip.at[seq], "seq"),
    ]
    chunk, feed = width, r.feed
    feeds = []
    for j in range(hidden // chunk):
        part = pl.ds(j * chunk, chunk)
        at = 2 - 2 * (j % 2)
        feeds.append(
            (
                copy(r.fc1_weight.at[:, part], feed.at[at]),
                copy(r.fc2_weight.at[part, :], feed.at[at + 1]),
            )
        )

    def start(copies):
        for item in copies:
            item.start()

    start(feeds[0])
    stores = {}

    def store(source, target):
        item = copy(source, target)
        item.start()
        stores[id(item)] = item
        return item

    def finish(item):
        stores.pop(id(item)).wait()

    joined, skips, grad_out = r.joined, r.skips, r.grad_out
    gap = PAD - half
    for load in (loads.in0, loads.sk0):
        load.wait()
    for item in traded:
        got_here(item)
    traded = remote(r.cotangent.at[1 - seq], r.raw_out.at[seq], "seq")
    for h in range(2):
        joined[pl.ds(h * PAD, PAD), :] = jnp.concatenate(
            [r.raw_in[h], jnp.zeros((gap, width), low)], axis=0
        )
        for f in range(2):
            skips[f, pl.ds(h * PAD, PAD), :] = jnp.concatenate(
                [r.raw_skip[f, h], jnp.zeros((gap, width // 2), low)], axis=0
            )
    loads.skip0.wait()
    loads.skip1.wait()
    stream = r.stream
    tiles = tiles_of(width)

    for columns in tiles:
        total = matmul(joined[...], feed[0, :, columns])
        total += matmul(skips[0], feed[1, pl.ds(0, width // 2), columns])
        total += matmul(skips[1], feed[1, pl.ds(width // 2, width // 2), columns])
        stream[:, columns] = total + r.skip_bias[columns]

    start(feeds[1])
    step = 128

    def norm(source, gain, shift, target):
        @pl.loop(0, ROWS // step)
        def _(i):
            rows = pl.ds(pl.multiple_of(i * step, step), step)
            unit, _ = norm_parts(source[rows, :])
            target[rows, :] = (unit * gain[...] + shift[...]).astype(low)

    normed, packed = r.normed, r.packed
    norm(stream, r.gain_one, r.shift_one, normed)
    for load in qkv_loads:
        load.wait()

    for k in range(3):
        for columns in tiles:
            target = pl.ds(k * width + columns.start, columns.size)
            packed[:, target] = matmul(normed[...], spare[k, :, columns]).astype(low)

    length = r.lengths[seq]
    at = lax.broadcasted_iota(jnp.int32, (1, ROWS), 1)
    inner = jnp.where(at >= PAD, at - PAD, at)
    position = jnp.where(at >= PAD, at - PAD + half, at)
    valid = (position == 0) | ((position >= 1) & (position <= length))
    valid = valid | ((position >= 1 + CAPTION) & (position < 1 + CAPTION + IMAGE))
    valid = valid & (inner < half)
    scale = HEAD_DIM ** (-0.5)
    window = 256

    def head_window(h):
        start = jnp.minimum(lax.div(h * HEAD_DIM, 128) * 128, width - window)
        start = pl.multiple_of(start, 128)
        lane = lax.broadcasted_iota(jnp.int32, (1, window), 1) + start
        mine = (lane >= h * HEAD_DIM) & (lane < (h + 1) * HEAD_DIM)
        return start, mine

    def part(which, start):
        return packed[:, pl.ds(pl.multiple_of(which * width + start, 128), window)]

    mixed_sum, probs = r.sum_a, r.probs

    def attend(h, carry):
        start, mine = head_window(h)
        query = jnp.where(mine, part(0, start), jnp.zeros((), low))
        scores = matmul_t(query, part(1, start)) * scale
        scores = jnp.where(valid, scores, masked_score)
        expo = jnp.exp(scores - jnp.max(scores, axis=-1, keepdims=True))
        share = expo * (1.0 / jnp.sum(expo, axis=-1, keepdims=True))
        share = share.astype(low)
        probs[h] = share
        found = matmul(share, part(2, start))
        columns = pl.ds(start, window)
        mixed_sum[:, columns] = jnp.where(mine, found, mixed_sum[:, columns])
        return carry

    lax.fori_loop(0, HEADS, attend, 0, unroll=4)
    mixed, stream_two = r.mixed, r.stream_two
    mixed[...] = mixed_sum[...].astype(low)
    loads.proj.wait()

    for columns in tiles:
        total = matmul(mixed[...], r.proj_buffer[:, columns]) + r.proj_bias[columns]
        stream_two[:, columns] = stream[:, columns] + total

    normed_two = r.normed_two
    norm(stream_two, r.gain_two, r.shift_two, normed_two)
    loads.ct0.wait()
    got_here(traded)
    for h in range(2):
        grad_out[pl.ds(h * PAD, PAD), :] = jnp.concatenate(
            [r.raw_out[h], jnp.zeros((gap, width), low)], axis=0
        )
    far_out = remote(grad_out, r.far_right_fc2, 0)
    sums = r.sums
    sums[7:8, :] = jnp.sum(grad_out[...].astype(jnp.float32), axis=0, keepdims=True)

    turned_ref = r.turned
    stages = {}

    def left(m, target, far, sources):
        matrix = matrices[m]
        stage = r.left_stage
        for item in stages.pop(0, ()):
            finish(item) if id(item) in stores else left_here(item)
        share, main, rest = matrix.share, matrix.main, matrix.rest
        folds, body = len(matrix.pieces), 16 * main
        first = 0
        for source in sources:
            turned_ref[pl.ds(32, width), :] = source.T.astype(jnp.float32)
            for k in range(width // share):
                number = first + k
                c, block = number // 2 % 2, number // 4 * 2 + number % 2
                base = 32 + k * share
                place = c ^ core
                stage[place, pl.ds(block * main, main), :] = turned_ref[
                    pl.ds(base, main), :
                ].astype(low)
                row = lax.broadcasted_iota(jnp.int32, (16, 1), 0)
                for q in range(folds):
                    part = turned_ref[pl.ds(base + main - q * rest, 16), :]
                    part = jnp.where((row >= q * rest) & (row < (q + 1) * rest), part, 0.0)
                    stage[place, pl.ds(body + (q * 16 + block) * 16, 16), :] = part.astype(low)
            first += width // share
        rows = matrix.left_rows(16)
        stages[0] = [
            store(stage.at[0, pl.ds(0, rows), :], target),
            remote(stage.at[1, pl.ds(0, rows), :], far, 0),
        ]

    body = 16 * matrices[1].main
    left(1, r.left_fc1, r.far_left_fc1, [normed_two[...]])
    far_left = remotes[-1]
    near = copy(r.left_stage.at[0, pl.ds(0, body), :], spare.at[0, pl.ds(0, body), pl.ds(2 * ROWS, ROWS)])
    near.start()
    stores[id(near)] = near
    far_hidden = []
    opened, loading = [], []

    def fetch(source, target):
        item = copy(source, target)
        item.start()
        return item

    def launch():
        while opened:
            u, hop, item = opened.pop(0)
            finish(item)
            dims = [3, 2, 1, "seq"]
            bit = seq if hop == "seq" else lax.rem(lax.div(dp, 1 << hop), 2)
            index = tuple(1 - bit if name == hop else slice(None) for name in dims)
            remote(getattr(r, f"grad_{u}").at[index], getattr(r, f"far_grad_{u}"), hop)

    fetched = {}

    def prefetch(p):
        got_here(far_hidden[p])
        source = r.far_right_fc1.at[:, pl.ds(p * chunk, chunk)]
        fetched[p] = [fetch(source, spare.at[2, pl.ds(ROWS, ROWS), :])]
        if p == 0:
            got_here(far_left)
            target = spare.at[0, pl.ds(body, body), pl.ds(2 * ROWS, ROWS)]
            fetched[p].append(fetch(r.far_left_fc1.at[pl.ds(0, body), :], target))
            got_here(far_out)
            loading.append(fetch(r.far_right_fc2, spare.at[2, pl.ds(0, ROWS), :]))
        prefetch_left(p)

    def prefetch_left(p):
        got_here(far_acted[p])
        count = 4 * matrices[0].share
        source = r.far_left_fc2.at[pl.ds(p * count, count), :]
        target = spare.at[1, pl.ds(p % 2 * count, count), pl.ds(p // 2 * ROWS, ROWS)]
        loading.append(fetch(source, target))

    def early_hidden(p):
        for item in fetched.pop(p):
            item.wait()
        if p == 0:
            finish(near)
        launch()
        near_rows, far_rows = (spare[0, pl.ds(k * body, body), pl.ds(2 * ROWS, ROWS)] for k in range(2))
        for columns in tiles:
            value = matmul(near_rows, grad_hidden[p % 2, :, columns])
            value += matmul(far_rows, spare[2, pl.ds(ROWS, ROWS), columns])
            value = value.astype(low).reshape(2, 2, 2, 2, matrices[1].main, columns.size)
            r.wide_stage[:, :, :, :, :, columns] = value
        u, hop = early[3 + p]
        opened.append((u, hop, store(r.wide_stage, getattr(r, f"grad_{u}"))))

    forward, backward = r.sum_a, r.sum_b
    acted, grad_hidden, staged = r.acted, r.grad_hidden, r.left_fc2_stage
    pending, far_acted = {}, []
    for j, feeding in enumerate(feeds):
        slot = j % 2
        first, second = feed.at[2 - 2 * slot], feed.at[3 - 2 * slot]
        for load in feeding:
            load.wait()
        for item in pending.get(slot, ()):
            finish(item) if id(item) in stores else left_here(item)

        for columns in tiles:
            whole = pl.ds(j * chunk + columns.start, columns.size)
            value = matmul(normed_two[...], first[:, columns])
            value += r.fc1_bias[whole]
            phi = 0.5 + 0.5 * lax.erf(value * (0.5**0.5))
            bell = jnp.exp(-0.5 * value * value) * ((2 * jnp.pi) ** -0.5)
            acted[slot, :, columns] = (value * phi).astype(low)
            back = matmul_t(grad_out[...], second[columns, :])
            back = (back * (phi + value * bell)).astype(low)
            grad_hidden[slot, :, columns] = back
            sums[pl.ds(8 + j, 1), columns] = jnp.sum(
                back.astype(jnp.float32), axis=0, keepdims=True
            )

        if j >= 1:
            prefetch(j - 1)
        for columns in tiles:
            ahead = matmul(acted[slot], second[:, columns])
            back = matmul_t(grad_hidden[slot], first[columns, :])
            if j == 0:
                forward[:, columns] = ahead
                backward[:, columns] = back
            else:
                forward[:, columns] += ahead
                backward[:, columns] += back

        share = matrices[0].share
        turned = acted[slot].T
        groups = chunk // (4 * share)
        for g in range(groups):
            begin = g * 4 * share
            lower, upper = turned[begin : begin + 2 * share], turned[begin + 2 * share : begin + 4 * share]
            number = j * groups + g
            rows = pl.ds(number % 4 * 2 * share, 2 * share)
            spare[0, rows, pl.ds(number // 4 * ROWS, ROWS)] = jnp.where(core == 0, lower, upper)
            staged[slot, pl.ds(g * 2 * share, 2 * share), :] = jnp.where(core == 0, upper, lower)
        count = groups * 2 * share
        far_acted.append(remote(staged.at[slot], r.far_left_fc2.at[pl.ds(j * count, count), :], 0))
        part_columns = pl.ds(j * chunk, chunk)
        far_hidden.append(remote(grad_hidden.at[slot], r.far_right_fc1.at[:, part_columns], 0))
        pending[slot] = [
            far_acted[-1],
            far_hidden[-1],
            store(grad_hidden.at[slot], r.right_fc1.at[:, part_columns]),
        ]
        if j + 2 < len(feeds):
            start(feeds[j + 2])
        if 1 <= j < 4:
            early_hidden(j - 1)

    left(2, r.left_proj, r.far_left_proj, [mixed[...]])
    launch()
    prefetch_left(3)
    left(3, r.left_qkv, r.far_left_qkv, [normed[...]])
    left(4, r.left_skip, r.far_left_skip, [joined[...], jnp.concatenate([skips[0], skips[1]], axis=1)])

    for item in loading:
        item.wait()
    share = matrices[0].share
    for p in range(3):
        start_column, size = matrices[0].pieces[p]
        columns = pl.ds(start_column, size)
        launch()
        for k in range(2):
            for g in range(2):
                rows, lanes = pl.ds(g * 4 * share, 4 * share), pl.ds(k * ROWS, ROWS)
                value = matmul(spare[0, rows, lanes], grad_out[:, columns])
                value += matmul(spare[1, rows, lanes], spare[2, pl.ds(0, ROWS), columns])
                r.tall_stage[k, g] = value.astype(low).reshape(2, 2, share, size)
        u, hop = early[p]
        opened.append((u, hop, store(r.tall_stage, getattr(r, f"grad_{u}"))))
    qkv_loads = load_qkv()

    grad_two = r.grad_two
    out_stage, grad_low = r.raw_out, r.grad_low
    for h in range(2):
        rows = pl.ds(h * PAD, half)
        value = stream_two[rows, :] + (forward[rows, :] + r.fc2_bias[...])
        out_stage[h] = value.astype(low)
    store(out_stage.at[seq], r.block_own)
    remote(out_stage.at[1 - seq], r.block_got, "seq")
    launch()

    def norm_back(source, gain, back, extra, target, target_low, gain_row, shift_row):
        partial = r.partial
        partial[...] = jnp.zeros_like(partial)

        @pl.loop(0, ROWS // step)
        def _(i):
            rows = pl.ds(pl.multiple_of(i * step, step), step)
            unit, spread = norm_parts(source[rows, :])
            value = back[rows, :]
            partial[0] += fold_rows(value * unit)
            partial[1] += fold_rows(value)
            value = value * gain[...]
            mean = jnp.mean(value, axis=-1, keepdims=True)
            slope = jnp.mean(value * unit, axis=-1, keepdims=True)
            value = spread * (value - mean - unit * slope)
            value = value + extra[rows, :].astype(jnp.float32)
            if target is not None:
                target[rows, :] = value
            rounded = value.astype(low)
            target_low[rows, :] = rounded
            partial[2] += fold_rows(rounded.astype(jnp.float32))

        sums[gain_row : gain_row + 1, :] = jnp.sum(partial[0], axis=0, keepdims=True)
        sums[shift_row : shift_row + 1, :] = jnp.sum(partial[1], axis=0, keepdims=True)
        return jnp.sum(partial[2], axis=0, keepdims=True)

    sums[3:4, :] = norm_back(stream_two, r.gain_two, backward, grad_out, grad_two, grad_low, 4, 5)
    store(grad_low, r.right_proj)
    remote(grad_low, r.far_right_proj, 0)
    grad_mixed = r.grad_mixed

    for columns in tiles:
        grad_mixed[:, columns] = matmul_t(grad_low[...], r.proj_buffer[columns, :]).astype(low)

    grad_query, grad_key, grad_value = r.sum_a, r.sum_b, r.sum_c

    def attend_back(h, carry):
        start, mine = head_window(h)
        zero = jnp.zeros((), low)
        columns = pl.ds(start, window)
        query = jnp.where(mine, part(0, start), zero)
        back = jnp.where(mine, grad_mixed[:, columns], zero)
        share = probs[h]
        grad_share = matmul_t(back, part(2, start))
        wide = share.astype(jnp.float32)
        level = jnp.sum(wide * grad_share, axis=-1, keepdims=True)
        grad_score = (wide * (grad_share - level)).astype(low)
        found = t_matmul(share, back)
        grad_value[:, columns] = jnp.where(mine, found, grad_value[:, columns])
        found = matmul(grad_score, part(1, start)) * scale
        grad_query[:, columns] = jnp.where(mine, found, grad_query[:, columns])
        found = t_matmul(grad_score, query) * scale
        grad_key[:, columns] = jnp.where(mine, found, grad_key[:, columns])
        return carry

    lax.fori_loop(0, HEADS, attend_back, 0, unroll=4)
    for k, source in enumerate((grad_query, grad_key, grad_value)):
        packed[:, pl.ds(k * width, width)] = source[...].astype(low)
    store(packed, r.right_qkv)
    remote(packed, r.far_right_qkv, 0)
    for load in qkv_loads:
        load.wait()
    grad_normed = r.sum_a

    for columns in tiles:
        total = matmul_t(packed[:, pl.ds(0, width)], spare[0, columns, :])
        for k in range(1, 3):
            total += matmul_t(packed[:, pl.ds(k * width, width)], spare[k, columns, :])
        grad_normed[:, columns] = total

    grad_stream = r.grad_mixed
    sums[0:1, :] = norm_back(stream, r.gain_one, grad_normed, grad_two, None, grad_stream, 1, 2)
    store(grad_stream, r.right_skip)
    remote(grad_stream, r.far_right_skip, 0)
    sums[12:16, :] = jnp.zeros((4, width), jnp.float32)
    sums[6:7, :] = jnp.zeros((1, width), jnp.float32)
    store(sums, r.vectors)

    for item in stores.values():
        item.wait()
    for item in remotes:
        got_here(item)
        left_here(item)


WEIGHTS = ["fc1", "proj", "qkv", "skip"]


def run_block(arrays, matrices, units, width, hidden, half):
    low, wide = jnp.bfloat16, jnp.float32
    shape = jax.ShapeDtypeStruct
    outs = dict(
        block_own=shape((half, width), low),
        block_got=shape((half, width), low),
        vectors=shape((16, width), wide),
    )
    for name, matrix in zip(WEIGHTS, matrices[1:]):
        for prefix in ("", "far_"):
            outs[prefix + "left_" + name] = shape((matrix.left_rows(16), ROWS), low)
            outs[prefix + "right_" + name] = shape((ROWS, matrix.columns), low)
    outs.update(
        far_left_fc2=shape((matrices[0].left_rows(16), ROWS), low),
        far_right_fc2=shape((ROWS, width), low),
    )
    for u in EARLY:
        tail = (units[u].rows, units[u].columns)
        outs[f"grad_{u}"] = shape((2, 2, 2, 2) + tail, low)
        outs[f"far_grad_{u}"] = shape((2, 2, 2) + tail, low)
    early = [(u, units[u].hops[0]) for u in EARLY]
    staged = 16 * matrices[0].share // (hidden // width)
    square = (ROWS, width)
    scratch = dict(
        raw_in=((2, half, width), low),
        raw_skip=((2, 2, half, width // 2), low),
        raw_out=((2, half, width), low),
        spare=((3, width, width), low),
        proj_buffer=((width, width), low),
        feed=((4, width, width), low),
        joined=(square, low),
        skips=((2, ROWS, width // 2), low),
        grad_out=(square, low),
        stream=(square, wide),
        normed=(square, low),
        packed=((ROWS, 3 * width), low),
        probs=((HEADS, ROWS, ROWS), low),
        sum_a=(square, wide),
        sum_b=(square, wide),
        sum_c=(square, wide),
        mixed=(square, low),
        stream_two=(square, wide),
        normed_two=(square, low),
        acted=((2,) + square, low),
        grad_hidden=((2,) + square, low),
        left_fc2_stage=((2, staged, ROWS), low),
        tall_stage=((2, 2, 2, 2, matrices[0].share, 384), low),
        wide_stage=((2, 2, 2, 2, matrices[1].main, width), low),
        left_stage=((2, max(m.left_rows(16) for m in matrices[1:]), ROWS), low),
        turned=((width + 64, ROWS), wide),
        sums=((16, width), wide),
        partial=((3, 8, width), wide),
        grad_two=(square, wide),
        grad_low=(square, low),
        grad_mixed=(square, low),
    )
    anywhere = pl.BlockSpec(memory_space=pl.ANY)
    vmem = pl.BlockSpec(memory_space=pltpu.VMEM)
    smem = pl.BlockSpec(memory_space=pltpu.SMEM)
    small = {name for name, a in arrays.items() if a.dtype == wide}
    specs = [smem if n == "lengths" else vmem if n in small else anywhere for n in arrays]
    names = list(arrays) + list(outs) + list(scratch) + ["sems", "send_sem", "recv_sem"]
    results = pl.pallas_call(
        functools.partial(block_kernel, half, hidden, matrices, early, names),
        out_shape=list(outs.values()),
        in_specs=specs,
        out_specs=[anywhere] * len(outs),
        scratch_shapes=[pltpu.VMEM(*s) for s in scratch.values()]
        + [pltpu.SemaphoreType.DMA((n,)) for n in (80, 40, 40)],
        compiler_params=pltpu.CompilerParams(
            collective_id=1, has_side_effects=True, vmem_limit_bytes=63 * 2**20
        ),
        name="block",
    )(*arrays.values())
    return types.SimpleNamespace(**dict(zip(outs, results)))


MESH = pl.DeviceIdType.MESH
LANES = 384
SHIPS = 2
TWO = 2 * LANES


class Matrix:
    def __init__(self, share, columns, pieces, cuts):
        self.share, self.columns = share, columns
        self.main = share - share % 16
        self.rest = share % 16
        self.pieces, start = [], 0
        for width in pieces:
            self.pieces.append((start, width))
            start += width
        self.cuts = cuts
        self.fold = self.rest and 16
        self.fold_width = max(pieces)

    def left_rows(self, blocks):
        folds = len(self.pieces) if self.rest else 0
        return blocks * (self.main + folds * 16)


class Unit:
    def __init__(self, matrix, rows, start, columns, hops, folded):
        self.matrix, self.rows, self.start, self.columns = matrix, rows, start, columns
        self.hops, self.folded = hops, folded


def make_units(matrices, hops_of):
    units = []
    for m, matrix in enumerate(matrices):
        for start, columns in matrix.cuts:
            units.append(Unit(m, matrix.main, start, columns, hops_of[len(units)], False))
        if matrix.rest:
            units.append(Unit(m, 16, 0, matrix.fold_width, hops_of[len(units)], True))
    return units


def reduce_kernel(matrices, units, events, dims, *refs):
    count = len(matrices)
    lefts, far_lefts, rights, far_rights = ([None, *refs[k : 16 : 4]] for k in range(4))
    refs = refs[16:]
    whole_grads, refs = refs[: len(EARLY)], refs[len(EARLY) :]
    far_grads, refs = refs[: len(EARLY)], refs[len(EARLY) :]
    vector_ref, skip_ref, refs = refs[0], refs[1], refs[2:]
    outs, refs = refs[:count], refs[count:]
    docks, refs = refs[:SHIPS], refs[SHIPS:]
    own_in, own_skip, refs = refs[0], refs[1], refs[2:]
    vector_out, refs = refs[0], refs[1:]
    grads, refs = refs[: len(units)], refs[len(units) :]
    hops = len(dims)
    landed = [refs[i * hops : (i + 1) * hops] for i in range(len(units))]
    refs = refs[len(units) * hops :]
    vector_land, vector_sum, refs = refs[0], refs[1], refs[2:]
    fold_sum, left_buffer, right_buffer, refs = refs[0], refs[1], refs[2], refs[3:]
    send_sem, recv_sem, vsend_sem, vrecv_sem, left_sem, right_sem, *refs = refs
    early_sem, ship_send, ship_recv, skip_buffer, grad_stream, *refs = refs
    back_in, back_skip, send_in, send_skip, skip_sem = refs
    ships = [send_in, send_skip]

    dp = lax.axis_index("dp")
    seq = lax.axis_index("seq")
    core = lax.rem(dp, 2)

    def bit(name):
        return seq if name == "seq" else lax.rem(lax.div(dp, 1 << name), 2)

    def partner(name):
        if name == "seq":
            return (dp, 1 - seq)
        return (dp + (1 - 2 * bit(name)) * (1 << name), seq)

    barrier = pltpu.get_barrier_semaphore()
    for name in [0] + list(dims):
        pl.semaphore_signal(barrier, inc=1, device_id=partner(name), device_id_type=MESH)
    pl.semaphore_wait(barrier, len(dims) + 1)

    sent = []

    def remote(source, target, send_at, recv_at, name):
        copy = pltpu.make_async_remote_copy(
            src_ref=source,
            dst_ref=target,
            send_sem=send_at,
            recv_sem=recv_at,
            device_id=partner(name),
            device_id_type=MESH,
        )
        copy.start()
        sent.append(copy)
        return copy

    early_copies = {}
    for k, u in enumerate(EARLY):
        hop = units[u].hops[0]
        index = tuple(bit(name) if name == hop else slice(None) for name in dims)
        early_copies[u] = [
            pltpu.make_async_copy(
                whole_grads[k].at[index], grads[u].at[index], early_sem.at[k, 0]
            ),
            pltpu.make_async_copy(far_grads[k], landed[u][0], early_sem.at[k, 1]),
        ]
        for copy in early_copies[u]:
            copy.start()

    width = skip_buffer.shape[2]
    skip_copies = [
        pltpu.make_async_copy(
            skip_ref.at[pl.ds(k * width, width), :], skip_buffer.at[k], skip_sem.at[k]
        )
        for k in range(2)
    ]
    skip_copies.append(pltpu.make_async_copy(rights[4], grad_stream, skip_sem.at[2]))
    kept = []

    def finish_inputs():
        wait(skip_copies)
        half, feature = send_in.shape[0], width // 2
        for columns in tiles_of(width):
            value = matmul_t(grad_stream[...], skip_buffer[0, columns, :])
            lower, upper = value[:half], value[PAD : PAD + half]
            back_in[:, columns] = jnp.where(seq == 0, lower, upper)
            send_in[:, columns] = jnp.where(seq == 0, upper, lower).astype(jnp.bfloat16)
        parts = [
            matmul_t(grad_stream[...], skip_buffer[1, pl.ds(f * feature, feature), :])
            for f in range(2)
        ]
        for h in range(2):
            lower, upper = (part[h * PAD : h * PAD + half] for part in parts)
            back_skip[h] = jnp.where(seq == 0, lower, upper)
            send_skip[h] = jnp.where(seq == 0, upper, lower).astype(jnp.bfloat16)
        kept.append(pltpu.make_async_copy(back_in, own_in, skip_sem.at[3]))
        kept.append(pltpu.make_async_copy(back_skip, own_skip, skip_sem.at[4]))
        start(kept)

    def left_copies(m):
        rows = matrices[m].left_rows(2 ** len(dims))
        return [
            pltpu.make_async_copy(
                (lefts[m], far_lefts[m])[k],
                left_buffer.at[m % 2, pl.ds(0, rows), pl.ds(k * LANES, LANES)],
                left_sem.at[m % 2, k],
            )
            for k in range(2)
        ]

    all_pieces = [(m, p) for m in range(1, count) for p in range(len(matrices[m].pieces))]

    def right_copies(index):
        m, p = all_pieces[index]
        start, width = matrices[m].pieces[p]
        return [
            pltpu.make_async_copy(
                (rights[m], far_rights[m])[k].at[:, pl.ds(start, width)],
                right_buffer.at[index % 2, pl.ds(k * LANES, LANES), pl.ds(0, width)],
                right_sem.at[index % 2, k],
            )
            for k in range(2)
        ]

    def start(copies):
        for copy in copies:
            copy.start()

    def wait(copies):
        for copy in copies:
            copy.wait()

    start(left_copies(1))
    for index in range(2):
        start(right_copies(index))
    start(left_copies(2))
    start(skip_copies)

    def send(u, h):
        unit = units[u]
        index = []
        for name in dims:
            if name in unit.hops[:h]:
                index.append(bit(name))
            elif name == unit.hops[h]:
                index.append(1 - bit(name))
            else:
                index.append(slice(None))
        return remote(
            grads[u].at[tuple(index)],
            landed[u][h],
            send_sem.at[u, h],
            recv_sem.at[u, h],
            unit.hops[h],
        )

    flying = {}

    def add(u, h):
        unit = units[u]
        if h == 0 and u in EARLY:
            wait(early_copies[u])
        else:
            flying[u, h].wait_recv()
        done = unit.hops[: h + 1]
        free = [name for name in dims if name not in done]
        step = next(n for n in (48, 32, 16) if unit.rows % n == 0)
        last = h + 1 == hops

        @pl.loop(0, 2 ** len(free) * (unit.rows // step))
        def _(i):
            block, row = lax.div(i, unit.rows // step), lax.rem(i, unit.rows // step) * step
            place = {
                name: lax.rem(lax.div(block, 1 << (len(free) - 1 - k)), 2)
                for k, name in enumerate(free)
            }
            rows = pl.ds(pl.multiple_of(row, step), step)
            own = tuple(place.get(name, bit(name)) for name in dims) + (rows,)
            got = tuple(place[name] for name in free) + (rows,)
            total = grads[u][own].astype(jnp.float32) + landed[u][h][got].astype(jnp.float32)
            if last and not unit.folded:
                outs[unit.matrix][rows, pl.ds(unit.start, unit.columns)] = total
            elif last:
                matrix = matrices[unit.matrix]
                for p, (begin, size) in enumerate(matrix.pieces):
                    part = total[p * matrix.rest : (p + 1) * matrix.rest, :size]
                    under = pl.ds(matrix.main, matrix.rest)
                    outs[unit.matrix][under, pl.ds(begin, size)] = part
            else:
                grads[u][own] = total.astype(jnp.bfloat16)

    def multiply(index):
        m, p = all_pieces[index]
        matrix = matrices[m]
        start_column, width = matrix.pieces[p]
        blocks = 2 ** len(dims)
        if p == 0:
            wait(left_copies(m))
        wait(right_copies(index))
        left, right = left_buffer.at[m % 2], right_buffer.at[index % 2]
        u = next(
            i
            for i, unit in enumerate(units)
            if unit.matrix == m
            and not unit.folded
            and unit.start <= start_column < unit.start + unit.columns
        )
        group = blocks
        while group * matrix.main > 640:
            group //= 2
        free = group.bit_length() - 1
        step = next(s for s in (384, 640, 512, 128) if width % s == 0)

        @pl.loop(0, 0 if u in EARLY else (blocks // group) * (width // step))
        def _(i):
            g, j = lax.div(i, width // step), lax.rem(i, width // step)
            rows = pl.ds(pl.multiple_of(g * (group * matrix.main), 16), group * matrix.main)
            columns = pl.ds(pl.multiple_of(j * step, 128), step)
            result = jnp.dot(left[rows, :], right[:, columns], preferred_element_type=jnp.float32)
            high = len(dims) - free
            where = tuple(lax.rem(lax.div(g, 1 << (high - 1 - k)), 2) for k in range(high))
            target = pl.ds(pl.multiple_of(start_column - units[u].start + j * step, 128), step)
            grads[u][where + (slice(None),) * (free + 1) + (target,)] = result.astype(
                jnp.bfloat16
            ).reshape((2,) * free + (matrix.main, step))

        if matrix.rest:
            offset = blocks * (matrix.main + 16 * p)

            @pl.loop(0, width // step)
            def _(j):
                columns = pl.ds(pl.multiple_of(j * step, 128), step)
                result = jnp.dot(
                    left[pl.ds(offset, blocks * 16), :],
                    right[:, columns],
                    preferred_element_type=jnp.float32,
                )
                if p == 0:
                    fold_sum[:, columns] = result
                else:
                    fold_sum[:, columns] += result

        if index + 2 < len(all_pieces):
            start(right_copies(index + 2))
        last = p + 1 == len(matrix.pieces)
        if last and m + 2 < count:
            start(left_copies(m + 2))
        if last and matrix.rest:
            f = next(i for i, unit in enumerate(units) if unit.matrix == m and unit.folded)
            folded = fold_sum[:, pl.ds(0, units[f].columns)].astype(jnp.bfloat16)
            grads[f][...] = folded.reshape((2,) * len(dims) + (16, units[f].columns))

    shipped = {}

    def ship(k):
        return remote(ships[k], docks[k], ship_send.at[k], ship_recv.at[k], "seq")

    path = [0] + list(dims)
    vector_flying = {}

    def vector_send(h):
        source = vector_ref if h == 0 else vector_sum.at[h - 1]
        return remote(source, vector_land.at[h], vsend_sem.at[h], vrecv_sem.at[h], path[h])

    def vector_add(h):
        vector_flying[h].wait_recv()
        before = vector_ref[...] if h == 0 else vector_sum[h - 1]
        total = before + vector_land[h]
        if h < hops:
            vector_sum[h] = total
            vector_flying[h + 1] = vector_send(h + 1)
        else:
            vector_out[...] = total

    vector_flying[0] = vector_send(0)
    vector_done, since = 0, 0
    for action, u, h in events:
        if action == COMPUTE and u == SHIP:
            finish_inputs()
        elif action == COMPUTE:
            multiply(u)
        elif action == SEND and u == SHIP:
            shipped[h] = ship(h)
        elif action == SEND:
            flying[u, h] = send(u, h)
        elif u == SHIP:
            shipped[h].wait_recv()
        else:
            add(u, h)
            since += 1
            if since % 12 == 0 and vector_done <= hops:
                vector_add(vector_done)
                vector_done += 1
    while vector_done <= hops:
        vector_add(vector_done)
        vector_done += 1
    wait(kept)
    for copy in sent:
        copy.wait_send()


EARLY = (0, 1, 2, 3, 4, 5)
X, Y, Z, ZZ = "seq", 1, 2, 3
XYZ, YXZ, YZX = (X, Y, Z, ZZ), (Y, X, Z, ZZ), (Y, Z, ZZ, X)
ZXY, ZYX, XZY = (Z, ZZ, X, Y), (Z, ZZ, Y, X), (X, Z, ZZ, Y)
COMPUTE, SEND, TAKE, SHIP = 0, 1, 2, -1
HOP_PLAN = [XZY, YXZ, ZYX, XYZ, YXZ, ZXY, YXZ, XYZ, YZX, XZY, YXZ, YXZ, YXZ, YXZ, XZY, XYZ, ZXY]
EVENTS = [
    (TAKE, 0, 0), (SEND, 0, 1), (TAKE, 1, 0), (SEND, 1, 1), (TAKE, 2, 0), (SEND, 2, 1),
    (TAKE, 3, 0), (SEND, 3, 1), (TAKE, 4, 0), (SEND, 4, 1), (TAKE, 5, 0), (SEND, 5, 1),
    (COMPUTE, 0, 0), (COMPUTE, 1, 0), (COMPUTE, 2, 0), (COMPUTE, 3, 0), (SEND, 6, 0),
    (TAKE, 3, 1), (SEND, 3, 2), (COMPUTE, SHIP, 0), (TAKE, 0, 1), (SEND, 7, 0), (TAKE, 1, 1),
    (SEND, 1, 2), (COMPUTE, 4, 0), (SEND, SHIP, 0), (TAKE, 4, 1), (COMPUTE, 5, 0),
    (COMPUTE, 6, 0), (SEND, 8, 0), (COMPUTE, 7, 0), (SEND, 0, 2), (TAKE, 2, 1), (SEND, 9, 0),
    (TAKE, 7, 0), (SEND, 10, 0), (TAKE, 6, 0), (COMPUTE, 8, 0), (COMPUTE, 9, 0), (SEND, 4, 2),
    (TAKE, 3, 2), (TAKE, SHIP, 0), (SEND, 6, 1), (COMPUTE, 10, 0), (SEND, 3, 3), (TAKE, 5, 1),
    (SEND, 14, 0), (TAKE, 9, 0), (SEND, 9, 1), (TAKE, 1, 2), (COMPUTE, 11, 0), (SEND, 16, 0),
    (SEND, 11, 0), (TAKE, 8, 0), (SEND, 15, 0), (TAKE, 6, 1), (SEND, 8, 1), (TAKE, 4, 2),
    (SEND, 1, 3), (SEND, 4, 3), (TAKE, 0, 2), (TAKE, 9, 1), (SEND, 9, 2), (TAKE, 3, 3),
    (SEND, 6, 2), (TAKE, 16, 0), (SEND, 16, 1), (SEND, 12, 0), (TAKE, 10, 0), (TAKE, 1, 3),
    (TAKE, 4, 3), (TAKE, 8, 1), (SEND, 8, 2), (TAKE, 9, 2), (SEND, 10, 1), (TAKE, 14, 0),
    (SEND, 14, 1), (TAKE, 16, 1), (SEND, 13, 0), (TAKE, 11, 0), (TAKE, 6, 2), (SEND, 6, 3),
    (TAKE, 8, 2), (SEND, 11, 1), (TAKE, 15, 0), (TAKE, 6, 3), (SEND, 5, 2), (TAKE, 10, 1),
    (SEND, 10, 2), (TAKE, 14, 1), (SEND, 14, 2), (SEND, 15, 1), (TAKE, 12, 0), (SEND, 12, 1),
    (TAKE, 11, 1), (SEND, 11, 2), (TAKE, 10, 2), (SEND, 10, 3), (SEND, 2, 2), (TAKE, 13, 0),
    (SEND, 13, 1), (TAKE, 5, 2), (TAKE, 14, 2), (TAKE, 11, 2), (SEND, 11, 3), (SEND, 7, 1),
    (TAKE, 15, 1), (SEND, 15, 2), (TAKE, 10, 3), (SEND, 8, 3), (SEND, 16, 2), (TAKE, 12, 1),
    (SEND, 12, 2), (SEND, 0, 3), (TAKE, 2, 2), (SEND, 2, 3), (SEND, SHIP, 1), (TAKE, 13, 1),
    (TAKE, 11, 3), (SEND, 13, 2), (TAKE, 15, 2), (SEND, 15, 3), (TAKE, 8, 3), (TAKE, 16, 2),
    (SEND, 14, 3), (SEND, 5, 3), (TAKE, 7, 1), (SEND, 7, 2), (TAKE, 12, 2), (SEND, 12, 3),
    (TAKE, 2, 3), (SEND, 16, 3), (SEND, 9, 3), (TAKE, 0, 3), (TAKE, 13, 2), (SEND, 13, 3),
    (TAKE, 15, 3), (TAKE, 14, 3), (TAKE, 5, 3), (TAKE, 7, 2), (SEND, 7, 3), (TAKE, 16, 3),
    (TAKE, 9, 3), (TAKE, 12, 3), (TAKE, 13, 3), (TAKE, 7, 3), (TAKE, SHIP, 1),
]


def weight_gradients(operands, vectors, skip_weight, half, plan, bits):
    matrices, units, events = plan
    blocks = 2**bits
    dims = list(reversed(range(1, bits))) + ["seq"]
    given = len(operands)
    operands = [*operands, vectors, skip_weight]
    width = skip_weight.shape[1]
    ends = [(half, width), (2, half, width // 2)]
    anywhere = pl.BlockSpec(memory_space=pl.ANY)
    vmem = pl.BlockSpec(memory_space=pltpu.VMEM)
    hops, count = len(dims), len(matrices)
    shape = jax.ShapeDtypeStruct
    outs = [shape((m.share, m.columns), jnp.float32) for m in matrices]
    outs += [shape(end, jnp.bfloat16) for end in ends]
    outs += [shape(end, jnp.float32) for end in ends]
    outs.append(shape(vectors.shape, jnp.float32))
    low = jnp.bfloat16
    scratch = [pltpu.VMEM((2,) * hops + (unit.rows, unit.columns), low) for unit in units]
    for unit in units:
        for h in range(hops):
            scratch.append(pltpu.VMEM((2,) * (hops - 1 - h) + (unit.rows, unit.columns), low))
    scratch.append(pltpu.VMEM((hops + 1,) + vectors.shape, jnp.float32))
    scratch.append(pltpu.VMEM((hops,) + vectors.shape, jnp.float32))
    folded = [matrix.fold_width for matrix in matrices if matrix.rest]
    scratch.append(pltpu.VMEM((blocks * 16, max(folded)), jnp.float32))
    scratch.append(pltpu.VMEM((2, max(m.left_rows(blocks) for m in matrices), TWO), low))
    scratch.append(pltpu.VMEM((2, TWO, max(max(w for _, w in m.pieces) for m in matrices)), low))
    scratch += [pltpu.SemaphoreType.DMA((len(units), hops))] * 2
    scratch += [pltpu.SemaphoreType.DMA((hops + 1,))] * 2
    scratch += [pltpu.SemaphoreType.DMA((2, 2))] * 2
    scratch += [pltpu.SemaphoreType.DMA((len(EARLY), 2))]
    scratch += [pltpu.SemaphoreType.DMA((SHIPS,))] * 2
    scratch += [pltpu.VMEM((2, width, width), low), pltpu.VMEM((LANES, width), low)]
    scratch += [pltpu.VMEM(end, jnp.float32) for end in ends]
    scratch += [pltpu.VMEM(end, low) for end in ends]
    scratch.append(pltpu.SemaphoreType.DMA((5,)))
    results = pl.pallas_call(
        functools.partial(reduce_kernel, matrices, units, events, dims),
        out_shape=outs,
        in_specs=[anywhere] * given + [vmem, anywhere],
        out_specs=[vmem] * count + [anywhere] * (2 * SHIPS) + [vmem],
        scratch_shapes=scratch,
        compiler_params=pltpu.CompilerParams(
            collective_id=0, has_side_effects=True, vmem_limit_bytes=62 * 2**20
        ),
        name="reduce_weights",
    )(*operands)
    return results[:count], results[-1], results[count:-1]


def even_cuts(columns, width):
    return [(start, width) for start in range(0, columns, width)]


def make_plan(width, hidden, chunks):
    matrices = [
        Matrix(hidden // chunks, width, [384] * 3, even_cuts(width, 384)),
        Matrix(width // chunks, hidden, [1152] * 4, even_cuts(hidden, 1152)),
        Matrix(width // chunks, width, [384] * 3, [(0, width)]),
        Matrix(width // chunks, 3 * width, [1152] * 3, even_cuts(3 * width, 1152)),
        Matrix(2 * width // chunks, width, [640, 512], [(0, 640), (640, 512)]),
    ]
    units = make_units(matrices, HOP_PLAN)
    return matrices, units, EVENTS


def halving(block, order, bits):
    dp_index = lax.axis_index("dp")
    seq_index = lax.axis_index("seq")
    dims = list(reversed(range(1, bits))) + ["seq"]
    for name in order:
        axis = dims.index(name)
        own = seq_index if name == "seq" else (dp_index >> name) & 1
        sent = pick(block, 1 - own, axis)
        kept = pick(block, own, axis)
        got = swap_seq(sent) if name == "seq" else swap_dp(sent, name)
        total = kept.astype(jnp.float32) + got.astype(jnp.float32)
        dims.pop(axis)
        block = total.astype(jnp.bfloat16) if dims else total
    return block


def local_permutes(
    inputs,
    skipped,
    lengths,
    cotangent,
    skip_weight,
    skip_bias,
    gain_one,
    shift_one,
    qkv_weight,
    proj_weight,
    proj_bias,
    gain_two,
    shift_two,
    fc1_weight,
    fc1_bias,
    fc2_weight,
    fc2_bias,
):
    items, half, width = inputs.shape
    seq_count = lax.axis_size("seq")
    dp_count = lax.axis_size("dp")
    bits = dp_count.bit_length() - 1
    seq_index = lax.axis_index("seq")
    core = lax.axis_index("dp") & 1
    first = seq_index == 0
    slots = half * seq_count

    def whole_item(values, axis):
        own = pick(values, seq_index, 0)
        got = swap_seq(pick(values, 1 - seq_index, 0))
        return place(first, own, got, axis)

    def to_owner(values, axis):
        parts = jnp.split(values, 2, axis=axis)
        own = jnp.where(first, parts[0], parts[1])
        other = jnp.where(first, parts[1], parts[0])
        got = swap_seq(other.astype(jnp.bfloat16)).astype(values.dtype)
        return place(first, own[None], got[None], 0)

    own_inputs = whole_item(inputs, 0)
    own_skip = whole_item(skipped, 1)
    grad_out = whole_item(cotangent, 0)
    length = pick(lengths, seq_index, 0)
    rows = slots

    joined = jnp.concatenate([own_inputs, own_skip], axis=-1)
    stream = matmul(joined, skip_weight) + skip_bias
    normed = layer_norm(stream, gain_one, shift_one).astype(jnp.bfloat16)
    packed = matmul(normed, qkv_weight).astype(jnp.bfloat16)
    heads = packed.reshape(rows, 3, HEADS, HEAD_DIM)
    query, keys, values = heads[:, 0], heads[:, 1], heads[:, 2]
    scale = HEAD_DIM ** (-0.5)
    positions = jnp.arange(slots, dtype=jnp.int32)
    caption = (positions >= 1) & (positions <= length)
    image = (positions >= 1 + CAPTION) & (positions < 1 + CAPTION + IMAGE)
    valid = (positions == 0) | caption | image

    def product(spec, left, right):
        return jnp.einsum(spec, left, right, preferred_element_type=jnp.float32)

    scores = product("qhd,khd->hqk", query, keys) * scale
    scores = jnp.where(valid[None, None, :], scores, masked_score)
    top = jnp.max(scores, axis=-1, keepdims=True)
    expo = jnp.exp(scores - top)
    probs = expo / jnp.sum(expo, axis=-1, keepdims=True)
    probs_low = probs.astype(jnp.bfloat16)
    mixed = product("hqk,khd->qhd", probs_low, values)
    mixed = mixed.astype(jnp.bfloat16).reshape(rows, width)
    attended = matmul(mixed, proj_weight) + proj_bias
    stream_two = stream + attended
    normed_two = layer_norm(stream_two, gain_two, shift_two).astype(jnp.bfloat16)
    hidden = matmul(normed_two, fc1_weight) + fc1_bias
    acted, gelu_back = jax.vjp(gelu_exact, hidden)
    acted_low = acted.astype(jnp.bfloat16)
    block_output = (stream_two + (matmul(acted_low, fc2_weight) + fc2_bias)).astype(jnp.bfloat16)

    blocks = dp_count // 2

    def own_rows(left, right):
        parts = left.reshape(rows, blocks, 2, -1)
        kept = pick(parts, core, 2).reshape(rows, -1)
        sent = pick(parts, 1 - core, 2).reshape(rows, -1)
        left_both = jnp.concatenate([kept, swap_dp(sent, 0)], axis=0)
        right_both = jnp.concatenate([right, swap_dp(right, 0)], axis=0)
        total = matmul(left_both.T, right_both).astype(jnp.bfloat16)
        share = total.shape[0] // (blocks * 2)
        return total.reshape((2,) * bits + (share, right.shape[1]))

    above = list(range(1, bits))
    order_x = ["seq"] + above
    order_y = above + ["seq"]
    order_z = above[1:] + ["seq"] + above[:1]

    grad_fc2 = halving(own_rows(acted_low, grad_out), order_x, bits)
    grad_fc2_bias = column_sum(grad_out)
    grad_acted = matmul(grad_out, fc2_weight.T)
    grad_hidden = gelu_back(grad_acted)[0].astype(jnp.bfloat16)
    grad_fc1 = halving(own_rows(normed_two, grad_hidden), order_x, bits)
    grad_fc1_bias = column_sum(grad_hidden)
    grad_normed_two = matmul(grad_hidden, fc1_weight.T)
    _, norm_back_two = jax.vjp(layer_norm, stream_two, gain_two, shift_two)
    back_two, grad_gain_two, grad_shift_two = norm_back_two(grad_normed_two)
    grad_stream_two = grad_out.astype(jnp.float32) + back_two
    grad_attended = grad_stream_two.astype(jnp.bfloat16)
    grad_proj = halving(own_rows(mixed, grad_attended), order_y, bits)
    grad_proj_bias = column_sum(grad_attended)
    grad_mixed = matmul(grad_attended, proj_weight.T)
    grad_mixed = grad_mixed.astype(jnp.bfloat16).reshape(rows, HEADS, HEAD_DIM)
    grad_probs = product("qhd,khd->hqk", grad_mixed, values)
    grad_scores = probs * (grad_probs - jnp.sum(probs * grad_probs, axis=-1, keepdims=True))
    grad_scores = grad_scores.astype(jnp.bfloat16)
    grad_values = product("hqk,qhd->khd", probs_low, grad_mixed)
    grad_query = product("hqk,khd->qhd", grad_scores, keys) * scale
    grad_keys = product("hqk,qhd->khd", grad_scores, query) * scale
    grad_packed = jnp.stack([grad_query, grad_keys, grad_values], axis=1)
    grad_packed = grad_packed.astype(jnp.bfloat16).reshape(rows, 3 * width)
    grad_qkv = halving(own_rows(normed, grad_packed), order_y, bits)
    grad_normed = matmul(grad_packed, qkv_weight.T)
    _, norm_back_one = jax.vjp(layer_norm, stream, gain_one, shift_one)
    back_one, grad_gain_one, grad_shift_one = norm_back_one(grad_normed)
    grad_stream = (grad_stream_two + back_one).astype(jnp.bfloat16)
    grad_skip = halving(own_rows(joined, grad_stream), order_z, bits)
    grad_skip_bias = column_sum(grad_stream)
    grad_joined = matmul(grad_stream, skip_weight.T)

    vectors = (
        grad_skip_bias,
        grad_gain_one,
        grad_shift_one,
        grad_proj_bias,
        grad_gain_two,
        grad_shift_two,
        grad_fc1_bias,
        grad_fc2_bias,
    )
    chunks = dp_count * seq_count
    line = jnp.concatenate([v.reshape(chunks, -1) for v in vectors], axis=1)
    line = lax.psum_scatter(line, ("dp", "seq"), scatter_dimension=0, tiled=True)[0]
    pieces, start = [], 0
    for vector in vectors:
        size = vector.shape[0] // chunks
        pieces.append(line[start : start + size])
        start += size

    return (
        to_owner(block_output, 0),
        to_owner(grad_joined[:, :width], 0),
        to_owner(grad_joined[:, width:], 1),
        grad_skip,
        pieces[0],
        pieces[1],
        pieces[2],
        grad_qkv,
        grad_proj,
        pieces[3],
        pieces[4],
        pieces[5],
        grad_fc1,
        pieces[6],
        grad_fc2,
        pieces[7],
    )


def local_kernels(*arguments):
    arrays = Arguments(*arguments)
    items, half, width = arrays.inputs.shape
    hidden = arrays.fc1_weight.shape[1]
    dp_count = lax.axis_size("dp")
    bits = dp_count.bit_length() - 1
    seq_index = lax.axis_index("seq")
    device = lax.axis_index("dp") * 2 + seq_index
    first = seq_index == 0
    chunks = dp_count * 2
    skipped = arrays.skipped.reshape(items, 2, half, width // 2)
    plan = make_plan(width, hidden, chunks)
    feed = dict(
        inputs=arrays.inputs,
        skipped=skipped,
        cotangent=arrays.cotangent,
        lengths=arrays.lengths,
    )
    for name in Arguments._fields[4:]:
        feed[name] = getattr(arrays, name)
    found = run_block(feed, *plan[:2], width, hidden, half)
    kinds = ("left_", "far_left_", "right_", "far_right_")
    operands = [getattr(found, kind + name) for name in WEIGHTS for kind in kinds]
    operands += [getattr(found, f"grad_{u}") for u in EARLY]
    operands += [getattr(found, f"far_grad_{u}") for u in EARLY]
    weights, vectors, got = weight_gradients(
        operands,
        found.vectors,
        arrays.skip_weight,
        half,
        plan,
        bits,
    )
    grad_in_got, grad_skip_got, grad_in_own, grad_skip_own = got

    def owner(own, other):
        other = other.astype(own.dtype)
        return jnp.where(first, jnp.stack([own, other]), jnp.stack([other, own]))

    share = width // chunks
    mine = lax.dynamic_slice(vectors, (0, device * share), (8, share))
    wide_share = hidden // chunks
    per_row = width // wide_share
    row = 8 + device // per_row
    bias = lax.dynamic_slice(vectors, (row, device % per_row * wide_share), (1, wide_share))[0]
    grad_fc2, grad_fc1, grad_proj, grad_qkv, grad_skip = weights
    return (
        owner(found.block_own, found.block_got),
        owner(grad_in_own, grad_in_got),
        owner(grad_skip_own, grad_skip_got).reshape(items, 2 * half, width // 2),
        grad_skip,
        mine[0],
        mine[1],
        mine[2],
        grad_qkv,
        grad_proj,
        mine[3],
        mine[4],
        mine[5],
        grad_fc1,
        bias,
        grad_fc2,
        mine[7],
    )


class Arguments(typing.NamedTuple):
    inputs: jax.Array
    skipped: jax.Array
    lengths: jax.Array
    cotangent: jax.Array
    skip_weight: jax.Array
    skip_bias: jax.Array
    gain_one: jax.Array
    shift_one: jax.Array
    qkv_weight: jax.Array
    proj_weight: jax.Array
    proj_bias: jax.Array
    gain_two: jax.Array
    shift_two: jax.Array
    fc1_weight: jax.Array
    fc1_bias: jax.Array
    fc2_weight: jax.Array
    fc2_bias: jax.Array


def solution(mesh):
    small = mesh.shape["dp"] == 16
    return jax.shard_map(
        local_kernels if small else local_permutes,
        mesh=mesh,
        in_specs=(
            P("dp", "seq", None),
            P("dp", None, "seq"),
            P("dp"),
            P("dp", "seq", None),
        )
        + (P(),) * 13,
        out_specs=(
            P("dp", "seq", None),
            P("dp", "seq", None),
            P("dp", None, "seq"),
            P(("dp", "seq"), None),
            P(("dp", "seq")),
            P(("dp", "seq")),
            P(("dp", "seq")),
            P(("dp", "seq"), None),
            P(("dp", "seq"), None),
            P(("dp", "seq")),
            P(("dp", "seq")),
            P(("dp", "seq")),
            P(("dp", "seq"), None),
            P(("dp", "seq")),
            P(("dp", "seq"), None),
            P(("dp", "seq")),
        ),
        check_vma=False,
    )
```
